32 devices in a mesh: ctx: 16 (over z, y, core), head: 2 (over x).
Axes of the slice: x: 2, y: 2, z: 4, core: 2. Of those that a mesh axis runs over, the one named last changes fastest.
Arguments:
- hidden_states: bfloat16 [8192, 5376], P('ctx', 'head'), may hold values from -6 to 6
- query_base: bfloat16 [8192, 4096], P('ctx', 'head'), may hold values from -8 to 8
- key_base: bfloat16 [8192, 2048], P('ctx', 'head'), may hold values from -8 to 8
- frozen_value_rows: bfloat16 [8192, 2048], P('ctx', 'head'), may hold values from -6 to 6
- query_down: bfloat16 [5376, 16], P('head'), may hold values from -0.078125 to 0.078125
- query_up: bfloat16 [16, 4096], P(None, 'head'), may hold values from -0.75 to 0.75
- value_down: bfloat16 [5376, 16], P('head'), may hold values from -0.078125 to 0.078125
- value_up_weight: bfloat16 [16, 2048], P(None, 'head'), may hold values from -0.75 to 0.75
- positions: int32 [8192], P('ctx'), may hold values from 0 to 16382, as said below
- block_mask: int32 [64, 9], replicated, may hold values from 0 to 1, as said below
- output_gradient: bfloat16 [8192, 4096], P('ctx', 'head'), may hold values from -96 to 96
Outputs:
- attention_out: bfloat16 [8192, 4096], P('ctx', 'head')
- grad_query_down: float32 [5376, 16], P('head')
- grad_query_up: float32 [16, 4096], P(None, 'head')
- grad_value_down: float32 [5376, 16], P('head')
- grad_value_up: float32 [16, 2048], P(None, 'head')
The draws below stay inside these ranges and needn't reach their ends.
Inputs may be any that keep to these rules, and one draw needn't show every extreme that they name: positions rise strictly along the tokens. `block_mask`: entry (b, o) is 1 where the query block b may attend the key block b - o; column 0 is 1 in every row.
All inputs are finite; a program needn't handle non-finite values.
Results may differ from the reference program's by a relative error of at most 0.04.
Values may be sent and summed in bfloat16 or wider, within the bound.
No kernel may reach another device: no remote copies, remote signals or barrier semaphores. Data moves between devices by JAX's collectives and lax.ppermute only.
A program may use at most 192 MiB of HBM per device.

```python
import jax
import jax.numpy as jnp
from jax import lax

D = 5376
QUERY_HEADS = 32
KEY_VALUE_HEADS = 16
HEAD_SIZE = 128
WINDOW = 1024
ADAPTER_RANK = 16
BLOCK = 128
TOK_DEV = 512
DOCUMENT_TOKENS = 8192
NBLK = 64
BAND = 9


def position_table(key):
    skips = jax.random.randint(jax.random.fold_in(key, 7), (DOCUMENT_TOKENS,), 0, 2).astype(jnp.int32)
    token_ids = jnp.arange(DOCUMENT_TOKENS, dtype=jnp.int32)
    rising = (token_ids + jnp.cumsum(skips).astype(jnp.int32) - skips[0]).astype(jnp.int32)
    return jnp.where(token_ids == DOCUMENT_TOKENS - 1, 2 * DOCUMENT_TOKENS - 2, rising).astype(jnp.int32)


def draw_positions(key, part):
    return position_table(key)


def draw_block_mask(key, part):
    coins = jax.random.randint(jax.random.fold_in(key, 53), (NBLK, BAND), 0, 4)
    column = jnp.arange(BAND, dtype=jnp.int32)[None, :]
    return jnp.where(column == 0, 1, (coins > 0).astype(jnp.int32)).astype(jnp.int32)


def draw_key_base(key, part):
    unadapted_result = jnp.clip(jax.random.normal(jax.random.fold_in(key, 41), (DOCUMENT_TOKENS, KEY_VALUE_HEADS * HEAD_SIZE), jnp.float32), -6.0, 6.0)
    return unadapted_result.astype(jnp.bfloat16)


def draw_query_base(key, part):
    unadapted_result = jnp.clip(jax.random.normal(jax.random.fold_in(key, 45), (DOCUMENT_TOKENS, QUERY_HEADS * HEAD_SIZE), jnp.float32), -6.0, 6.0)
    return unadapted_result.astype(jnp.bfloat16)


def block_scale(stream_key, dims, pieces, smallest, top_value):
    gain, own = 1.0, jax.random.fold_in(stream_key, 6)
    for dim, shards_of in pieces:
        draws = jnp.exp(jax.random.uniform(jax.random.fold_in(own, dim), (shards_of,), jnp.float32, smallest / len(pieces), top_value / len(pieces)))
        gain = gain * jnp.repeat(draws, dims[dim] // shards_of).reshape([-1 if axis == dim else 1 for axis in range(len(dims))])
    return gain


def bell_draw(own_key, dims, width, limit, split=(), kind=jnp.bfloat16):
    drawn = jax.random.normal(own_key, dims, jnp.float32) * width
    if len(split) > 0:
        drawn = block_scale(own_key, dims, split, -0.22, 0.18) * drawn
    return jnp.clip(drawn, min=-limit, max=limit).astype(kind)


def setup_inputs(seed: int = 0) -> dict:
    key_list = jax.random.split(jax.random.key(seed), 12)
    return {
        "hidden_states": bell_draw(key_list[0], (DOCUMENT_TOKENS, D), 1.0, 6.0, ((0, 16), (1, 2))),
        "query_base": draw_query_base(jax.random.fold_in(key_list[11], 71), 0),
        "key_base": draw_key_base(jax.random.fold_in(key_list[11], 71), 0),
        "frozen_value_rows": bell_draw(key_list[3], (DOCUMENT_TOKENS, KEY_VALUE_HEADS * HEAD_SIZE), 1.0, 6.0, ((0, 16), (1, 2))),
        "query_down": bell_draw(key_list[4], (D, ADAPTER_RANK), D ** -0.5, 0.078125, ((0, 2),)),
        "query_up": bell_draw(key_list[5], (ADAPTER_RANK, QUERY_HEADS * HEAD_SIZE), (4 * ADAPTER_RANK) ** -0.5, 0.75, ((1, 2),)),
        "value_down": bell_draw(key_list[6], (D, ADAPTER_RANK), D ** -0.5, 0.078125, ((0, 2),)),
        "value_up_weight": bell_draw(key_list[7], (ADAPTER_RANK, KEY_VALUE_HEADS * HEAD_SIZE), (4 * ADAPTER_RANK) ** -0.5, 0.75, ((1, 2),)),
        "positions": draw_positions(jax.random.fold_in(key_list[11], 71), 0),
        "block_mask": draw_block_mask(jax.random.fold_in(key_list[11], 71), 0),
        "output_gradient": bell_draw(key_list[10], (DOCUMENT_TOKENS, QUERY_HEADS * HEAD_SIZE), 16.0, 96.0, ((0, 16), (1, 2))),
    }


rope_base = 10000.0


def rotate(row_block, position_ids, turn_sign):
    count = row_block.shape[0]
    col_count = row_block.shape[1]
    half_width = HEAD_SIZE // 2
    frequency = rope_base ** (-(2.0 * jnp.arange(half_width, dtype=jnp.float32)) / HEAD_SIZE)
    angles = position_ids.astype(jnp.float32)[:, None] * frequency[None, :]
    cosines = jnp.concatenate([jnp.cos(angles), jnp.cos(angles)], axis=-1)
    sines = jnp.concatenate([jnp.sin(angles), jnp.sin(angles)], axis=-1)
    shaped = row_block.reshape(count, col_count // HEAD_SIZE, HEAD_SIZE)
    turned = jnp.concatenate([-shaped[..., half_width:], shaped[..., :half_width]], axis=-1)
    return (shaped * cosines[:, None, :] + turn_sign * turned * sines[:, None, :]).reshape(count, col_count)


def allowed_pairs(mask_rows, query_first, key_first, count_of_queries, key_count):
    query_ids = query_first + jnp.arange(count_of_queries, dtype=jnp.int32)
    key_ids = key_first + jnp.arange(key_count, dtype=jnp.int32)
    token_gap = key_ids[None, :] - query_ids[:, None]
    token_ok = (token_gap <= 0) & (token_gap > -WINDOW) & (key_ids >= 0)[None, :]
    query_blocks = query_first // BLOCK + jnp.arange(count_of_queries // BLOCK, dtype=jnp.int32)
    key_blocks = key_first // BLOCK + jnp.arange(key_count // BLOCK, dtype=jnp.int32)
    offset = query_blocks[:, None] - key_blocks[None, :]
    band_size = mask_rows.shape[1]
    band_hit = jnp.any((offset[:, :, None] == jnp.arange(band_size, dtype=jnp.int32)[None, None, :]) & (mask_rows[:, None, :] == 1), axis=-1)
    spread_out = jnp.broadcast_to(band_hit[:, None, :, None], (count_of_queries // BLOCK, BLOCK, key_count // BLOCK, BLOCK)).reshape(count_of_queries, key_count)
    return token_ok & spread_out


def reference(hidden_states, query_base, key_base, frozen_value_rows, query_down, query_up, value_down, value_up_weight, positions, block_mask, output_gradient):
    query_low = jnp.dot(hidden_states, query_down, preferred_element_type=jnp.float32).astype(jnp.bfloat16)
    value_low = jnp.dot(hidden_states, value_down, preferred_element_type=jnp.float32).astype(jnp.bfloat16)
    query_rows = rotate(query_base.astype(jnp.float32) + jnp.dot(query_low, query_up, preferred_element_type=jnp.float32), positions, 1.0).astype(jnp.bfloat16)
    keys = rotate(key_base.astype(jnp.float32), positions, 1.0).astype(jnp.bfloat16)
    values = (frozen_value_rows.astype(jnp.float32) + jnp.dot(value_low, value_up_weight, preferred_element_type=jnp.float32)).astype(jnp.bfloat16)
    count_of_queries = TOK_DEV
    key_extent = WINDOW // TOK_DEV
    key_range_length = (key_extent + 1) * count_of_queries
    query_groups = QUERY_HEADS // KEY_VALUE_HEADS
    score_scale = (D // QUERY_HEADS) ** -0.5
    leading_rows = jnp.zeros((key_extent * count_of_queries, KEY_VALUE_HEADS * HEAD_SIZE), jnp.bfloat16)
    key_rows_padded = jnp.concatenate([leading_rows, keys], axis=0)
    value_rows_padded = jnp.concatenate([leading_rows, values], axis=0)
    block_count = DOCUMENT_TOKENS // count_of_queries

    def block_step(value_sums, block_index):
        leading_token = block_index * count_of_queries
        block_query_rows = lax.dynamic_slice_in_dim(query_rows, leading_token, count_of_queries, 0).reshape(count_of_queries, KEY_VALUE_HEADS, query_groups, HEAD_SIZE).astype(jnp.float32)
        block_gradient_rows = lax.dynamic_slice_in_dim(output_gradient, leading_token, count_of_queries, 0).reshape(count_of_queries, KEY_VALUE_HEADS, query_groups, HEAD_SIZE).astype(jnp.float32)
        block_key_rows = lax.dynamic_slice_in_dim(key_rows_padded, leading_token, key_range_length, 0).reshape(key_range_length, KEY_VALUE_HEADS, HEAD_SIZE).astype(jnp.float32)
        block_value_rows = lax.dynamic_slice_in_dim(value_rows_padded, leading_token, key_range_length, 0).reshape(key_range_length, KEY_VALUE_HEADS, HEAD_SIZE).astype(jnp.float32)
        mask_rows = lax.dynamic_slice_in_dim(block_mask, block_index * (count_of_queries // BLOCK), count_of_queries // BLOCK, 0)
        allowed = allowed_pairs(mask_rows, leading_token, leading_token - key_extent * count_of_queries, count_of_queries, key_range_length)
        scores = jnp.einsum('lhgd,khd->hglk', block_query_rows, block_key_rows) * score_scale
        scores = jnp.where(allowed[None, None], scores, -jnp.inf)
        row_max = jnp.max(scores, axis=-1, keepdims=True)
        log_total = row_max[..., 0] + jnp.log(jnp.sum(jnp.exp(scores - row_max), axis=-1))
        weights = jnp.exp(scores - log_total[..., None])
        rounded_length = weights.astype(jnp.bfloat16)
        block_out = jnp.einsum('hglk,khd->lhgd', rounded_length.astype(jnp.float32), block_value_rows).astype(jnp.bfloat16)
        row_delta = jnp.transpose(jnp.sum(block_gradient_rows * block_out.astype(jnp.float32), axis=-1), (1, 2, 0))
        grad_weights = jnp.einsum('lhgd,khd->hglk', block_gradient_rows, block_value_rows)
        grad_scores = (weights * (grad_weights - row_delta[..., None]) * score_scale).astype(jnp.bfloat16)
        query_part = jnp.einsum('hglk,khd->lhgd', grad_scores.astype(jnp.float32), block_key_rows).reshape(count_of_queries, QUERY_HEADS * HEAD_SIZE)
        value_portion = jnp.einsum('xwzn,zxwy->nxy', rounded_length.astype(jnp.float32), block_gradient_rows).reshape(key_range_length, KEY_VALUE_HEADS * HEAD_SIZE)
        current = lax.dynamic_slice_in_dim(value_sums, leading_token, key_range_length, 0)
        value_sums = lax.dynamic_update_slice_in_dim(value_sums, current + value_portion, leading_token, 0)
        return value_sums, (block_out.reshape(count_of_queries, QUERY_HEADS * HEAD_SIZE), query_part)

    starting_sums = jnp.zeros((DOCUMENT_TOKENS + key_extent * count_of_queries, KEY_VALUE_HEADS * HEAD_SIZE), jnp.float32)
    value_sums, (out_blocks, query_parts) = lax.scan(block_step, starting_sums, jnp.arange(block_count, dtype=jnp.int32))
    attention_out = out_blocks.reshape(DOCUMENT_TOKENS, QUERY_HEADS * HEAD_SIZE)
    query_grad = rotate(query_parts.reshape(DOCUMENT_TOKENS, QUERY_HEADS * HEAD_SIZE), positions, -1.0).astype(jnp.bfloat16)
    value_grad = value_sums[key_extent * count_of_queries:].astype(jnp.bfloat16)
    query_back = jnp.dot(query_grad, query_up.T, preferred_element_type=jnp.float32).astype(jnp.bfloat16)
    value_back = jnp.dot(value_grad, value_up_weight.T, preferred_element_type=jnp.float32).astype(jnp.bfloat16)
    loss_scale = DOCUMENT_TOKENS ** -0.5
    grad_query_down = jnp.dot(hidden_states.T, query_back, preferred_element_type=jnp.float32) * loss_scale
    grad_value_down = jnp.dot(hidden_states.T, value_back, preferred_element_type=jnp.float32) * loss_scale
    grad_query_up = jnp.dot(query_low.T, query_grad, preferred_element_type=jnp.float32) * loss_scale
    grad_value_up = jnp.dot(value_low.T, value_grad, preferred_element_type=jnp.float32) * loss_scale
    return (attention_out, grad_query_down, grad_query_up, grad_value_down, grad_value_up)
```

```python
import functools

import jax
import jax.numpy as jnp
from jax import lax
from jax.experimental import pallas as pl
from jax.experimental.pallas import tpu as pltpu
from jax.sharding import PartitionSpec as P

D = 5376
QUERY_HEADS = 32
KEY_VALUE_HEADS = 16
HEAD_SIZE = 128
WINDOW = 1024
BLOCK = 128
GROUPS = QUERY_HEADS // KEY_VALUE_HEADS
GROUP_WIDTH = GROUPS * HEAD_SIZE
SCORE_SCALE = (D // QUERY_HEADS) ** (-0.5)
LOG2_E = 1.4426950408889634
ROPE_BASE = 10000.0
FORBIDDEN = -1e30
RANK = 16

SUB = 256
KEYS = SUB + WINDOW
LANES = 128

CHUNKS = ((0, 3), (3, 6), (6, 8))

ROWS_BY_COLS = (((1,), (0,)), ((), ()))
BOTH_MINOR = (((1,), (1,)), ((), ()))
BOTH_MAJOR = (((0,), (0,)), ((), ()))


def mm(left, right, dims=ROWS_BY_COLS):
    return lax.dot_general(left, right, dims, preferred_element_type=jnp.float32)


def swap_halves(x):
    return pltpu.roll(x, HEAD_SIZE // 2, 1)


def prologue_kernel(chunks, positions_ref, frequency_ref, key_ref, value_ref, cos_ref, sin_ref, *outs):
    angles = positions_ref[...].astype(jnp.float32) * frequency_ref[...]
    lane = lax.broadcasted_iota(jnp.int32, angles.shape, 1)
    cosines = jnp.cos(angles)
    sines = jnp.sin(angles)
    sines = jnp.where(lane < HEAD_SIZE // 2, -sines, sines)
    cos_ref[...] = cosines
    sin_ref[...] = sines
    for (first, last), out_ref in zip(chunks, outs):
        count = last - first
        for head in range(first, last):
            cols = pl.ds(head * HEAD_SIZE, HEAD_SIZE)
            key = key_ref[:, cols].astype(jnp.float32)
            turned = key * cosines + swap_halves(key) * sines
            out_ref[:, pl.ds((head - first) * HEAD_SIZE, HEAD_SIZE)] = turned.astype(jnp.bfloat16)
            out_ref[:, pl.ds((count + head - first) * HEAD_SIZE, HEAD_SIZE)] = value_ref[:, cols]


def attention_kernel(
    first,
    parity_ref,
    query_ref,
    gradient_ref,
    key_own_ref,
    value_own_ref,
    key_one_ref,
    value_one_ref,
    key_even_ref,
    value_even_ref,
    key_odd_ref,
    value_odd_ref,
    query_up_ref,
    value_up_ref,
    query_low_ref,
    query_low_t_ref,
    cos_ref,
    sin_ref,
    value_low_ref,
    bias_ref,
    *rest,
):
    if first:
        out_ref, up_query_ref, up_value_ref, query_back_ref, value_back_ref, key_buf, value_buf = rest
    else:
        (_, query_back_in, value_back_in) = rest[:3]
        out_ref, up_query_ref, up_value_ref, query_back_ref, value_back_ref, key_buf, value_buf = rest[3:]
    tokens = query_ref.shape[0]

    @pl.when(pl.program_id(0) == 0)
    def _():
        key_buf[:, HEAD_SIZE:] = bias_ref[...]
        value_buf[:, HEAD_SIZE:] = value_low_ref[...]
        if first:
            query_back_ref[...] = jnp.zeros_like(query_back_ref)
            value_back_ref[...] = jnp.zeros_like(value_back_ref)
        else:
            query_back_ref[...] = query_back_in[...]
            value_back_ref[...] = value_back_in[...]

    odd = parity_ref[0] == 1
    key_buf[0:tokens, :HEAD_SIZE] = jnp.where(odd, key_odd_ref[...], key_even_ref[...])
    key_buf[tokens : 2 * tokens, :HEAD_SIZE] = key_one_ref[...]
    key_buf[2 * tokens :, :HEAD_SIZE] = key_own_ref[...]
    value_buf[0:tokens, :HEAD_SIZE] = jnp.where(odd, value_odd_ref[...], value_even_ref[...])
    value_buf[tokens : 2 * tokens, :HEAD_SIZE] = value_one_ref[...]
    value_buf[2 * tokens :, :HEAD_SIZE] = value_own_ref[...]

    query_up = query_up_ref[...]
    value_up = value_up_ref[...]
    value_up_pad = jnp.concatenate(
        [value_up, jnp.zeros((LANES - RANK, HEAD_SIZE), jnp.bfloat16)], axis=0
    )
    rows = GROUPS * SUB
    row = lax.broadcasted_iota(jnp.int32, (rows, LANES), 0)
    lane = lax.broadcasted_iota(jnp.int32, (rows, LANES), 1)
    second = (row % SUB) // BLOCK == 1
    lower = lane <= row % BLOCK
    extent = KEYS // BLOCK
    limits = {
        0: ~lower,
        1: ~lower | ~second,
        extent - 2: lower | second,
        extent - 1: lower,
    }

    up_query = jnp.zeros((RANK, GROUP_WIDTH), jnp.float32)
    up_value = jnp.zeros((HEAD_SIZE, HEAD_SIZE), jnp.float32)
    for step in range(tokens // SUB):
        own = pl.ds(step * SUB, SUB)
        window = pl.ds(step * SUB, KEYS)
        cosines = cos_ref[own, :]
        sines = sin_ref[own, :]
        adapted = query_ref[own, :].astype(jnp.float32) + mm(query_low_ref[own, :], query_up)
        turned = []
        for head in range(GROUPS):
            part = adapted[:, head * HEAD_SIZE : (head + 1) * HEAD_SIZE]
            turned.append(part * cosines + swap_halves(part) * sines)
        queries = (jnp.concatenate(turned, axis=0) * (SCORE_SCALE * LOG2_E)).astype(jnp.bfloat16)
        block_of = (row % SUB) // BLOCK + step * (SUB // BLOCK)
        chosen = (lane == block_of).astype(jnp.float32).astype(jnp.bfloat16)
        queries = jnp.concatenate([queries, chosen], axis=1)
        gradient = jnp.concatenate(
            [gradient_ref[own, head * HEAD_SIZE : (head + 1) * HEAD_SIZE] for head in range(GROUPS)],
            axis=0,
        )

        scores = mm(queries, key_buf[window, :], BOTH_MINOR)
        blocks = []
        for block in range(extent):
            part = scores[:, block * BLOCK : (block + 1) * BLOCK]
            if block in limits:
                part = jnp.where(limits[block], part, FORBIDDEN)
            blocks.append(part)
        highest = blocks[0]
        for part in blocks[1:]:
            highest = jnp.maximum(highest, part)
        highest = jnp.max(highest, axis=1, keepdims=True)
        weights = jnp.concatenate(
            [jnp.exp2(part - highest).astype(jnp.bfloat16) for part in blocks], axis=1
        )
        products = mm(weights, value_buf[window, :])
        total = products[:, HEAD_SIZE + RANK : HEAD_SIZE + RANK + 1]
        inverse = 1.0 / total
        low_part = (products[:, HEAD_SIZE:] * inverse).astype(jnp.bfloat16)
        outputs = (products[:, :HEAD_SIZE] * inverse + mm(low_part, value_up_pad)).astype(jnp.bfloat16)
        for head in range(GROUPS):
            out_ref[own, head * HEAD_SIZE : (head + 1) * HEAD_SIZE] = outputs[
                head * SUB : (head + 1) * SUB, :
            ]
        delta = jnp.sum(
            outputs.astype(jnp.float32) * gradient.astype(jnp.float32), axis=1, keepdims=True
        )
        up_value += mm(low_part, gradient, BOTH_MAJOR)

        gradient_low = mm(gradient, value_up_pad, BOTH_MINOR)
        grad_weights = mm(
            jnp.concatenate([gradient, gradient_low.astype(jnp.bfloat16)], axis=1),
            value_buf[window, :],
            BOTH_MINOR,
        )
        grad_scores = weights * (grad_weights - delta).astype(jnp.bfloat16)
        query_sums = mm(grad_scores, key_buf[window, :HEAD_SIZE]) * (inverse * SCORE_SCALE)
        turned = []
        for head in range(GROUPS):
            part = query_sums[head * SUB : (head + 1) * SUB, :]
            turned.append(part * cosines - swap_halves(part) * sines)
        query_grad = jnp.concatenate(turned, axis=1).astype(jnp.bfloat16)
        up_query += mm(query_low_t_ref[:, own], query_grad)
        query_back_ref[:, own] += mm(query_up, query_grad, BOTH_MINOR)
        spread = jnp.transpose(gradient_low * inverse)[:RANK, :].astype(jnp.bfloat16)
        value_back_ref[:, window] += mm(spread, weights)
    up_query_ref[...] = up_query
    up_value_ref[...] = up_value[:RANK, :]


def attention_chunk(first, last, parity, query_base, gradient, own, one, even, odd, shared, carried):
    count = last - first
    tokens = query_base.shape[0]
    keys = 3 * tokens
    wide = pl.BlockSpec((tokens, GROUP_WIDTH), lambda i, s: (0, first + i))
    near = pl.BlockSpec((tokens, HEAD_SIZE), lambda i, s: (0, i))
    far = pl.BlockSpec((tokens, HEAD_SIZE), lambda i, s: (0, count + i))

    def whole(rows, cols):
        return pl.BlockSpec((rows, cols), lambda i, s: (0, 0))

    query_up, value_up, query_low, query_low_t, cosines, sines, value_low, bias = shared
    in_specs = [
        wide,
        wide,
        *([near, far] * 4),
        pl.BlockSpec((RANK, GROUP_WIDTH), lambda i, s: (0, first + i)),
        pl.BlockSpec((RANK, HEAD_SIZE), lambda i, s: (0, first + i)),
        whole(tokens, RANK),
        whole(RANK, tokens),
        whole(tokens, HEAD_SIZE),
        whole(tokens, HEAD_SIZE),
        whole(keys, LANES),
        whole(keys, LANES),
    ]
    arguments = [
        query_base,
        gradient,
        own,
        own,
        one,
        one,
        even,
        even,
        odd,
        odd,
        query_up,
        value_up,
        query_low,
        query_low_t,
        cosines,
        sines,
        value_low,
        bias,
    ]
    aliases = {}
    if carried is not None:
        in_specs += [pl.BlockSpec(memory_space=pl.ANY), whole(RANK, tokens), whole(RANK, keys)]
        arguments += list(carried)
        aliases = {1 + len(arguments) - 3: 0}
    return pl.pallas_call(
        functools.partial(attention_kernel, carried is None),
        grid_spec=pltpu.PrefetchScalarGridSpec(
            num_scalar_prefetch=1,
            grid=(count,),
            in_specs=in_specs,
            out_specs=[
                wide,
                pl.BlockSpec((RANK, GROUP_WIDTH), lambda i, s: (0, i)),
                pl.BlockSpec((RANK, HEAD_SIZE), lambda i, s: (0, i)),
                whole(RANK, tokens),
                whole(RANK, keys),
            ],
            scratch_shapes=[
                pltpu.VMEM((keys, HEAD_SIZE + LANES), jnp.bfloat16),
                pltpu.VMEM((keys, HEAD_SIZE + LANES), jnp.bfloat16),
            ],
        ),
        out_shape=[
            jax.ShapeDtypeStruct(query_base.shape, jnp.bfloat16),
            jax.ShapeDtypeStruct((RANK, count * GROUP_WIDTH), jnp.float32),
            jax.ShapeDtypeStruct((RANK, count * HEAD_SIZE), jnp.float32),
            jax.ShapeDtypeStruct((RANK, tokens), jnp.float32),
            jax.ShapeDtypeStruct((RANK, keys), jnp.float32),
        ],
        input_output_aliases=aliases,
        compiler_params=pltpu.CompilerParams(vmem_limit_bytes=50 * 2**20),
    )(parity, *arguments)


def head_sum(x):
    if lax.axis_size("head") == 2:
        return x + lax.ppermute(x, "head", [(0, 1), (1, 0)])
    return lax.psum(x, "head")


def mask_bias(block_mask, device_index, mask_height):
    band = block_mask.shape[1]
    own_mask = lax.dynamic_slice_in_dim(block_mask, device_index * mask_height, mask_height, 0)
    reach = WINDOW // BLOCK
    key_blocks = jnp.arange(mask_height + reach, dtype=jnp.int32)
    offset = reach + jnp.arange(mask_height, dtype=jnp.int32)[None, :] - key_blocks[:, None]
    hit = jnp.any(
        (offset[:, :, None] == jnp.arange(band, dtype=jnp.int32)[None, None, :])
        & (own_mask[None, :, :] == 1),
        axis=-1,
    )
    real = device_index * mask_height - reach + key_blocks >= 0
    bias = jnp.where(hit & real[:, None], 0.0, FORBIDDEN).astype(jnp.bfloat16)
    bias = jnp.pad(bias, ((0, 0), (0, LANES - mask_height)))
    return jnp.repeat(bias, BLOCK, axis=0)


def per_device(
    hidden_states,
    query_base,
    key_base,
    frozen_value_rows,
    query_down,
    query_up,
    value_down,
    value_up_weight,
    positions,
    block_mask,
    output_gradient,
):
    tokens = hidden_states.shape[0]
    devices = lax.axis_size("ctx")
    device_index = lax.axis_index("ctx")
    kv_heads = key_base.shape[1] // HEAD_SIZE
    forward_one = [(i, i + 1) for i in range(devices - 1)]
    even_two = [(i, i + 2) for i in range(0, devices - 2, 2)]
    even_one = [(i, i + 1) for i in range(0, devices - 1, 2)]

    half = HEAD_SIZE // 2
    frequency = ROPE_BASE ** (-(2.0 * jnp.arange(half, dtype=jnp.float32)) / HEAD_SIZE)
    frequency = jnp.concatenate([frequency, frequency])[None, :]
    cosines, sines, *packed = pl.pallas_call(
        functools.partial(prologue_kernel, CHUNKS),
        out_shape=[
            jax.ShapeDtypeStruct((tokens, HEAD_SIZE), jnp.float32),
            jax.ShapeDtypeStruct((tokens, HEAD_SIZE), jnp.float32),
            *(
                jax.ShapeDtypeStruct((tokens, 2 * (last - first) * HEAD_SIZE), jnp.bfloat16)
                for first, last in CHUNKS
            ),
        ],
        compiler_params=pltpu.CompilerParams(vmem_limit_bytes=50 * 2**20),
    )(positions[:, None], frequency, key_base, frozen_value_rows)

    both_down = jnp.concatenate([query_down, value_down], axis=1)
    low = head_sum(mm(both_down, hidden_states, (((0,), (1,)), ((), ())))).astype(jnp.bfloat16)
    query_low_t = low[:RANK]
    value_low_t = low[RANK:]
    low_one = lax.ppermute(value_low_t, "ctx", forward_one)
    low_two = lax.ppermute(value_low_t, "ctx", [(i, i + 2) for i in range(devices - 2)])
    value_low = jnp.concatenate([low_two, low_one, value_low_t], axis=1)
    value_low = jnp.concatenate(
        [
            value_low,
            jnp.ones((1, 3 * tokens), jnp.bfloat16),
            jnp.zeros((LANES - RANK - 1, 3 * tokens), jnp.bfloat16),
        ],
        axis=0,
    ).T
    bias = mask_bias(block_mask, device_index, tokens // BLOCK)
    parity = (device_index % 2).astype(jnp.int32).reshape(1)

    ones, evens, odds = [], [], []
    for own in packed:
        ones.append(lax.ppermute(own, "ctx", forward_one))
        evens.append(lax.ppermute(own, "ctx", even_two))
    for one in ones:
        odds.append(lax.ppermute(one, "ctx", even_one))

    shared = (
        query_up,
        value_up_weight,
        query_low_t.T,
        query_low_t,
        cosines,
        sines,
        value_low,
        bias,
    )
    carried = None
    up_queries, up_values = [], []
    for chunk, (first, last) in enumerate(CHUNKS):
        attention_out, up_query, up_value, query_back, value_back = attention_chunk(
            first,
            last,
            parity,
            query_base,
            output_gradient,
            packed[chunk],
            ones[chunk],
            evens[chunk],
            odds[chunk],
            shared,
            carried,
        )
        carried = (attention_out, query_back, value_back)
        up_queries.append(up_query)
        up_values.append(up_value)

    back_one = lax.ppermute(
        value_back[:, tokens : 2 * tokens], "ctx", [(i + 1, i) for i in range(devices - 1)]
    )
    back_two = lax.ppermute(value_back[:, :tokens], "ctx", [(i + 2, i) for i in range(devices - 2)])
    value_back = value_back[:, 2 * tokens :] + back_one + back_two
    back = head_sum(jnp.concatenate([query_back, value_back], axis=0)).astype(jnp.bfloat16)
    down = mm(back, hidden_states)
    features = down.shape[1]
    partial = jnp.concatenate([down[:RANK], down[RANK:], *up_queries, *up_values], axis=1)
    columns = partial.shape[1]
    piece = -(-columns // (devices * LANES)) * LANES
    partial = jnp.pad(partial.astype(jnp.bfloat16), ((0, 0), (0, devices * piece - columns)))
    partial = partial.reshape(RANK, devices, piece).transpose(1, 0, 2)
    received = lax.all_to_all(partial, "ctx", 0, 0)
    mine = jnp.sum(received.astype(jnp.float32), axis=0) * ((devices * tokens) ** (-0.5))
    mine = jnp.broadcast_to(mine.astype(jnp.bfloat16)[None], (devices, RANK, piece))
    summed = lax.all_to_all(mine, "ctx", 0, 0)
    summed = summed.transpose(1, 0, 2).reshape(RANK, devices * piece).astype(jnp.float32)
    query_columns = kv_heads * GROUP_WIDTH
    up_first = 2 * features
    return (
        attention_out,
        summed[:, :features].T,
        summed[:, up_first : up_first + query_columns],
        summed[:, features:up_first].T,
        summed[:, up_first + query_columns : columns],
    )


def solution(mesh):
    placed = (
        P("ctx", "head"),
        P("ctx", "head"),
        P("ctx", "head"),
        P("ctx", "head"),
        P("head", None),
        P(None, "head"),
        P("head", None),
        P(None, "head"),
        P("ctx"),
        P(),
        P("ctx", "head"),
    )
    return jax.shard_map(
        per_device,
        mesh=mesh,
        in_specs=placed,
        out_specs=(
            P("ctx", "head"),
            P("head", None),
            P(None, "head"),
            P("head", None),
            P(None, "head"),
        ),
        check_vma=False,
    )
```

```python
import functools

import jax
import jax.numpy as jnp
import numpy as np
from jax import lax
from jax.experimental import pallas as pl
from jax.experimental.pallas import tpu as pltpu
from jax.sharding import PartitionSpec as P

D = 5376
QUERY_HEADS = 32
KEY_VALUE_HEADS = 16
HEAD_SIZE = 128
WINDOW = 1024
BLOCK = 128
GROUPS = QUERY_HEADS // KEY_VALUE_HEADS
GROUP_WIDTH = GROUPS * HEAD_SIZE
SCORE_SCALE = (D // QUERY_HEADS) ** (-0.5)
LOG2_E = 1.4426950408889634
ROPE_BASE = 10000.0
FORBIDDEN = -1e30
RANK = 16

SUB = 256
KEYS = SUB + WINDOW
LANES = 128
OFFSET_LANE = 64
ONES_LANE = RANK

CHUNKS = ((0, 2), (2, 4), (4, 6), (6, 8))

ROWS_BY_COLS = (((1,), (0,)), ((), ()))
BOTH_MINOR = (((1,), (1,)), ((), ()))
BOTH_MAJOR = (((0,), (0,)), ((), ()))


def mm(left, right, dims=ROWS_BY_COLS):
    return lax.dot_general(left, right, dims, preferred_element_type=jnp.float32)


def swap_halves(x):
    return pltpu.roll(x, HEAD_SIZE // 2, 1)


def prologue_kernel(chunks, positions_ref, frequency_ref, key_ref, value_ref, cos_ref, sin_ref, *outs):
    tokens = key_ref.shape[0]
    half = HEAD_SIZE // 2
    angles = frequency_ref[...] * positions_ref[...].astype(jnp.float32)
    both = jnp.transpose(jnp.concatenate([jnp.cos(angles), jnp.sin(angles)], axis=0))
    turned = swap_halves(both)
    low_half = lax.broadcasted_iota(jnp.int32, both.shape, 1) < half
    cosines = jnp.where(low_half, both, turned)
    sines = jnp.where(low_half, -turned, both)
    cos_ref[...] = cosines
    sin_ref[...] = sines
    own = pl.ds(0, tokens)
    for (first, last), out_ref in zip(chunks, outs):
        count = last - first
        for head in range(first, last):
            cols = pl.ds(head * HEAD_SIZE, HEAD_SIZE)
            key = key_ref[:, cols].astype(jnp.float32)
            rotated = key * cosines + swap_halves(key) * sines
            out_ref[own, pl.ds((head - first) * HEAD_SIZE, HEAD_SIZE)] = rotated.astype(jnp.bfloat16)
            out_ref[own, pl.ds((count + head - first) * HEAD_SIZE, HEAD_SIZE)] = value_ref[:, cols]


def attention_kernel(
    first,
    place_ref,
    mask_ref,
    query_ref,
    gradient_ref,
    key_own_ref,
    value_own_ref,
    key_one_ref,
    value_one_ref,
    key_even_ref,
    value_even_ref,
    key_odd_ref,
    value_odd_ref,
    query_up_ref,
    value_up_ref,
    query_low_ref,
    query_low_t_ref,
    cos_ref,
    sin_ref,
    low_own_ref,
    low_one_ref,
    low_even_ref,
    low_odd_ref,
    *rest,
):
    if not first:
        (_, query_back_in, value_back_in) = rest[:3]
        rest = rest[3:]
    out_ref, up_query_ref, up_value_ref, query_back_ref, value_back_ref = rest[:5]
    key_buf, value_buf, query_buf, gradient_buf, weight_buf, score_buf, product_buf = rest[5:]
    tokens = query_ref.shape[0]
    keys = key_buf.shape[0]
    steps = tokens // SUB
    tiles = keys // SUB
    step_tiles = KEYS // SUB
    rows = GROUPS * SUB
    odd = place_ref[1] == 1

    @pl.when(pl.program_id(0) == 0)
    def _():
        first_block = place_ref[0] * (tokens // BLOCK)
        reach = WINDOW // BLOCK
        lane = lax.broadcasted_iota(jnp.int32, (BLOCK, LANES), 1)
        for key_block in range(keys // BLOCK):
            extra = jnp.where(lane == OFFSET_LANE, 1.0, 0.0)
            exists = first_block + (key_block - reach) >= 0
            for block in range(tokens // BLOCK):
                offset = reach + block - key_block
                if 0 <= offset <= reach:
                    hit = (mask_ref[offset, first_block + block] == 1) & exists
                    term = jnp.where(hit, 0.0, FORBIDDEN)
                else:
                    term = FORBIDDEN
                extra = jnp.where(lane == block, term, extra)
            key_buf[key_block * BLOCK : (key_block + 1) * BLOCK, HEAD_SIZE:] = extra.astype(jnp.bfloat16)
        low_far = jnp.where(odd, low_odd_ref[...], low_even_ref[...])
        low = jnp.concatenate([low_far, low_one_ref[...], low_own_ref[...]], axis=1)
        low = jnp.concatenate(
            [
                low.astype(jnp.float32),
                jnp.ones((2, keys), jnp.float32),
                jnp.zeros((LANES - RANK - 2, keys), jnp.float32),
            ],
            axis=0,
        )
        value_buf[:, HEAD_SIZE:] = jnp.transpose(low).astype(jnp.bfloat16)
        if first:
            query_back_ref[...] = jnp.zeros_like(query_back_ref)
            value_back_ref[...] = jnp.zeros_like(value_back_ref)
        else:
            query_back_ref[...] = query_back_in[...]
            value_back_ref[...] = value_back_in[...]

    key_buf[0:tokens, :HEAD_SIZE] = jnp.where(odd, key_odd_ref[...], key_even_ref[...])
    key_buf[tokens : 2 * tokens, :HEAD_SIZE] = key_one_ref[...]
    key_buf[2 * tokens :, :HEAD_SIZE] = key_own_ref[...]
    value_buf[0:tokens, :HEAD_SIZE] = jnp.where(odd, value_odd_ref[...], value_even_ref[...])
    value_buf[tokens : 2 * tokens, :HEAD_SIZE] = value_one_ref[...]
    value_buf[2 * tokens :, :HEAD_SIZE] = value_own_ref[...]

    query_up = query_up_ref[...]
    value_up = jnp.concatenate(
        [value_up_ref[...], jnp.zeros((LANES - RANK, HEAD_SIZE), jnp.bfloat16)], axis=0
    )
    lane = lax.broadcasted_iota(jnp.int32, (rows, LANES), 1)
    row = lax.broadcasted_iota(jnp.int32, (rows, LANES), 0) % SUB
    reach_of_key = jnp.max(
        jnp.abs(key_buf[:, :HEAD_SIZE].astype(jnp.float32)), axis=0, keepdims=True
    )

    def own(step):
        return slice(step * SUB, (step + 1) * SUB)

    def span(step):
        return slice(step * rows, (step + 1) * rows)

    def window(step):
        return slice(step * SUB, step * SUB + KEYS)

    def tile_steps(tile):
        return max(0, tile - step_tiles + 1), min(steps, tile + 1)

    def limit(step, tile, part):
        place = tile - step
        if 0 < place < step_tiles - 1:
            return part
        halves = []
        for block in range(SUB // BLOCK):
            inside = lane > row % BLOCK if place == 0 else lane <= row % BLOCK
            inside = inside | (row // BLOCK != block)
            halves.append(
                jnp.where(inside, part[:, block * BLOCK : (block + 1) * BLOCK], FORBIDDEN)
            )
        return jnp.concatenate(halves, axis=1)

    for step in range(steps):
        cosines = cos_ref[own(step), :]
        sines = sin_ref[own(step), :]
        adapted = query_ref[own(step), :].astype(jnp.float32) + mm(query_low_ref[own(step), :], query_up)
        turned = []
        for head in range(GROUPS):
            part = adapted[:, head * HEAD_SIZE : (head + 1) * HEAD_SIZE]
            turned.append(part * cosines + swap_halves(part) * sines)
        queries = jnp.concatenate(turned, axis=0) * (SCORE_SCALE * LOG2_E)
        bound = jnp.sum(jnp.abs(queries) * reach_of_key, axis=1, keepdims=True)
        chosen = (lane == row // BLOCK + step * (SUB // BLOCK)).astype(jnp.float32)
        query_buf[span(step), :HEAD_SIZE] = queries.astype(jnp.bfloat16)
        query_buf[span(step), HEAD_SIZE:] = jnp.where(lane == OFFSET_LANE, -bound, chosen).astype(
            jnp.bfloat16
        )
        gradient_buf[span(step), :HEAD_SIZE] = jnp.concatenate(
            [
                gradient_ref[own(step), head * HEAD_SIZE : (head + 1) * HEAD_SIZE]
                for head in range(GROUPS)
            ],
            axis=0,
        )

    def forward():
        for tile in range(tiles):
            low, high = tile_steps(tile)
            cols = slice(tile * SUB, (tile + 1) * SUB)
            scores = mm(query_buf[low * rows : high * rows, :], key_buf[cols, :], BOTH_MINOR)
            for step in range(low, high):
                part = limit(step, tile, scores[(step - low) * rows : (step - low + 1) * rows, :])
                weight_buf[span(step), cols] = jnp.exp2(part).astype(jnp.bfloat16)
        for step in range(steps):
            product_buf[span(step), :] = mm(weight_buf[span(step), window(step)], value_buf[window(step), :])

    forward()
    ones = slice(HEAD_SIZE + ONES_LANE, HEAD_SIZE + ONES_LANE + 1)

    @pl.when(jnp.min(product_buf[:, ones]) < 1e-18)
    def _():
        for step in range(steps):
            extra = query_buf[span(step), HEAD_SIZE:].astype(jnp.float32)
            query_buf[span(step), HEAD_SIZE:] = jnp.where(lane == OFFSET_LANE, 0.0, extra).astype(
                jnp.bfloat16
            )
            highest = jnp.full((rows, 1), FORBIDDEN, jnp.float32)
            for tile in range(step, step + step_tiles):
                cols = slice(tile * SUB, (tile + 1) * SUB)
                part = mm(query_buf[span(step), :], key_buf[cols, :], BOTH_MINOR)
                part = limit(step, tile, part)
                highest = jnp.maximum(highest, jnp.max(part, axis=1, keepdims=True))
            query_buf[span(step), HEAD_SIZE:] = jnp.where(lane == OFFSET_LANE, -highest, extra).astype(
                jnp.bfloat16
            )
        forward()

    spreads = []
    inverses = []
    up_value = jnp.zeros((LANES, HEAD_SIZE), jnp.float32)
    for step in range(steps):
        gradient = gradient_buf[span(step), :HEAD_SIZE]
        gradient_low = mm(gradient, value_up, BOTH_MINOR)
        inverse = 1.0 / product_buf[span(step), ones]
        low_part = (product_buf[span(step), HEAD_SIZE:] * inverse).astype(jnp.bfloat16)
        outputs = product_buf[span(step), :HEAD_SIZE] * inverse + mm(low_part, value_up)
        outputs = outputs.astype(jnp.bfloat16)
        for head in range(GROUPS):
            out_ref[own(step), head * HEAD_SIZE : (head + 1) * HEAD_SIZE] = outputs[own(head), :]
        delta = jnp.sum(
            outputs.astype(jnp.float32) * gradient.astype(jnp.float32), axis=1, keepdims=True
        )
        delta_high = delta.astype(jnp.bfloat16).astype(jnp.float32)
        extra = jnp.where(lane == ONES_LANE, -delta_high, gradient_low)
        extra = jnp.where(lane == ONES_LANE + 1, delta_high - delta, extra)
        gradient_buf[span(step), HEAD_SIZE:] = extra.astype(jnp.bfloat16)
        up_value += mm(low_part, gradient, BOTH_MAJOR)
        spreads.append(jnp.transpose(gradient_low * inverse)[:RANK, :].astype(jnp.bfloat16))
        inverses.append(inverse * SCORE_SCALE)
    up_value_ref[...] = up_value[:RANK, :]
    spread = jnp.concatenate(spreads, axis=1)

    for tile in range(tiles):
        low, high = tile_steps(tile)
        cols = slice(tile * SUB, (tile + 1) * SUB)
        part = slice(low * rows, high * rows)
        grad_weights = mm(gradient_buf[part, :], value_buf[cols, :], BOTH_MINOR)
        weights = weight_buf[part, cols]
        score_buf[part, cols] = weights * grad_weights.astype(jnp.bfloat16)
        value_back_ref[:, cols] += mm(spread[:, part], weights)

    query_grads = []
    for step in range(steps):
        cosines = cos_ref[own(step), :]
        sines = sin_ref[own(step), :]
        sums = mm(score_buf[span(step), window(step)], key_buf[window(step), :HEAD_SIZE]) * inverses[step]
        turned = []
        for head in range(GROUPS):
            part = sums[own(head), :]
            turned.append(part * cosines - swap_halves(part) * sines)
        query_grads.append(jnp.concatenate(turned, axis=1).astype(jnp.bfloat16))
    query_grad = jnp.concatenate(query_grads, axis=0)
    up_query_ref[...] = mm(query_low_t_ref[...], query_grad)
    query_back_ref[...] += mm(query_up, query_grad, BOTH_MINOR)


def attention_chunk(first, last, scalars, query_base, gradient, received, shared, lows, carried):
    count = last - first
    tokens = query_base.shape[0]
    keys = 3 * tokens
    wide = pl.BlockSpec((tokens, GROUP_WIDTH), lambda i, *s: (0, first + i))
    near = pl.BlockSpec((tokens, HEAD_SIZE), lambda i, *s: (0, i))
    far = pl.BlockSpec((tokens, HEAD_SIZE), lambda i, *s: (0, count + i))
    low_rows = pl.BlockSpec((RANK, tokens), lambda i, *s: (tokens // RANK, 0))

    def whole(rows, cols):
        return pl.BlockSpec((rows, cols), lambda i, *s: (0, 0))

    in_specs = [
        wide,
        wide,
        *([near, far] * 4),
        pl.BlockSpec((RANK, GROUP_WIDTH), lambda i, *s: (0, first + i)),
        pl.BlockSpec((RANK, HEAD_SIZE), lambda i, *s: (0, first + i)),
        whole(tokens, RANK),
        whole(RANK, tokens),
        whole(tokens, HEAD_SIZE),
        whole(tokens, HEAD_SIZE),
        *([low_rows] * 4),
    ]
    arguments = [query_base, gradient]
    for array in received:
        arguments += [array, array]
    arguments += [*shared, *lows]
    aliases = {}
    if carried is not None:
        in_specs += [pl.BlockSpec(memory_space=pl.ANY), whole(RANK, tokens), whole(RANK, keys)]
        arguments += list(carried)
        aliases = {len(scalars) + len(arguments) - 3: 0}
    rows = GROUPS * tokens
    wide_buf = HEAD_SIZE + LANES
    return pl.pallas_call(
        functools.partial(attention_kernel, carried is None),
        grid_spec=pltpu.PrefetchScalarGridSpec(
            num_scalar_prefetch=len(scalars),
            grid=(count,),
            in_specs=in_specs,
            out_specs=[
                wide,
                pl.BlockSpec((RANK, GROUP_WIDTH), lambda i, *s: (0, i)),
                pl.BlockSpec((RANK, HEAD_SIZE), lambda i, *s: (0, i)),
                whole(RANK, tokens),
                whole(RANK, keys),
            ],
            scratch_shapes=[
                pltpu.VMEM((keys, wide_buf), jnp.bfloat16),
                pltpu.VMEM((keys, wide_buf), jnp.bfloat16),
                pltpu.VMEM((rows, wide_buf), jnp.bfloat16),
                pltpu.VMEM((rows, wide_buf), jnp.bfloat16),
                pltpu.VMEM((rows, keys), jnp.bfloat16),
                pltpu.VMEM((rows, keys), jnp.bfloat16),
                pltpu.VMEM((rows, wide_buf), jnp.float32),
            ],
        ),
        out_shape=[
            jax.ShapeDtypeStruct(query_base.shape, jnp.bfloat16),
            jax.ShapeDtypeStruct((RANK, count * GROUP_WIDTH), jnp.float32),
            jax.ShapeDtypeStruct((RANK, count * HEAD_SIZE), jnp.float32),
            jax.ShapeDtypeStruct((RANK, tokens), jnp.float32),
            jax.ShapeDtypeStruct((RANK, keys), jnp.float32),
        ],
        input_output_aliases=aliases,
        compiler_params=pltpu.CompilerParams(vmem_limit_bytes=50 * 2**20),
    )(*scalars, *arguments)


def head_sum(x):
    if lax.axis_size("head") == 2:
        return x + lax.ppermute(x, "head", [(0, 1), (1, 0)])
    return lax.psum(x, "head")


def after(value, *others):
    return lax.optimization_barrier((value, *others))[0]


def per_device(
    hidden_states,
    query_base,
    key_base,
    frozen_value_rows,
    query_down,
    query_up,
    value_down,
    value_up_weight,
    positions,
    block_mask,
    output_gradient,
):
    tokens = hidden_states.shape[0]
    devices = lax.axis_size("ctx")
    device_index = lax.axis_index("ctx")
    kv_heads = key_base.shape[1] // HEAD_SIZE
    forward_one = [(i, i + 1) for i in range(devices - 1)]
    even_two = [(i, i + 2) for i in range(0, devices - 2, 2)]
    even_one = [(i, i + 1) for i in range(0, devices - 1, 2)]

    both_down = jnp.concatenate([query_down, value_down], axis=1)
    low = head_sum(mm(both_down, hidden_states, (((0,), (1,)), ((), ())))).astype(jnp.bfloat16)
    query_low_t = low[:RANK]
    value_low_t = low[RANK:]

    half = np.arange(HEAD_SIZE // 2, dtype=np.float64)
    frequency = (ROPE_BASE ** (-2.0 * half / HEAD_SIZE)).astype(np.float32)[:, None]
    cosines, sines, *packed = pl.pallas_call(
        functools.partial(prologue_kernel, CHUNKS),
        out_shape=[
            jax.ShapeDtypeStruct((tokens, HEAD_SIZE), jnp.float32),
            jax.ShapeDtypeStruct((tokens, HEAD_SIZE), jnp.float32),
            *(
                jax.ShapeDtypeStruct(
                    (tokens + (RANK if first == 0 else 0), 2 * (last - first) * HEAD_SIZE),
                    jnp.bfloat16,
                )
                for first, last in CHUNKS
            ),
        ],
        compiler_params=pltpu.CompilerParams(vmem_limit_bytes=50 * 2**20),
    )(positions[None, :], jnp.asarray(frequency), key_base, frozen_value_rows)
    packed[0] = lax.dynamic_update_slice(packed[0], value_low_t, (tokens, 0))

    place = jnp.stack([device_index, device_index % 2]).astype(jnp.int32)
    scalars = (place, block_mask.T)
    shared = (query_up, value_up_weight, query_low_t.T, query_low_t, cosines, sines)

    ones, evens = [], []
    for chunk, own in enumerate(packed):
        if chunk == 1:
            own = after(own, ones[0])
        elif chunk == 2:
            own = after(own, evens[0])
        elif chunk > 2:
            own = after(own, ones[chunk - 2], evens[chunk - 2])
        ones.append(lax.ppermute(own, "ctx", forward_one))
        evens.append(lax.ppermute(own, "ctx", even_two))

    carried = None
    lows = None
    up_queries, up_values = [], []
    for chunk, (first, last) in enumerate(CHUNKS):
        one = ones[chunk]
        if carried is not None:
            one = after(one, carried[1])
        odd = lax.ppermute(one, "ctx", even_one)
        received = (packed[chunk], one, evens[chunk], odd)
        if lows is None:
            lows = received
        attention_out, up_query, up_value, query_back, value_back = attention_chunk(
            first,
            last,
            scalars,
            query_base,
            output_gradient,
            received,
            shared,
            lows,
            carried,
        )
        carried = (attention_out, query_back, value_back)
        up_queries.append(up_query)
        up_values.append(up_value)

    back_one = lax.ppermute(
        value_back[:, tokens : 2 * tokens], "ctx", [(i + 1, i) for i in range(devices - 1)]
    )
    back_two = lax.ppermute(value_back[:, :tokens], "ctx", [(i + 2, i) for i in range(devices - 2)])
    value_back = value_back[:, 2 * tokens :] + back_one + back_two
    back = head_sum(jnp.concatenate([query_back, value_back], axis=0)).astype(jnp.bfloat16)
    down = mm(back, hidden_states)
    features = down.shape[1]
    partial = jnp.concatenate([down[:RANK], down[RANK:], *up_queries, *up_values], axis=1)
    columns = partial.shape[1]
    piece = -(-columns // (devices * LANES)) * LANES
    partial = jnp.pad(partial.astype(jnp.bfloat16), ((0, 0), (0, devices * piece - columns)))
    partial = partial.reshape(RANK, devices, piece).transpose(1, 0, 2)
    received = lax.all_to_all(partial, "ctx", 0, 0)
    mine = jnp.sum(received.astype(jnp.float32), axis=0) * ((devices * tokens) ** (-0.5))
    mine = jnp.broadcast_to(mine.astype(jnp.bfloat16)[None], (devices, RANK, piece))
    summed = lax.all_to_all(mine, "ctx", 0, 0)
    summed = summed.transpose(1, 0, 2).reshape(RANK, devices * piece).astype(jnp.float32)
    query_columns = kv_heads * GROUP_WIDTH
    up_first = 2 * features
    return (
        attention_out,
        summed[:, :features].T,
        summed[:, up_first : up_first + query_columns],
        summed[:, features:up_first].T,
        summed[:, up_first + query_columns : columns],
    )


def solution(mesh):
    placed = (
        P("ctx", "head"),
        P("ctx", "head"),
        P("ctx", "head"),
        P("ctx", "head"),
        P("head", None),
        P(None, "head"),
        P("head", None),
        P(None, "head"),
        P("ctx"),
        P(),
        P("ctx", "head"),
    )
    return jax.shard_map(
        per_device,
        mesh=mesh,
        in_specs=placed,
        out_specs=(
            P("ctx", "head"),
            P("head", None),
            P(None, "head"),
            P("head", None),
            P(None, "head"),
        ),
        check_vma=False,
    )
```

```python
import functools

import jax
import jax.numpy as jnp
import numpy as np
from jax import lax
from jax.experimental import pallas as pl
from jax.experimental.pallas import tpu as pltpu
from jax.sharding import PartitionSpec as P

D = 5376
QUERY_HEADS = 32
KEY_VALUE_HEADS = 16
HEAD_SIZE = 128
WINDOW = 1024
BLOCK = 128
GROUPS = QUERY_HEADS // KEY_VALUE_HEADS
GROUP_WIDTH = GROUPS * HEAD_SIZE
SCORE_SCALE = (D // QUERY_HEADS) ** (-0.5)
LOG2_E = 1.4426950408889634
ROPE_BASE = 10000.0
FORBIDDEN = -1e30
RANK = 16

SUB = 256
KEYS = SUB + WINDOW
LANES = 128
OFFSET_LANE = 64
ONES_LANE = RANK

CHUNKS = ((0, 2), (2, 5), (5, 8))

ROWS_BY_COLS = (((1,), (0,)), ((), ()))
BOTH_MINOR = (((1,), (1,)), ((), ()))
BOTH_MAJOR = (((0,), (0,)), ((), ()))


def mm(left, right, dims=ROWS_BY_COLS):
    return lax.dot_general(left, right, dims, preferred_element_type=jnp.float32)


def swap_halves(x):
    return pltpu.roll(x, HEAD_SIZE // 2, 1)


def prologue_kernel(chunks, positions_ref, frequency_ref, key_ref, value_ref, cos_ref, sin_ref, *outs):
    tokens = key_ref.shape[0]
    half = HEAD_SIZE // 2
    angles = frequency_ref[...] * positions_ref[...].astype(jnp.float32)
    both = jnp.transpose(jnp.concatenate([jnp.cos(angles), jnp.sin(angles)], axis=0))
    turned = swap_halves(both)
    low_half = lax.broadcasted_iota(jnp.int32, both.shape, 1) < half
    cosines = jnp.where(low_half, both, turned)
    sines = jnp.where(low_half, -turned, both)
    cos_ref[...] = cosines
    sin_ref[...] = sines
    own = pl.ds(0, tokens)
    for (first, last), out_ref in zip(chunks, outs):
        count = last - first
        for head in range(first, last):
            cols = pl.ds(head * HEAD_SIZE, HEAD_SIZE)
            key = key_ref[:, cols].astype(jnp.float32)
            rotated = key * cosines + swap_halves(key) * sines
            out_ref[own, pl.ds((head - first) * HEAD_SIZE, HEAD_SIZE)] = rotated.astype(jnp.bfloat16)
            out_ref[own, pl.ds((count + head - first) * HEAD_SIZE, HEAD_SIZE)] = value_ref[:, cols]


def attention_kernel(first, place_ref, *refs):
    if first:
        mask_ref, *refs = refs
    (
        query_ref,
        gradient_ref,
        key_own_ref,
        value_own_ref,
        key_one_ref,
        value_one_ref,
        key_even_ref,
        value_even_ref,
        key_odd_ref,
        value_odd_ref,
        query_up_ref,
        value_up_ref,
        query_low_ref,
        query_low_t_ref,
        cos_ref,
        sin_ref,
        *refs,
    ) = refs
    if first:
        low_own_ref, low_one_ref, low_even_ref, low_odd_ref, *refs = refs
    else:
        key_extra_in, value_extra_in, _, query_back_in, value_back_in, *refs = refs
    out_ref, up_query_ref, up_value_ref, query_back_ref, value_back_ref, *refs = refs
    if first:
        key_extra_ref, value_extra_ref, *refs = refs
    key_buf, value_buf, query_buf, gradient_buf, weight_buf, score_buf, product_buf = refs
    steps = query_back_ref.shape[0]
    tokens = steps * SUB
    keys = key_buf.shape[0]
    step_tiles = KEYS // SUB
    rows = GROUPS * SUB
    step = pl.program_id(1)
    odd = place_ref[1] == 1

    @pl.when((pl.program_id(0) == 0) & (step == 0))
    def _():
        if not first:
            key_buf[:, HEAD_SIZE:] = key_extra_in[...]
            value_buf[:, HEAD_SIZE:] = value_extra_in[...]
            query_back_ref[...] = query_back_in[...]
            value_back_ref[...] = value_back_in[...]
            return
        first_block = place_ref[0] * (tokens // BLOCK)
        reach = WINDOW // BLOCK
        lane = lax.broadcasted_iota(jnp.int32, (BLOCK, LANES), 1)
        for key_block in range(keys // BLOCK):
            extra = jnp.where(lane == OFFSET_LANE, 1.0, 0.0)
            exists = first_block + (key_block - reach) >= 0
            for block in range(tokens // BLOCK):
                offset = reach + block - key_block
                if 0 <= offset <= reach:
                    hit = (mask_ref[offset, first_block + block] == 1) & exists
                    term = jnp.where(hit, 0.0, FORBIDDEN)
                else:
                    term = FORBIDDEN
                extra = jnp.where(lane == block, term, extra)
            key_buf[key_block * BLOCK : (key_block + 1) * BLOCK, HEAD_SIZE:] = extra.astype(jnp.bfloat16)
        low_far = jnp.where(odd, low_odd_ref[...], low_even_ref[...])
        low = jnp.concatenate([low_far, low_one_ref[...], low_own_ref[...]], axis=1)
        low = jnp.concatenate(
            [
                low.astype(jnp.float32),
                jnp.ones((2, keys), jnp.float32),
                jnp.zeros((LANES - RANK - 2, keys), jnp.float32),
            ],
            axis=0,
        )
        value_buf[:, HEAD_SIZE:] = jnp.transpose(low).astype(jnp.bfloat16)
        key_extra_ref[...] = key_buf[:, HEAD_SIZE:]
        value_extra_ref[...] = value_buf[:, HEAD_SIZE:]
        query_back_ref[...] = jnp.zeros_like(query_back_ref)
        value_back_ref[...] = jnp.zeros_like(value_back_ref)

    @pl.when(step == 0)
    def _():
        key_buf[0:tokens, :HEAD_SIZE] = jnp.where(odd, key_odd_ref[...], key_even_ref[...])
        key_buf[tokens : 2 * tokens, :HEAD_SIZE] = key_one_ref[...]
        key_buf[2 * tokens :, :HEAD_SIZE] = key_own_ref[...]
        value_buf[0:tokens, :HEAD_SIZE] = jnp.where(odd, value_odd_ref[...], value_even_ref[...])
        value_buf[tokens : 2 * tokens, :HEAD_SIZE] = value_one_ref[...]
        value_buf[2 * tokens :, :HEAD_SIZE] = value_own_ref[...]
        up_query_ref[...] = jnp.zeros_like(up_query_ref)
        up_value_ref[...] = jnp.zeros_like(up_value_ref)

    query_up = query_up_ref[...]
    value_up = jnp.concatenate(
        [value_up_ref[...], jnp.zeros((LANES - RANK, HEAD_SIZE), jnp.bfloat16)], axis=0
    )
    lane = lax.broadcasted_iota(jnp.int32, (rows, LANES), 1)
    row = lax.broadcasted_iota(jnp.int32, (rows, LANES), 0) % SUB
    start = pl.multiple_of(step * SUB, SUB)
    window = pl.ds(start, KEYS)
    cosines = cos_ref[...]
    sines = sin_ref[...]

    def own(head):
        return slice(head * SUB, (head + 1) * SUB)

    def head_cols(head):
        return slice(head * HEAD_SIZE, (head + 1) * HEAD_SIZE)

    def near(tile):
        return pl.ds(pl.multiple_of(start + tile * SUB, SUB), SUB)

    def cols(tile):
        return slice(tile * SUB, (tile + 1) * SUB)

    def limit(tile, part):
        if 0 < tile < step_tiles - 1:
            return part
        halves = []
        for block in range(SUB // BLOCK):
            inside = lane > row % BLOCK if tile == 0 else lane <= row % BLOCK
            inside = inside | (row // BLOCK != block)
            halves.append(
                jnp.where(inside, part[:, block * BLOCK : (block + 1) * BLOCK], FORBIDDEN)
            )
        return jnp.concatenate(halves, axis=1)

    reach_of_key = jnp.max(
        jnp.abs(key_buf[window, :HEAD_SIZE].astype(jnp.float32)), axis=0, keepdims=True
    )
    adapted = query_ref[...].astype(jnp.float32) + mm(query_low_ref[...], query_up)
    turned = []
    for head in range(GROUPS):
        part = adapted[:, head_cols(head)]
        turned.append(part * cosines + swap_halves(part) * sines)
    queries = jnp.concatenate(turned, axis=0) * (SCORE_SCALE * LOG2_E)
    bound = jnp.sum(jnp.abs(queries) * reach_of_key, axis=1, keepdims=True)
    chosen = (lane == row // BLOCK + step * (SUB // BLOCK)).astype(jnp.float32)
    query_buf[:, :HEAD_SIZE] = queries.astype(jnp.bfloat16)
    query_buf[:, HEAD_SIZE:] = jnp.where(lane == OFFSET_LANE, -bound, chosen).astype(jnp.bfloat16)
    gradient = jnp.concatenate([gradient_ref[:, head_cols(head)] for head in range(GROUPS)], axis=0)

    def forward():
        for tile in range(step_tiles):
            scores = limit(tile, mm(query_buf[...], key_buf[near(tile), :], BOTH_MINOR))
            weight_buf[:, cols(tile)] = jnp.exp2(scores).astype(jnp.bfloat16)
        product_buf[...] = mm(weight_buf[...], value_buf[window, :])

    forward()
    ones = slice(HEAD_SIZE + ONES_LANE, HEAD_SIZE + ONES_LANE + 1)

    @pl.when(jnp.min(product_buf[:, ones]) < 1e-18)
    def _():
        extra = query_buf[:, HEAD_SIZE:].astype(jnp.float32)
        query_buf[:, HEAD_SIZE:] = jnp.where(lane == OFFSET_LANE, 0.0, extra).astype(jnp.bfloat16)
        highest = jnp.full((rows, 1), FORBIDDEN, jnp.float32)
        for tile in range(step_tiles):
            part = limit(tile, mm(query_buf[...], key_buf[near(tile), :], BOTH_MINOR))
            highest = jnp.maximum(highest, jnp.max(part, axis=1, keepdims=True))
        query_buf[:, HEAD_SIZE:] = jnp.where(lane == OFFSET_LANE, -highest, extra).astype(jnp.bfloat16)
        forward()

    gradient_low = mm(gradient, value_up, BOTH_MINOR)
    inverse = 1.0 / product_buf[:, ones]
    low_part = (product_buf[:, HEAD_SIZE:] * inverse).astype(jnp.bfloat16)
    outputs = product_buf[:, :HEAD_SIZE] * inverse + mm(low_part, value_up)
    outputs = outputs.astype(jnp.bfloat16)
    for head in range(GROUPS):
        out_ref[:, head_cols(head)] = outputs[own(head), :]
    delta = jnp.sum(
        outputs.astype(jnp.float32) * gradient.astype(jnp.float32), axis=1, keepdims=True
    )
    delta_high = delta.astype(jnp.bfloat16).astype(jnp.float32)
    extra = jnp.where(lane == ONES_LANE, -delta_high, gradient_low)
    extra = jnp.where(lane == ONES_LANE + 1, delta_high - delta, extra)
    gradient_buf[:, :HEAD_SIZE] = gradient
    gradient_buf[:, HEAD_SIZE:] = extra.astype(jnp.bfloat16)
    up_value_ref[...] += mm(low_part, gradient, BOTH_MAJOR)[:RANK, :]
    spread = jnp.transpose(gradient_low * inverse)[:RANK, :].astype(jnp.bfloat16)

    for tile in range(step_tiles):
        grad_weights = mm(gradient_buf[...], value_buf[near(tile), :], BOTH_MINOR)
        weights = weight_buf[:, cols(tile)]
        score_buf[:, cols(tile)] = weights * grad_weights.astype(jnp.bfloat16)
        value_back_ref[step + tile] += mm(spread, weights)

    sums = mm(score_buf[...], key_buf[window, :HEAD_SIZE]) * (inverse * SCORE_SCALE)
    turned = []
    for head in range(GROUPS):
        part = sums[own(head), :]
        turned.append(part * cosines - swap_halves(part) * sines)
    query_grad = jnp.concatenate(turned, axis=1).astype(jnp.bfloat16)
    up_query_ref[...] += mm(query_low_t_ref[...], query_grad)
    query_back_ref[step] += mm(query_up, query_grad, BOTH_MINOR)


def attention_chunk(first, last, place, mask, query_base, gradient, received, shared, carried):
    count = last - first
    tokens = query_base.shape[0]
    keys = 3 * tokens
    steps = tokens // SUB
    wide = pl.BlockSpec((SUB, GROUP_WIDTH), lambda i, j, *s: (j, first + i))
    near = pl.BlockSpec((tokens, HEAD_SIZE), lambda i, j, *s: (0, i))
    far = pl.BlockSpec((tokens, HEAD_SIZE), lambda i, j, *s: (0, count + i))
    table = pl.BlockSpec((SUB, HEAD_SIZE), lambda i, j, *s: (j, 0))

    def whole(*shape):
        return pl.BlockSpec(shape, lambda i, j, *s: (0,) * len(shape))

    in_specs = [
        wide,
        wide,
        *([near, far] * 4),
        pl.BlockSpec((RANK, GROUP_WIDTH), lambda i, j, *s: (0, first + i)),
        pl.BlockSpec((RANK, HEAD_SIZE), lambda i, j, *s: (0, first + i)),
        pl.BlockSpec((SUB, RANK), lambda i, j, *s: (j, 0)),
        pl.BlockSpec((RANK, SUB), lambda i, j, *s: (0, j)),
        table,
        table,
    ]
    arguments = [query_base, gradient]
    for array in received:
        arguments += [array, array]
    arguments += shared
    out_specs = [
        wide,
        pl.BlockSpec((RANK, GROUP_WIDTH), lambda i, j, *s: (0, i)),
        pl.BlockSpec((RANK, HEAD_SIZE), lambda i, j, *s: (0, i)),
        whole(steps, RANK, SUB),
        whole(keys // SUB, RANK, SUB),
    ]
    out_shape = [
        jax.ShapeDtypeStruct(query_base.shape, jnp.bfloat16),
        jax.ShapeDtypeStruct((RANK, count * GROUP_WIDTH), jnp.float32),
        jax.ShapeDtypeStruct((RANK, count * HEAD_SIZE), jnp.float32),
        jax.ShapeDtypeStruct((steps, RANK, SUB), jnp.float32),
        jax.ShapeDtypeStruct((keys // SUB, RANK, SUB), jnp.float32),
    ]
    aliases = {}
    if carried is None:
        scalars = (place, mask)
        in_specs += [pl.BlockSpec((RANK, tokens), lambda i, j, *s: (tokens // RANK, 0))] * 4
        arguments += received
        out_specs += [whole(keys, LANES)] * 2
        out_shape += [jax.ShapeDtypeStruct((keys, LANES), jnp.bfloat16)] * 2
    else:
        scalars = (place,)
        in_specs += [
            whole(keys, LANES),
            whole(keys, LANES),
            pl.BlockSpec(memory_space=pl.ANY),
            whole(steps, RANK, SUB),
            whole(keys // SUB, RANK, SUB),
        ]
        arguments += carried
        aliases = {len(scalars) + len(arguments) - 3: 0}
    rows = GROUPS * SUB
    wide_buf = HEAD_SIZE + LANES
    return pl.pallas_call(
        functools.partial(attention_kernel, carried is None),
        grid_spec=pltpu.PrefetchScalarGridSpec(
            num_scalar_prefetch=len(scalars),
            grid=(count, steps),
            in_specs=in_specs,
            out_specs=out_specs,
            scratch_shapes=[
                pltpu.VMEM((keys, wide_buf), jnp.bfloat16),
                pltpu.VMEM((keys, wide_buf), jnp.bfloat16),
                pltpu.VMEM((rows, wide_buf), jnp.bfloat16),
                pltpu.VMEM((rows, wide_buf), jnp.bfloat16),
                pltpu.VMEM((rows, KEYS), jnp.bfloat16),
                pltpu.VMEM((rows, KEYS), jnp.bfloat16),
                pltpu.VMEM((rows, wide_buf), jnp.float32),
            ],
        ),
        out_shape=out_shape,
        input_output_aliases=aliases,
        compiler_params=pltpu.CompilerParams(vmem_limit_bytes=32 * 2**20),
    )(*scalars, *arguments)


def head_sum(x):
    if lax.axis_size("head") == 2:
        return x + lax.ppermute(x, "head", [(0, 1), (1, 0)])
    return lax.psum(x, "head")


def group_exchange(x, groups):
    return lax.all_to_all(x, "ctx", 0, 0, axis_index_groups=groups)


def ctx_sum(x):
    devices = lax.axis_size("ctx")
    near = 4 if devices % 4 == 0 else 1
    far = devices // near
    near_groups = [[i * near + j for j in range(near)] for i in range(far)]
    far_groups = [[i * near + j for i in range(far)] for j in range(near)]
    columns = x.shape[1]
    piece = -(-columns // (near * LANES)) * LANES
    x = jnp.pad(x, ((0, 0), (0, near * piece - columns)))
    x = jnp.stack([x[:, i * piece : (i + 1) * piece] for i in range(near)])
    mine = jnp.sum(group_exchange(x, near_groups).astype(jnp.float32), axis=0).astype(jnp.bfloat16)
    mine = group_exchange(jnp.broadcast_to(mine[None], (far, RANK, piece)), far_groups)
    mine = jnp.sum(mine.astype(jnp.float32), axis=0).astype(jnp.bfloat16)
    x = group_exchange(jnp.broadcast_to(mine[None], (near, RANK, piece)), near_groups)
    return jnp.concatenate([x[i] for i in range(near)], axis=1)[:, :columns].astype(jnp.float32)


def after(value, *others):
    return lax.optimization_barrier((value, *others))[0]


def per_device(
    hidden_states,
    query_base,
    key_base,
    frozen_value_rows,
    query_down,
    query_up,
    value_down,
    value_up_weight,
    positions,
    block_mask,
    output_gradient,
):
    tokens = hidden_states.shape[0]
    devices = lax.axis_size("ctx")
    device_index = lax.axis_index("ctx")
    kv_heads = key_base.shape[1] // HEAD_SIZE
    forward_one = [(i, i + 1) for i in range(devices - 1)]
    even_two = [(i, i + 2) for i in range(0, devices - 2, 2)]
    even_one = [(i, i + 1) for i in range(0, devices - 1, 2)]

    both_down = jnp.concatenate([query_down, value_down], axis=1)
    low = head_sum(mm(both_down, hidden_states, (((0,), (1,)), ((), ())))).astype(jnp.bfloat16)
    query_low_t = low[:RANK]
    value_low_t = low[RANK:]

    half = np.arange(HEAD_SIZE // 2, dtype=np.float64)
    frequency = (ROPE_BASE ** (-2.0 * half / HEAD_SIZE)).astype(np.float32)[:, None]
    cosines, sines, *packed = pl.pallas_call(
        functools.partial(prologue_kernel, CHUNKS),
        out_shape=[
            jax.ShapeDtypeStruct((tokens, HEAD_SIZE), jnp.float32),
            jax.ShapeDtypeStruct((tokens, HEAD_SIZE), jnp.float32),
            *(
                jax.ShapeDtypeStruct(
                    (tokens + (RANK if first == 0 else 0), 2 * (last - first) * HEAD_SIZE),
                    jnp.bfloat16,
                )
                for first, last in CHUNKS
            ),
        ],
        compiler_params=pltpu.CompilerParams(vmem_limit_bytes=50 * 2**20),
    )(positions[None, :], jnp.asarray(frequency), key_base, frozen_value_rows)
    packed[0] = lax.dynamic_update_slice(packed[0], value_low_t, (tokens, 0))

    place = jnp.stack([device_index, device_index % 2]).astype(jnp.int32)
    shared = [query_up, value_up_weight, query_low_t.T, query_low_t, cosines, sines]

    ones, evens = [], []
    for chunk, own in enumerate(packed):
        if chunk > 0:
            own = after(own, ones[chunk - 1], evens[chunk - 1])
        ones.append(lax.ppermute(own, "ctx", forward_one))
        evens.append(lax.ppermute(own, "ctx", even_two))

    carried = None
    up_queries, up_values = [], []
    for chunk, (first, last) in enumerate(CHUNKS):
        one = ones[chunk]
        if carried is not None:
            one = after(one, carried[3])
        odd = lax.ppermute(one, "ctx", even_one)
        received = [packed[chunk], one, evens[chunk], odd]
        attention_out, up_query, up_value, query_back, value_back, *tables = attention_chunk(
            first,
            last,
            place,
            block_mask.T,
            query_base,
            output_gradient,
            received,
            shared,
            carried,
        )
        if carried is None:
            extras = tables
        carried = [*extras, attention_out, query_back, value_back]
        up_queries.append(up_query)
        up_values.append(up_value)

    steps = tokens // SUB
    back_one = lax.ppermute(value_back[steps : 2 * steps], "ctx", [(i + 1, i) for i in range(devices - 1)])
    back_two = lax.ppermute(value_back[:steps], "ctx", [(i + 2, i) for i in range(devices - 2)])
    value_back = value_back[2 * steps :] + back_one + back_two
    back = head_sum(jnp.concatenate([query_back, value_back], axis=1))
    back = jnp.concatenate([back[step] for step in range(steps)], axis=1).astype(jnp.bfloat16)
    down = mm(back, hidden_states)
    features = down.shape[1]
    partial = jnp.concatenate([down[:RANK], down[RANK:], *up_queries, *up_values], axis=1)
    summed = ctx_sum(partial.astype(jnp.bfloat16)) * ((devices * tokens) ** (-0.5))
    query_columns = kv_heads * GROUP_WIDTH
    up_first = 2 * features
    return (
        attention_out,
        summed[:, :features].T,
        summed[:, up_first : up_first + query_columns],
        summed[:, features:up_first].T,
        summed[:, up_first + query_columns :],
    )


def solution(mesh):
    placed = (
        P("ctx", "head"),
        P("ctx", "head"),
        P("ctx", "head"),
        P("ctx", "head"),
        P("head", None),
        P(None, "head"),
        P("head", None),
        P(None, "head"),
        P("ctx"),
        P(),
        P("ctx", "head"),
    )
    return jax.shard_map(
        per_device,
        mesh=mesh,
        in_specs=placed,
        out_specs=(
            P("ctx", "head"),
            P("head", None),
            P(None, "head"),
            P("head", None),
            P(None, "head"),
        ),
        check_vma=False,
    )
```

```python
import functools

import jax
import jax.numpy as jnp
import numpy as np
from jax import lax
from jax.experimental import pallas as pl
from jax.experimental.pallas import tpu as pltpu
from jax.sharding import PartitionSpec as P

D = 5376
QUERY_HEADS = 32
KEY_VALUE_HEADS = 16
HEAD_SIZE = 128
WINDOW = 1024
BLOCK = 128
GROUPS = QUERY_HEADS // KEY_VALUE_HEADS
GROUP_WIDTH = GROUPS * HEAD_SIZE
SCORE_SCALE = (D // QUERY_HEADS) ** (-0.5)
LOG2_E = 1.4426950408889634
ROPE_BASE = 10000.0
FORBIDDEN = -1e30
RANK = 16

SUB = 256
KEYS = SUB + WINDOW
LANES = 128
OFFSET_LANE = 64
ONES_LANE = RANK

CHUNKS = ((0, 2), (2, 5), (5, 8))

ROWS_BY_COLS = (((1,), (0,)), ((), ()))
BOTH_MINOR = (((1,), (1,)), ((), ()))
BOTH_MAJOR = (((0,), (0,)), ((), ()))


def mm(left, right, dims=ROWS_BY_COLS):
    return lax.dot_general(left, right, dims, preferred_element_type=jnp.float32)


def swap_halves(x):
    return pltpu.roll(x, HEAD_SIZE // 2, 1)


def prologue_kernel(chunks, positions_ref, frequency_ref, key_ref, value_ref, cos_ref, sin_ref, *outs):
    tokens = key_ref.shape[0]
    half = HEAD_SIZE // 2
    angles = frequency_ref[...] * positions_ref[...].astype(jnp.float32)
    both = jnp.transpose(jnp.concatenate([jnp.cos(angles), jnp.sin(angles)], axis=0))
    turned = swap_halves(both)
    low_half = lax.broadcasted_iota(jnp.int32, both.shape, 1) < half
    cosines = jnp.where(low_half, both, turned)
    sines = jnp.where(low_half, -turned, both)
    cos_ref[...] = cosines
    sin_ref[...] = sines
    own = pl.ds(0, tokens)
    for (first, last), out_ref in zip(chunks, outs):
        count = last - first
        for head in range(first, last):
            cols = pl.ds(head * HEAD_SIZE, HEAD_SIZE)
            key = key_ref[:, cols].astype(jnp.float32)
            rotated = key * cosines + swap_halves(key) * sines
            out_ref[own, pl.ds((head - first) * HEAD_SIZE, HEAD_SIZE)] = rotated.astype(jnp.bfloat16)
            out_ref[own, pl.ds((count + head - first) * HEAD_SIZE, HEAD_SIZE)] = value_ref[:, cols]


def attention_kernel(first, start, place_ref, *refs):
    if first:
        mask_ref, *refs = refs
    (
        query_hbm,
        gradient_hbm,
        own_ref,
        one_ref,
        even_ref,
        odd_ref,
        query_up_ref,
        value_up_ref,
        query_low_ref,
        query_low_t_ref,
        cos_ref,
        sin_ref,
        *refs,
    ) = refs
    if not first:
        key_extra_in, value_extra_in, _, query_back_in, value_back_in, *refs = refs
    out_hbm, up_query_ref, up_value_ref, query_back_ref, value_back_ref, *refs = refs
    if first:
        key_extra_ref, value_extra_ref, *refs = refs
    else:
        key_extra_ref, value_extra_ref = key_extra_in, value_extra_in
    (
        query_in,
        gradient_in,
        out_buf,
        key_buf,
        value_buf,
        query_buf,
        gradient_buf,
        weight_buf,
        score_buf,
        product_buf,
        sems,
    ) = refs
    heads = key_buf.shape[0]
    tokens = query_in.shape[0]
    keys = key_buf.shape[1]
    steps = tokens // SUB
    tiles = keys // SUB
    step_tiles = KEYS // SUB
    rows = GROUPS * SUB
    odd = place_ref[1] == 1

    chunk_cols = pl.ds(start * GROUP_WIDTH, heads * GROUP_WIDTH)
    query_copy = pltpu.make_async_copy(query_hbm.at[:, chunk_cols], query_in, sems.at[0])
    gradient_copy = pltpu.make_async_copy(gradient_hbm.at[:, chunk_cols], gradient_in, sems.at[1])
    query_copy.start()
    gradient_copy.start()

    if first:
        first_block = place_ref[0] * (tokens // BLOCK)
        reach = WINDOW // BLOCK
        block_lane = lax.broadcasted_iota(jnp.int32, (BLOCK, LANES), 1)
        for key_block in range(keys // BLOCK):
            extra = jnp.where(block_lane == OFFSET_LANE, 1.0, 0.0)
            exists = first_block + (key_block - reach) >= 0
            for block in range(tokens // BLOCK):
                offset = reach + block - key_block
                if 0 <= offset <= reach:
                    hit = (mask_ref[offset, first_block + block] == 1) & exists
                    term = jnp.where(hit, 0.0, FORBIDDEN)
                else:
                    term = FORBIDDEN
                extra = jnp.where(block_lane == block, term, extra)
            key_extra_ref[key_block * BLOCK : (key_block + 1) * BLOCK, :] = extra.astype(jnp.bfloat16)
        last = slice(tokens, tokens + RANK)
        low_far = jnp.where(odd, odd_ref[last, :], even_ref[last, :])
        low = jnp.concatenate([low_far, one_ref[last, :], own_ref[last, :]], axis=1)
        low = jnp.concatenate(
            [
                low.astype(jnp.float32),
                jnp.ones((2, keys), jnp.float32),
                jnp.zeros((LANES - RANK - 2, keys), jnp.float32),
            ],
            axis=0,
        )
        value_extra_ref[...] = jnp.transpose(low).astype(jnp.bfloat16)
        query_back_ref[...] = jnp.zeros_like(query_back_ref)
        value_back_ref[...] = jnp.zeros_like(value_back_ref)
    else:
        query_back_ref[...] = query_back_in[...]
        value_back_ref[...] = value_back_in[...]

    lane = lax.broadcasted_iota(jnp.int32, (rows, LANES), 1)
    row = lax.broadcasted_iota(jnp.int32, (rows, LANES), 0) % SUB
    ones = slice(HEAD_SIZE + ONES_LANE, HEAD_SIZE + ONES_LANE + 1)

    def own(step):
        return slice(step * SUB, (step + 1) * SUB)

    def span(step):
        return slice(step * rows, (step + 1) * rows)

    def window(step):
        return slice(step * SUB, step * SUB + KEYS)

    def tile_steps(tile):
        return max(0, tile - step_tiles + 1), min(steps, tile + 1)

    def group_cols(head, member):
        return slice((head * GROUPS + member) * HEAD_SIZE, (head * GROUPS + member + 1) * HEAD_SIZE)

    def query_up_of(head):
        at = (start + head) * GROUP_WIDTH
        return query_up_ref[:, at : at + GROUP_WIDTH]

    def value_up_of(head):
        at = (start + head) * HEAD_SIZE
        return jnp.concatenate(
            [value_up_ref[:, at : at + HEAD_SIZE], jnp.zeros((LANES - RANK, HEAD_SIZE), jnp.bfloat16)],
            axis=0,
        )

    def limit(step, tile, part):
        place = tile - step
        if 0 < place < step_tiles - 1:
            return part
        halves = []
        for block in range(SUB // BLOCK):
            inside = lane > row % BLOCK if place == 0 else lane <= row % BLOCK
            inside = inside | (row // BLOCK != block)
            halves.append(
                jnp.where(inside, part[:, block * BLOCK : (block + 1) * BLOCK], FORBIDDEN)
            )
        return jnp.concatenate(halves, axis=1)

    def fill(head):
        for buf, extra_ref, at in (
            (key_buf, key_extra_ref, head * HEAD_SIZE),
            (value_buf, value_extra_ref, (heads + head) * HEAD_SIZE),
        ):
            cols = slice(at, at + HEAD_SIZE)
            buf[head, 0:tokens, :HEAD_SIZE] = jnp.where(
                odd, odd_ref[0:tokens, cols], even_ref[0:tokens, cols]
            )
            buf[head, tokens : 2 * tokens, :HEAD_SIZE] = one_ref[0:tokens, cols]
            buf[head, 2 * tokens :, :HEAD_SIZE] = own_ref[0:tokens, cols]
            buf[head, :, HEAD_SIZE:] = extra_ref[...]

    def prepare(head):
        reach_of_key = jnp.max(
            jnp.abs(key_buf[head, :, :HEAD_SIZE].astype(jnp.float32)), axis=0, keepdims=True
        )
        for step in range(steps):
            cosines = cos_ref[own(step), :]
            sines = sin_ref[own(step), :]
            adapted = mm(query_low_ref[own(step), :], query_up_of(head))
            turned = []
            for member in range(GROUPS):
                part = query_in[own(step), group_cols(head, member)].astype(jnp.float32)
                part = part + adapted[:, member * HEAD_SIZE : (member + 1) * HEAD_SIZE]
                turned.append(part * cosines + swap_halves(part) * sines)
            queries = jnp.concatenate(turned, axis=0) * (SCORE_SCALE * LOG2_E)
            bound = jnp.sum(jnp.abs(queries) * reach_of_key, axis=1, keepdims=True)
            chosen = (lane == row // BLOCK + step * (SUB // BLOCK)).astype(jnp.float32)
            query_buf[head, span(step), :HEAD_SIZE] = queries.astype(jnp.bfloat16)
            query_buf[head, span(step), HEAD_SIZE:] = jnp.where(
                lane == OFFSET_LANE, -bound, chosen
            ).astype(jnp.bfloat16)

    def forward_scores(head):
        for tile in range(tiles):
            low, high = tile_steps(tile)
            cols = slice(tile * SUB, (tile + 1) * SUB)
            scores = mm(
                query_buf[head, low * rows : high * rows, :], key_buf[head, cols, :], BOTH_MINOR
            )
            for step in range(low, high):
                part = limit(step, tile, scores[(step - low) * rows : (step - low + 1) * rows, :])
                weight_buf[head, span(step), cols] = jnp.exp2(part).astype(jnp.bfloat16)

    def forward_products(head):
        for step in range(steps):
            product_buf[head, span(step), :] = mm(
                weight_buf[head, span(step), window(step)], value_buf[head, window(step), :]
            )

    def repeat(head, carry):
        for step in range(steps):
            extra = query_buf[head, span(step), HEAD_SIZE:].astype(jnp.float32)
            query_buf[head, span(step), HEAD_SIZE:] = jnp.where(lane == OFFSET_LANE, 0.0, extra).astype(
                jnp.bfloat16
            )
            highest = jnp.full((rows, 1), FORBIDDEN, jnp.float32)
            for tile in range(step, step + step_tiles):
                cols = slice(tile * SUB, (tile + 1) * SUB)
                part = mm(query_buf[head, span(step), :], key_buf[head, cols, :], BOTH_MINOR)
                part = limit(step, tile, part)
                highest = jnp.maximum(highest, jnp.max(part, axis=1, keepdims=True))
            query_buf[head, span(step), HEAD_SIZE:] = jnp.where(
                lane == OFFSET_LANE, -highest, extra
            ).astype(jnp.bfloat16)
        forward_scores(head)
        forward_products(head)
        return carry

    kept = {}

    def finish_forward(head):
        value_up = value_up_of(head)
        spreads = []
        inverses = []
        up_value = jnp.zeros((LANES, HEAD_SIZE), jnp.float32)
        for step in range(steps):
            gradient = jnp.concatenate(
                [gradient_in[own(step), group_cols(head, member)] for member in range(GROUPS)], axis=0
            )
            gradient_low = mm(gradient, value_up, BOTH_MINOR)
            inverse = 1.0 / product_buf[head, span(step), ones]
            low_part = (product_buf[head, span(step), HEAD_SIZE:] * inverse).astype(jnp.bfloat16)
            outputs = product_buf[head, span(step), :HEAD_SIZE] * inverse + mm(low_part, value_up)
            outputs = outputs.astype(jnp.bfloat16)
            for member in range(GROUPS):
                out_buf[own(step), group_cols(head, member)] = outputs[own(member), :]
            delta = jnp.sum(
                outputs.astype(jnp.float32) * gradient.astype(jnp.float32), axis=1, keepdims=True
            )
            delta_high = delta.astype(jnp.bfloat16).astype(jnp.float32)
            extra = jnp.where(lane == ONES_LANE, -delta_high, gradient_low)
            extra = jnp.where(lane == ONES_LANE + 1, delta_high - delta, extra)
            gradient_buf[head, span(step), :HEAD_SIZE] = gradient
            gradient_buf[head, span(step), HEAD_SIZE:] = extra.astype(jnp.bfloat16)
            up_value += mm(low_part, gradient, BOTH_MAJOR)
            spreads.append(jnp.transpose(gradient_low * inverse)[:RANK, :].astype(jnp.bfloat16))
            inverses.append(inverse * SCORE_SCALE)
        up_value_ref[:, head * HEAD_SIZE : (head + 1) * HEAD_SIZE] = up_value[:RANK, :]
        kept[head] = jnp.concatenate(spreads, axis=1), inverses

    def backward_scores(head):
        spread = kept[head][0]
        for tile in range(tiles):
            low, high = tile_steps(tile)
            cols = slice(tile * SUB, (tile + 1) * SUB)
            part = slice(low * rows, high * rows)
            grad_weights = mm(gradient_buf[head, part, :], value_buf[head, cols, :], BOTH_MINOR)
            weights = weight_buf[head, part, cols]
            score_buf[head, part, cols] = weights * grad_weights.astype(jnp.bfloat16)
            value_back_ref[:, cols] += mm(spread[:, part], weights)

    def backward_products(head):
        query_grads = []
        for step in range(steps):
            cosines = cos_ref[own(step), :]
            sines = sin_ref[own(step), :]
            sums = mm(score_buf[head, span(step), window(step)], key_buf[head, window(step), :HEAD_SIZE])
            sums = sums * kept[head][1][step]
            turned = []
            for member in range(GROUPS):
                part = sums[own(member), :]
                turned.append(part * cosines - swap_halves(part) * sines)
            query_grads.append(jnp.concatenate(turned, axis=1).astype(jnp.bfloat16))
        query_grad = jnp.concatenate(query_grads, axis=0)
        up_query_ref[:, head * GROUP_WIDTH : (head + 1) * GROUP_WIDTH] = mm(
            query_low_t_ref[...], query_grad
        )
        query_back_ref[...] += mm(query_up_of(head), query_grad, BOTH_MINOR)

    for head in range(heads):
        fill(head)
    query_copy.wait()
    prepare(0)
    for head in range(heads):
        forward_scores(head)
        if head + 1 < heads:
            prepare(head + 1)
        forward_products(head)

    @pl.when(jnp.min(product_buf[:, :, ones]) < 1e-18)
    def _():
        lax.fori_loop(0, heads, repeat, 0)

    gradient_copy.wait()
    finish_forward(0)
    for head in range(heads):
        backward_scores(head)
        if head + 1 < heads:
            finish_forward(head + 1)
        backward_products(head)
    out_copy = pltpu.make_async_copy(out_buf, out_hbm.at[:, chunk_cols], sems.at[2])
    out_copy.start()
    out_copy.wait()


def attention_chunk(first, last, place, mask, query_base, gradient, received, shared, carried):
    count = last - first
    tokens = query_base.shape[0]
    keys = 3 * tokens
    rows = GROUPS * tokens
    whole = pl.BlockSpec(memory_space=pltpu.VMEM)
    scalar = pl.BlockSpec(memory_space=pltpu.SMEM)
    remote = pl.BlockSpec(memory_space=pl.ANY)
    out_specs = [remote, whole, whole, whole, whole]
    out_shape = [
        jax.ShapeDtypeStruct(query_base.shape, jnp.bfloat16),
        jax.ShapeDtypeStruct((RANK, count * GROUP_WIDTH), jnp.float32),
        jax.ShapeDtypeStruct((RANK, count * HEAD_SIZE), jnp.float32),
        jax.ShapeDtypeStruct((RANK, tokens), jnp.float32),
        jax.ShapeDtypeStruct((RANK, keys), jnp.float32),
    ]
    aliases = {}
    if carried is None:
        scalars = [place, mask]
        out_specs += [whole, whole]
        out_shape += [jax.ShapeDtypeStruct((keys, LANES), jnp.bfloat16)] * 2
        carried = []
    else:
        scalars = [place]
    arguments = [query_base, gradient, *received, *shared, *carried]
    in_specs = [remote, remote] + [whole] * (len(arguments) - 2)
    if carried:
        in_specs[-3] = remote
        aliases = {len(scalars) + len(arguments) - 3: 0}
    wide_buf = HEAD_SIZE + LANES
    return pl.pallas_call(
        functools.partial(attention_kernel, not carried, first),
        in_specs=[scalar] * len(scalars) + in_specs,
        out_specs=out_specs,
        scratch_shapes=[
            pltpu.VMEM((tokens, count * GROUP_WIDTH), jnp.bfloat16),
            pltpu.VMEM((tokens, count * GROUP_WIDTH), jnp.bfloat16),
            pltpu.VMEM((tokens, count * GROUP_WIDTH), jnp.bfloat16),
            pltpu.VMEM((count, keys, wide_buf), jnp.bfloat16),
            pltpu.VMEM((count, keys, wide_buf), jnp.bfloat16),
            pltpu.VMEM((count, rows, wide_buf), jnp.bfloat16),
            pltpu.VMEM((count, rows, wide_buf), jnp.bfloat16),
            pltpu.VMEM((count, rows, keys), jnp.bfloat16),
            pltpu.VMEM((count, rows, keys), jnp.bfloat16),
            pltpu.VMEM((count, rows, wide_buf), jnp.float32),
            pltpu.SemaphoreType.DMA((3,)),
        ],
        out_shape=out_shape,
        input_output_aliases=aliases,
        compiler_params=pltpu.CompilerParams(vmem_limit_bytes=50 * 2**20),
    )(*scalars, *arguments)


def head_sum(x):
    if lax.axis_size("head") == 2:
        return x + lax.ppermute(x, "head", [(0, 1), (1, 0)])
    return lax.psum(x, "head")


def ctx_sum(x):
    devices = lax.axis_size("ctx")
    near = 4
    index = lax.axis_index("ctx")

    def exchange(value, distance):
        return lax.ppermute(value, "ctx", [(i, i ^ distance) for i in range(devices)])

    columns = x.shape[1]
    piece = -(-columns // (near * LANES)) * LANES
    x = jnp.pad(x, ((0, 0), (0, near * piece - columns)))
    place = index % near
    pieces = [
        lax.dynamic_slice_in_dim(x, (place ^ distance) * piece, piece, 1) for distance in range(near)
    ]
    mine = pieces[0].astype(jnp.float32)
    for distance in range(1, near):
        mine = mine + exchange(pieces[distance], distance).astype(jnp.float32)
    distance = near
    while distance < devices:
        mine = mine.astype(jnp.bfloat16)
        mine = mine.astype(jnp.float32) + exchange(mine, distance).astype(jnp.float32)
        distance *= 2
    mine = mine.astype(jnp.bfloat16)
    gathered = [mine] + [exchange(mine, distance) for distance in range(1, near)]
    parts = []
    for at in range(near):
        part = gathered[0]
        for distance in range(1, near):
            part = jnp.where((place ^ at) == distance, gathered[distance], part)
        parts.append(part)
    return jnp.concatenate(parts, axis=1)[:, :columns].astype(jnp.float32)


def after(value, *others):
    return lax.optimization_barrier((value, *others))[0]


def per_device(
    hidden_states,
    query_base,
    key_base,
    frozen_value_rows,
    query_down,
    query_up,
    value_down,
    value_up_weight,
    positions,
    block_mask,
    output_gradient,
):
    tokens = hidden_states.shape[0]
    devices = lax.axis_size("ctx")
    device_index = lax.axis_index("ctx")
    kv_heads = key_base.shape[1] // HEAD_SIZE
    forward_one = [(i, i + 1) for i in range(devices - 1)]
    even_two = [(i, i + 2) for i in range(0, devices - 2, 2)]
    even_one = [(i, i + 1) for i in range(0, devices - 1, 2)]

    both_down = jnp.concatenate([query_down, value_down], axis=1)
    low = head_sum(mm(both_down, hidden_states, (((0,), (1,)), ((), ())))).astype(jnp.bfloat16)
    query_low_t = low[:RANK]
    value_low_t = low[RANK:]

    half = np.arange(HEAD_SIZE // 2, dtype=np.float64)
    frequency = (ROPE_BASE ** (-2.0 * half / HEAD_SIZE)).astype(np.float32)[:, None]
    cosines, sines, *packed = pl.pallas_call(
        functools.partial(prologue_kernel, CHUNKS),
        out_shape=[
            jax.ShapeDtypeStruct((tokens, HEAD_SIZE), jnp.float32),
            jax.ShapeDtypeStruct((tokens, HEAD_SIZE), jnp.float32),
            *(
                jax.ShapeDtypeStruct(
                    (tokens + (RANK if first == 0 else 0), 2 * (last - first) * HEAD_SIZE),
                    jnp.bfloat16,
                )
                for first, last in CHUNKS
            ),
        ],
        compiler_params=pltpu.CompilerParams(vmem_limit_bytes=50 * 2**20),
    )(positions[None, :], jnp.asarray(frequency), key_base, frozen_value_rows)
    packed[0] = lax.dynamic_update_slice(packed[0], value_low_t, (tokens, 0))

    place = jnp.stack([device_index, device_index % 2]).astype(jnp.int32)
    shared = [query_up, value_up_weight, query_low_t.T, query_low_t, cosines, sines]

    ones, evens = [], []
    for chunk, own in enumerate(packed):
        if chunk > 0:
            own = after(own, ones[chunk - 1], evens[chunk - 1])
        ones.append(lax.ppermute(own, "ctx", forward_one))
        evens.append(lax.ppermute(own, "ctx", even_two))

    carried = None
    up_queries, up_values = [], []
    for chunk, (first, last) in enumerate(CHUNKS):
        one = ones[chunk]
        if carried is not None:
            one = after(one, carried[3])
        odd = lax.ppermute(one, "ctx", even_one)
        received = [packed[chunk], one, evens[chunk], odd]
        attention_out, up_query, up_value, query_back, value_back, *tables = attention_chunk(
            first,
            last,
            place,
            block_mask.T,
            query_base,
            output_gradient,
            received,
            shared,
            carried,
        )
        if carried is None:
            extras = tables
        carried = [*extras, attention_out, query_back, value_back]
        up_queries.append(up_query)
        up_values.append(up_value)

    def back_by(value, distance, cross):
        pairs = []
        for i in range(devices - distance):
            for j in range(2):
                pairs.append(((i + distance) * 2 + j, i * 2 + (1 - j if cross else j)))
        return lax.ppermute(value, ("ctx", "head"), pairs)

    back_own = jnp.concatenate([query_back, value_back[:, 2 * tokens :]], axis=0)
    back_one = value_back[:, tokens : 2 * tokens]
    back_two = value_back[:, :tokens]
    arrived = [
        back_by(value, distance, cross)
        for distance, value in ((2, back_two), (1, back_one))
        for cross in (True, False)
    ]
    back = back_own + back_by(back_own, 0, True)
    back = jnp.concatenate([back[:RANK], back[RANK:] + sum(arrived)], axis=0).astype(jnp.bfloat16)
    down = mm(back, hidden_states)
    features = down.shape[1]
    partial = jnp.concatenate([down[:RANK], down[RANK:], *up_queries, *up_values], axis=1)
    summed = ctx_sum(partial.astype(jnp.bfloat16)) * ((devices * tokens) ** (-0.5))
    query_columns = kv_heads * GROUP_WIDTH
    up_first = 2 * features
    return (
        attention_out,
        summed[:, :features].T,
        summed[:, up_first : up_first + query_columns],
        summed[:, features:up_first].T,
        summed[:, up_first + query_columns :],
    )


def solution(mesh):
    placed = (
        P("ctx", "head"),
        P("ctx", "head"),
        P("ctx", "head"),
        P("ctx", "head"),
        P("head", None),
        P(None, "head"),
        P("head", None),
        P(None, "head"),
        P("ctx"),
        P(),
        P("ctx", "head"),
    )
    return jax.shard_map(
        per_device,
        mesh=mesh,
        in_specs=placed,
        out_specs=(
            P("ctx", "head"),
            P("head", None),
            P(None, "head"),
            P("head", None),
            P(None, "head"),
        ),
        check_vma=False,
    )
```

```python
import functools

import jax
import jax.numpy as jnp
import numpy as np
from jax import lax
from jax.experimental import pallas as pl
from jax.experimental.pallas import tpu as pltpu
from jax.sharding import PartitionSpec as P

D = 5376
QUERY_HEADS = 32
KEY_VALUE_HEADS = 16
HEAD_SIZE = 128
WINDOW = 1024
BLOCK = 128
GROUPS = QUERY_HEADS // KEY_VALUE_HEADS
GROUP_WIDTH = GROUPS * HEAD_SIZE
SCORE_SCALE = (D // QUERY_HEADS) ** (-0.5)
LOG2_E = 1.4426950408889634
ROPE_BASE = 10000.0
FORBIDDEN = -1e30
RANK = 16

SUB = 256
KEYS = SUB + WINDOW
LANES = 128
OFFSET_LANE = 64
ONES_LANE = RANK

CHUNKS = ((0, 2), (2, 5), (5, 8))

ROWS_BY_COLS = (((1,), (0,)), ((), ()))
BOTH_MINOR = (((1,), (1,)), ((), ()))
BOTH_MAJOR = (((0,), (0,)), ((), ()))


def mm(left, right, dims=ROWS_BY_COLS):
    return lax.dot_general(left, right, dims, preferred_element_type=jnp.float32)


def swap_halves(x):
    return pltpu.roll(x, HEAD_SIZE // 2, 1)


def rotate_into(chunks, cosines, sines, key_ref, value_ref, outs):
    own = pl.ds(0, key_ref.shape[0])
    for (first, last), out_ref in zip(chunks, outs):
        count = last - first
        for head in range(first, last):
            cols = pl.ds(head * HEAD_SIZE, HEAD_SIZE)
            key = key_ref[:, cols].astype(jnp.float32)
            rotated = key * cosines + swap_halves(key) * sines
            out_ref[own, pl.ds((head - first) * HEAD_SIZE, HEAD_SIZE)] = rotated.astype(jnp.bfloat16)
            out_ref[own, pl.ds((count + head - first) * HEAD_SIZE, HEAD_SIZE)] = value_ref[:, cols]


def prologue_kernel(chunks, positions_ref, frequency_ref, key_ref, value_ref, cos_ref, sin_ref, *outs):
    half = HEAD_SIZE // 2
    angles = frequency_ref[...] * positions_ref[...].astype(jnp.float32)
    both = jnp.transpose(jnp.concatenate([jnp.cos(angles), jnp.sin(angles)], axis=0))
    turned = swap_halves(both)
    low_half = lax.broadcasted_iota(jnp.int32, both.shape, 1) < half
    cosines = jnp.where(low_half, both, turned)
    sines = jnp.where(low_half, -turned, both)
    cos_ref[...] = cosines
    sin_ref[...] = sines
    rotate_into(chunks, cosines, sines, key_ref, value_ref, outs)


def later_prologue_kernel(chunks, cos_ref, sin_ref, key_ref, value_ref, *outs):
    rotate_into(chunks, cos_ref[...], sin_ref[...], key_ref, value_ref, outs)


def attention_kernel(first, start, up_columns, place_ref, *refs):
    if first:
        mask_ref, *refs = refs
    (
        query_hbm,
        gradient_hbm,
        own_hbm,
        one_hbm,
        even_hbm,
        odd_hbm,
        query_up_ref,
        value_up_ref,
        query_low_ref,
        query_low_t_ref,
        cos_ref,
        sin_ref,
        *refs,
    ) = refs
    if not first:
        key_extra_hbm, value_extra_hbm, _, _, query_back_in, value_back_in, *refs = refs
    out_hbm, partial_hbm, query_back_ref, value_back_ref, *refs = refs
    if first:
        key_extra_hbm, value_extra_hbm, *refs = refs
    (
        query_in,
        gradient_in,
        out_buf,
        up_query_buf,
        up_value_buf,
        low_buf,
        key_buf,
        value_buf,
        query_buf,
        gradient_buf,
        weight_buf,
        score_buf,
        product_buf,
        sems,
        head_sems,
    ) = refs
    heads = key_buf.shape[0]
    tokens = query_in.shape[0]
    keys = key_buf.shape[1]
    steps = tokens // SUB
    tiles = keys // SUB
    step_tiles = KEYS // SUB
    rows = GROUPS * SUB
    odd = place_ref[1] == 1

    def copy(source, target, sem):
        return pltpu.make_async_copy(source, target, sem)

    def start_far(even_source, odd_source, target, sem):
        @pl.when(odd)
        def _():
            copy(odd_source, target, sem).start()

        @pl.when(jnp.logical_not(odd))
        def _():
            copy(even_source, target, sem).start()

        return copy(even_source, target, sem)

    own_rows = pl.ds(0, tokens)
    low_copies = []
    if first:
        last = pl.ds(tokens, RANK)
        low_copies.append(start_far(even_hbm.at[last], odd_hbm.at[last], low_buf.at[0], sems.at[3]))
        for at, source in ((1, one_hbm), (2, own_hbm)):
            low_copies.append(copy(source.at[last], low_buf.at[at], sems.at[3 + at]))
            low_copies[-1].start()
    chunk_cols = pl.ds(start * GROUP_WIDTH, heads * GROUP_WIDTH)
    query_copy = copy(query_hbm.at[:, chunk_cols], query_in, sems.at[0])
    query_copy.start()
    in_copies = []
    for head in range(heads):
        in_copies.append([])
        for kind, buf, at in ((0, key_buf, head), (1, value_buf, heads + head)):
            cols = pl.ds(at * HEAD_SIZE, HEAD_SIZE)
            main = pl.ds(0, HEAD_SIZE)
            sem = head_sems.at[head, kind]
            copies = [
                start_far(
                    even_hbm.at[own_rows, cols],
                    odd_hbm.at[own_rows, cols],
                    buf.at[head, pl.ds(0, tokens), main],
                    sem.at[0],
                ),
                copy(one_hbm.at[own_rows, cols], buf.at[head, pl.ds(tokens, tokens), main], sem.at[1]),
                copy(own_hbm.at[own_rows, cols], buf.at[head, pl.ds(2 * tokens, tokens), main], sem.at[2]),
            ]
            if not first:
                extra_hbm = (key_extra_hbm, value_extra_hbm)[kind]
                copies.append(copy(extra_hbm, buf.at[head, :, pl.ds(HEAD_SIZE, LANES)], sem.at[3]))
            for later in copies[1:]:
                later.start()
            in_copies[head].append(copies)
    gradient_copy = copy(gradient_hbm.at[:, chunk_cols], gradient_in, sems.at[1])
    gradient_copy.start()

    if first:
        first_block = place_ref[0] * (tokens // BLOCK)
        reach = WINDOW // BLOCK
        block_lane = lax.broadcasted_iota(jnp.int32, (BLOCK, LANES), 1)
        for key_block in range(keys // BLOCK):
            extra = jnp.where(block_lane == OFFSET_LANE, 1.0, 0.0)
            exists = first_block + (key_block - reach) >= 0
            for block in range(tokens // BLOCK):
                offset = reach + block - key_block
                if 0 <= offset <= reach:
                    hit = (mask_ref[offset, first_block + block] == 1) & exists
                    term = jnp.where(hit, 0.0, FORBIDDEN)
                else:
                    term = FORBIDDEN
                extra = jnp.where(block_lane == block, term, extra)
            for head in range(heads):
                key_buf[head, key_block * BLOCK : (key_block + 1) * BLOCK, HEAD_SIZE:] = extra.astype(
                    jnp.bfloat16
                )
        for low_copy in low_copies:
            low_copy.wait()
        low = jnp.concatenate([low_buf[at] for at in range(3)], axis=1)
        low = jnp.concatenate(
            [
                low.astype(jnp.float32),
                jnp.ones((2, keys), jnp.float32),
                jnp.zeros((LANES - RANK - 2, keys), jnp.float32),
            ],
            axis=0,
        )
        low = jnp.transpose(low).astype(jnp.bfloat16)
        for head in range(heads):
            value_buf[head, :, HEAD_SIZE:] = low
        extras = (
            copy(key_buf.at[0, :, pl.ds(HEAD_SIZE, LANES)], key_extra_hbm, sems.at[6]),
            copy(value_buf.at[0, :, pl.ds(HEAD_SIZE, LANES)], value_extra_hbm, sems.at[7]),
        )
        for extra_copy in extras:
            extra_copy.start()
        query_back_ref[...] = jnp.zeros_like(query_back_ref)
        value_back_ref[...] = jnp.zeros_like(value_back_ref)
    else:
        extras = ()
        query_back_ref[...] = query_back_in[...]
        value_back_ref[...] = value_back_in[...]

    lane = lax.broadcasted_iota(jnp.int32, (rows, LANES), 1)
    row = lax.broadcasted_iota(jnp.int32, (rows, LANES), 0) % SUB
    ones = slice(HEAD_SIZE + ONES_LANE, HEAD_SIZE + ONES_LANE + 1)

    def own(step):
        return slice(step * SUB, (step + 1) * SUB)

    def span(step):
        return slice(step * rows, (step + 1) * rows)

    def window(step):
        return slice(step * SUB, step * SUB + KEYS)

    def tile_steps(tile):
        return max(0, tile - step_tiles + 1), min(steps, tile + 1)

    def group_cols(head, member):
        return slice((head * GROUPS + member) * HEAD_SIZE, (head * GROUPS + member + 1) * HEAD_SIZE)

    def query_up_of(head):
        at = (start + head) * GROUP_WIDTH
        return query_up_ref[:, at : at + GROUP_WIDTH]

    def value_up_of(head):
        at = (start + head) * HEAD_SIZE
        return jnp.concatenate(
            [value_up_ref[:, at : at + HEAD_SIZE], jnp.zeros((LANES - RANK, HEAD_SIZE), jnp.bfloat16)],
            axis=0,
        )

    def limit(step, tile, part):
        place = tile - step
        if 0 < place < step_tiles - 1:
            return part
        halves = []
        for block in range(SUB // BLOCK):
            inside = lane > row % BLOCK if place == 0 else lane <= row % BLOCK
            inside = inside | (row // BLOCK != block)
            halves.append(
                jnp.where(inside, part[:, block * BLOCK : (block + 1) * BLOCK], FORBIDDEN)
            )
        return jnp.concatenate(halves, axis=1)

    def prepare(head):
        reach_of_key = jnp.max(
            jnp.abs(key_buf[head, :, :HEAD_SIZE].astype(jnp.float32)), axis=0, keepdims=True
        )
        for step in range(steps):
            cosines = cos_ref[own(step), :]
            sines = sin_ref[own(step), :]
            adapted = mm(query_low_ref[own(step), :], query_up_of(head))
            turned = []
            for member in range(GROUPS):
                part = query_in[own(step), group_cols(head, member)].astype(jnp.float32)
                part = part + adapted[:, member * HEAD_SIZE : (member + 1) * HEAD_SIZE]
                turned.append(part * cosines + swap_halves(part) * sines)
            queries = jnp.concatenate(turned, axis=0) * (SCORE_SCALE * LOG2_E)
            bound = jnp.sum(jnp.abs(queries) * reach_of_key, axis=1, keepdims=True)
            chosen = (lane == row // BLOCK + step * (SUB // BLOCK)).astype(jnp.float32)
            query_buf[head, span(step), :HEAD_SIZE] = queries.astype(jnp.bfloat16)
            query_buf[head, span(step), HEAD_SIZE:] = jnp.where(
                lane == OFFSET_LANE, -bound, chosen
            ).astype(jnp.bfloat16)

    def forward_scores(head):
        for tile in range(tiles):
            low, high = tile_steps(tile)
            cols = slice(tile * SUB, (tile + 1) * SUB)
            scores = mm(
                query_buf[head, low * rows : high * rows, :], key_buf[head, cols, :], BOTH_MINOR
            )
            for step in range(low, high):
                part = limit(step, tile, scores[(step - low) * rows : (step - low + 1) * rows, :])
                weight_buf[head, span(step), cols] = jnp.exp2(part).astype(jnp.bfloat16)

    def forward_products(head):
        for step in range(steps):
            product_buf[head, span(step), :] = mm(
                weight_buf[head, span(step), window(step)], value_buf[head, window(step), :]
            )

    def repeat(head, carry):
        for step in range(steps):
            extra = query_buf[head, span(step), HEAD_SIZE:].astype(jnp.float32)
            query_buf[head, span(step), HEAD_SIZE:] = jnp.where(lane == OFFSET_LANE, 0.0, extra).astype(
                jnp.bfloat16
            )
            highest = jnp.full((rows, 1), FORBIDDEN, jnp.float32)
            for tile in range(step, step + step_tiles):
                cols = slice(tile * SUB, (tile + 1) * SUB)
                part = mm(query_buf[head, span(step), :], key_buf[head, cols, :], BOTH_MINOR)
                part = limit(step, tile, part)
                highest = jnp.maximum(highest, jnp.max(part, axis=1, keepdims=True))
            query_buf[head, span(step), HEAD_SIZE:] = jnp.where(
                lane == OFFSET_LANE, -highest, extra
            ).astype(jnp.bfloat16)
        forward_scores(head)
        forward_products(head)
        return carry

    kept = {}

    def finish_forward(head):
        value_up = value_up_of(head)
        spreads = []
        inverses = []
        up_value = jnp.zeros((LANES, HEAD_SIZE), jnp.float32)
        for step in range(steps):
            gradient = jnp.concatenate(
                [gradient_in[own(step), group_cols(head, member)] for member in range(GROUPS)], axis=0
            )
            gradient_low = mm(gradient, value_up, BOTH_MINOR)
            inverse = 1.0 / product_buf[head, span(step), ones]
            low_part = (product_buf[head, span(step), HEAD_SIZE:] * inverse).astype(jnp.bfloat16)
            outputs = product_buf[head, span(step), :HEAD_SIZE] * inverse + mm(low_part, value_up)
            outputs = outputs.astype(jnp.bfloat16)
            for member in range(GROUPS):
                out_buf[own(step), group_cols(head, member)] = outputs[own(member), :]
            delta = jnp.sum(
                outputs.astype(jnp.float32) * gradient.astype(jnp.float32), axis=1, keepdims=True
            )
            delta_high = delta.astype(jnp.bfloat16).astype(jnp.float32)
            extra = jnp.where(lane == ONES_LANE, -delta_high, gradient_low)
            extra = jnp.where(lane == ONES_LANE + 1, delta_high - delta, extra)
            gradient_buf[head, span(step), :HEAD_SIZE] = gradient
            gradient_buf[head, span(step), HEAD_SIZE:] = extra.astype(jnp.bfloat16)
            up_value += mm(low_part, gradient, BOTH_MAJOR)
            spreads.append(jnp.transpose(gradient_low * inverse)[:RANK, :].astype(jnp.bfloat16))
            inverses.append(inverse * SCORE_SCALE)
        up_value_buf[:, head * HEAD_SIZE : (head + 1) * HEAD_SIZE] = up_value[:RANK, :].astype(
            jnp.bfloat16
        )
        at = pl.ds(head * GROUP_WIDTH, GROUP_WIDTH)
        hbm_at = pl.ds((start + head) * GROUP_WIDTH, GROUP_WIDTH)
        out_copies.append(copy(out_buf.at[:, at], out_hbm.at[:, hbm_at], head_sems.at[head, 2, 0]))
        out_copies[-1].start()
        kept[head] = jnp.concatenate(spreads, axis=1), inverses

    def backward_scores(head):
        spread = kept[head][0]
        for tile in range(tiles):
            low, high = tile_steps(tile)
            cols = slice(tile * SUB, (tile + 1) * SUB)
            part = slice(low * rows, high * rows)
            grad_weights = mm(gradient_buf[head, part, :], value_buf[head, cols, :], BOTH_MINOR)
            weights = weight_buf[head, part, cols]
            score_buf[head, part, cols] = weights * grad_weights.astype(jnp.bfloat16)
            value_back_ref[:, cols] += mm(spread[:, part], weights)

    def backward_products(head):
        query_grads = []
        for step in range(steps):
            cosines = cos_ref[own(step), :]
            sines = sin_ref[own(step), :]
            sums = mm(score_buf[head, span(step), window(step)], key_buf[head, window(step), :HEAD_SIZE])
            sums = sums * kept[head][1][step]
            turned = []
            for member in range(GROUPS):
                part = sums[own(member), :]
                turned.append(part * cosines - swap_halves(part) * sines)
            query_grads.append(jnp.concatenate(turned, axis=1).astype(jnp.bfloat16))
        query_grad = jnp.concatenate(query_grads, axis=0)
        up_query_buf[:, head * GROUP_WIDTH : (head + 1) * GROUP_WIDTH] = mm(
            query_low_t_ref[...], query_grad
        ).astype(jnp.bfloat16)
        query_back_ref[...] += mm(query_up_of(head), query_grad, BOTH_MINOR)

    def arrive(head, kind):
        for in_copy in in_copies[head][kind]:
            in_copy.wait()

    out_copies = []
    query_copy.wait()
    arrive(0, 0)
    prepare(0)
    for head in range(heads):
        forward_scores(head)
        if head + 1 < heads:
            arrive(head + 1, 0)
            prepare(head + 1)
        arrive(head, 1)
        forward_products(head)

    @pl.when(jnp.min(product_buf[:, :, ones]) < 1e-18)
    def _():
        lax.fori_loop(0, heads, repeat, 0)

    gradient_copy.wait()
    finish_forward(0)
    for head in range(heads):
        backward_scores(head)
        if head + 1 < heads:
            finish_forward(head + 1)
        backward_products(head)
    up_copies = (
        copy(
            up_query_buf,
            partial_hbm.at[:, pl.ds(start * GROUP_WIDTH, heads * GROUP_WIDTH)],
            sems.at[8],
        ),
        copy(
            up_value_buf,
            partial_hbm.at[:, pl.ds(up_columns + start * HEAD_SIZE, heads * HEAD_SIZE)],
            sems.at[9],
        ),
    )
    for up_copy in up_copies:
        up_copy.start()
    for done in (*extras, *out_copies, *up_copies):
        done.wait()


VMEM = pl.BlockSpec(memory_space=pltpu.VMEM)
SMEM = pl.BlockSpec(memory_space=pltpu.SMEM)
HBM = pl.BlockSpec(memory_space=pltpu.HBM)
NEAR = 4


def attention_chunk(
    first, last, columns, place, mask, query_base, gradient, received, shared, tables, carried
):
    count = last - first
    tokens = query_base.shape[0]
    keys = 3 * tokens
    rows = GROUPS * tokens
    out_specs = [HBM, HBM, VMEM, VMEM]
    out_shape = [
        jax.ShapeDtypeStruct(query_base.shape, jnp.bfloat16),
        jax.ShapeDtypeStruct((RANK, columns), jnp.bfloat16),
        jax.ShapeDtypeStruct((RANK, tokens), jnp.float32),
        jax.ShapeDtypeStruct((RANK, keys), jnp.float32),
    ]
    arguments = [place]
    in_specs = [SMEM]
    if carried is None:
        arguments.append(mask)
        in_specs.append(SMEM)
        out_specs += [HBM, HBM]
        out_shape += [jax.ShapeDtypeStruct((keys, LANES), jnp.bfloat16)] * 2
    arguments += [query_base, gradient, *received, *shared]
    in_specs += [HBM] * 6 + [VMEM] * len(shared)
    aliases = {}
    if carried is not None:
        arguments += [*tables, *carried]
        in_specs += [HBM, HBM, HBM, HBM, VMEM, VMEM]
        aliases = {len(arguments) - 4: 0, len(arguments) - 3: 1}
    wide_buf = HEAD_SIZE + LANES
    return pl.pallas_call(
        functools.partial(attention_kernel, carried is None, first, query_base.shape[1]),
        in_specs=in_specs,
        out_specs=out_specs,
        scratch_shapes=[
            pltpu.VMEM((tokens, count * GROUP_WIDTH), jnp.bfloat16),
            pltpu.VMEM((tokens, count * GROUP_WIDTH), jnp.bfloat16),
            pltpu.VMEM((tokens, count * GROUP_WIDTH), jnp.bfloat16),
            pltpu.VMEM((RANK, count * GROUP_WIDTH), jnp.bfloat16),
            pltpu.VMEM((RANK, count * HEAD_SIZE), jnp.bfloat16),
            pltpu.VMEM((3, RANK, tokens), jnp.bfloat16),
            pltpu.VMEM((count, keys, wide_buf), jnp.bfloat16),
            pltpu.VMEM((count, keys, wide_buf), jnp.bfloat16),
            pltpu.VMEM((count, rows, wide_buf), jnp.bfloat16),
            pltpu.VMEM((count, rows, wide_buf), jnp.bfloat16),
            pltpu.VMEM((count, rows, keys), jnp.bfloat16),
            pltpu.VMEM((count, rows, keys), jnp.bfloat16),
            pltpu.VMEM((count, rows, wide_buf), jnp.float32),
            pltpu.SemaphoreType.DMA((10,)),
            pltpu.SemaphoreType.DMA((count, 3, 4)),
        ],
        out_shape=out_shape,
        input_output_aliases=aliases,
        compiler_params=pltpu.CompilerParams(vmem_limit_bytes=50 * 2**20),
    )(*arguments)


def down_kernel(first_column, query_ref, value_ref, cross_ref, *refs):
    *arrived, hidden_ref, _, partial_hbm, down_buf, sems = refs
    tokens = query_ref.shape[1]
    features = hidden_ref.shape[1]
    query_back = query_ref[...] + cross_ref[:RANK, :]
    value_back = value_ref[:, 2 * tokens :] + cross_ref[RANK:, :]
    for part in arrived:
        value_back += part[...]
    back = jnp.concatenate([query_back, value_back], axis=0).astype(jnp.bfloat16)
    down_buf[...] = mm(back, hidden_ref[...]).astype(jnp.bfloat16)
    copies = [
        pltpu.make_async_copy(
            down_buf.at[pl.ds(at * RANK, RANK)],
            partial_hbm.at[:, pl.ds(first_column + at * features, features)],
            sems.at[at],
        )
        for at in range(2)
    ]
    for each in copies:
        each.start()
    for each in copies:
        each.wait()


def final_kernel(scale, place_ref, *refs):
    gathered = [ref[...].astype(jnp.float32) * scale for ref in refs[:NEAR]]
    query_up_ref, value_up_ref, query_down_ref, value_down_ref = refs[NEAR:]
    parts = []
    for at in range(NEAR):
        distance = (at % 2 * 2 + at // 2) ^ place_ref[0]
        part = gathered[0]
        for other in range(1, NEAR):
            part = jnp.where(distance == other, gathered[other], part)
        parts.append(part)
    total = jnp.concatenate(parts, axis=1)
    column = 0
    for ref in (query_up_ref, value_up_ref, query_down_ref, value_down_ref):
        ref[...] = total[:, column : column + ref.shape[1]]
        column += ref.shape[1]


def head_sum(x):
    if lax.axis_size("head") == 2:
        return x + lax.ppermute(x, "head", [(0, 1), (1, 0)])
    return lax.psum(x, "head")


def ctx_sum(x):
    devices = lax.axis_size("ctx")
    place = lax.axis_index("ctx") % NEAR

    def exchange(value, distance):
        return lax.ppermute(value, "ctx", [(i, i ^ distance) for i in range(devices)])

    def halve(value, bit, distance):
        half = value.shape[1] // 2
        kept = lax.dynamic_slice_in_dim(value, bit * half, half, 1)
        given = lax.dynamic_slice_in_dim(value, (1 - bit) * half, half, 1)
        return add(kept, exchange(given, distance))

    def add(one, other):
        return (one.astype(jnp.float32) + other.astype(jnp.float32)).astype(jnp.bfloat16)

    x = halve(x, place % 2, 1)
    x = halve(x, place // 2, 2)
    distance = NEAR
    while distance < devices:
        x = add(x, exchange(x, distance))
        distance *= 2
    return [x] + [exchange(x, distance) for distance in range(1, NEAR)]


def after(value, *others):
    return lax.optimization_barrier((value, *others))[0]


def per_device(
    hidden_states,
    query_base,
    key_base,
    frozen_value_rows,
    query_down,
    query_up,
    value_down,
    value_up_weight,
    positions,
    block_mask,
    output_gradient,
):
    tokens = hidden_states.shape[0]
    devices = lax.axis_size("ctx")
    device_index = lax.axis_index("ctx")
    kv_heads = key_base.shape[1] // HEAD_SIZE
    forward_one = [(i, i + 1) for i in range(devices - 1)]
    even_two = [(i, i + 2) for i in range(0, devices - 2, 2)]
    even_one = [(i, i + 1) for i in range(0, devices - 1, 2)]

    both_down = jnp.concatenate([query_down, value_down], axis=1)
    low = head_sum(mm(both_down, hidden_states, (((0,), (1,)), ((), ())))).astype(jnp.bfloat16)
    query_low_t = low[:RANK]
    value_low_t = low[RANK:]

    half = np.arange(HEAD_SIZE // 2, dtype=np.float64)
    frequency = (ROPE_BASE ** (-2.0 * half / HEAD_SIZE)).astype(np.float32)[:, None]

    def payload(chunk):
        first, last = chunk
        extra = RANK if first == 0 else 0
        return jax.ShapeDtypeStruct((tokens + extra, 2 * (last - first) * HEAD_SIZE), jnp.bfloat16)

    table = jax.ShapeDtypeStruct((tokens, HEAD_SIZE), jnp.float32)
    cosines, sines, packed_first = pl.pallas_call(
        functools.partial(prologue_kernel, CHUNKS[:1]),
        out_shape=[table, table, payload(CHUNKS[0])],
        compiler_params=pltpu.CompilerParams(vmem_limit_bytes=32 * 2**20),
    )(positions[None, :], jnp.asarray(frequency), key_base, frozen_value_rows)
    packed_first = lax.dynamic_update_slice(packed_first, value_low_t, (tokens, 0))
    packed_later = pl.pallas_call(
        functools.partial(later_prologue_kernel, CHUNKS[1:]),
        out_shape=[payload(chunk) for chunk in CHUNKS[1:]],
        compiler_params=pltpu.CompilerParams(vmem_limit_bytes=32 * 2**20),
    )(cosines, after(sines, packed_first), key_base, frozen_value_rows)
    packed = [packed_first, *packed_later]

    place = jnp.stack([device_index, device_index % 2]).astype(jnp.int32)
    shared = [query_up, value_up_weight, query_low_t.T, query_low_t, cosines, sines]

    ones, evens = [], []
    for chunk, own in enumerate(packed):
        if chunk > 1:
            own = after(own, ones[chunk - 1], evens[chunk - 2])
        ones.append(lax.ppermute(own, "ctx", forward_one))
        evens.append(lax.ppermute(own, "ctx", even_two))

    features = hidden_states.shape[1]
    query_columns = kv_heads * GROUP_WIDTH
    value_columns = kv_heads * HEAD_SIZE
    columns = query_columns + value_columns + 2 * features
    columns = -(-columns // (NEAR * LANES)) * NEAR * LANES
    carried = None
    tables = None
    for chunk, (first, last) in enumerate(CHUNKS):
        one = ones[chunk]
        one = after(one, evens[0] if carried is None else carried[3])
        odd = lax.ppermute(one, "ctx", even_one)
        *carried, = attention_chunk(
            first,
            last,
            columns,
            place,
            block_mask.T,
            query_base,
            output_gradient,
            [packed[chunk], one, evens[chunk], odd],
            shared,
            tables,
            carried,
        )
        if tables is None:
            tables = carried[4:]
            carried = carried[:4]
    attention_out, partial, query_back, value_back = carried

    def back_by(value, distance, cross):
        pairs = []
        for i in range(devices - distance):
            for j in range(2):
                pairs.append(((i + distance) * 2 + j, i * 2 + (1 - j if cross else j)))
        return lax.ppermute(value, ("ctx", "head"), pairs)

    back_one = value_back[:, tokens : 2 * tokens]
    back_two = value_back[:, :tokens]
    arrived = [
        back_by(value, distance, cross)
        for distance, value in ((2, back_two), (1, back_one))
        for cross in (True, False)
    ]
    cross = back_by(jnp.concatenate([query_back, value_back[:, 2 * tokens :]], axis=0), 0, True)
    arguments = [query_back, value_back, cross, *arrived, hidden_states, partial]
    partial = pl.pallas_call(
        functools.partial(down_kernel, query_columns + value_columns),
        in_specs=[VMEM] * (len(arguments) - 1) + [HBM],
        out_specs=HBM,
        out_shape=jax.ShapeDtypeStruct(partial.shape, partial.dtype),
        scratch_shapes=[
            pltpu.VMEM((2 * RANK, features), jnp.bfloat16),
            pltpu.SemaphoreType.DMA((2,)),
        ],
        input_output_aliases={len(arguments) - 1: 0},
        compiler_params=pltpu.CompilerParams(vmem_limit_bytes=32 * 2**20),
    )(*arguments)
    gathered = ctx_sum(partial)
    widths = (query_columns, value_columns, features, features)
    up_query, up_value, down_query, down_value = pl.pallas_call(
        functools.partial(final_kernel, float((devices * tokens) ** (-0.5))),
        in_specs=[SMEM] + [VMEM] * NEAR,
        out_specs=[VMEM] * 4,
        out_shape=[jax.ShapeDtypeStruct((RANK, width), jnp.float32) for width in widths],
    )((device_index % NEAR).astype(jnp.int32).reshape(1), *gathered)
    return attention_out, down_query.T, up_query, down_value.T, up_value


def solution(mesh):
    placed = (
        P("ctx", "head"),
        P("ctx", "head"),
        P("ctx", "head"),
        P("ctx", "head"),
        P("head", None),
        P(None, "head"),
        P("head", None),
        P(None, "head"),
        P("ctx"),
        P(),
        P("ctx", "head"),
    )
    return jax.shard_map(
        per_device,
        mesh=mesh,
        in_specs=placed,
        out_specs=(
            P("ctx", "head"),
            P("head", None),
            P(None, "head"),
            P("head", None),
            P(None, "head"),
        ),
        check_vma=False,
    )
```

```python
import functools

import jax
import jax.numpy as jnp
import numpy as np
from jax import lax
from jax.experimental import pallas as pl
from jax.experimental.pallas import tpu as pltpu
from jax.sharding import PartitionSpec as P

D = 5376
QUERY_HEADS = 32
KEY_VALUE_HEADS = 16
HEAD_SIZE = 128
WINDOW = 1024
BLOCK = 128
GROUPS = QUERY_HEADS // KEY_VALUE_HEADS
GROUP_WIDTH = GROUPS * HEAD_SIZE
SCORE_SCALE = (D // QUERY_HEADS) ** (-0.5)
LOG2_E = 1.4426950408889634
ROPE_BASE = 10000.0
FORBIDDEN = -1e30
RANK = 16

SUB = 256
KEYS = SUB + WINDOW
LANES = 128
OFFSET_LANE = 64
ONES_LANE = RANK

CHUNKS = ((0, 3), (3, 8))
GROUP = 3

ROWS_BY_COLS = (((1,), (0,)), ((), ()))
BOTH_MINOR = (((1,), (1,)), ((), ()))
BOTH_MAJOR = (((0,), (0,)), ((), ()))


def mm(left, right, dims=ROWS_BY_COLS):
    return lax.dot_general(left, right, dims, preferred_element_type=jnp.float32)


def swap_halves(x):
    return pltpu.roll(x, HEAD_SIZE // 2, 1)


def rotate_into(chunks, cosines, sines, key_ref, value_ref, outs):
    own = pl.ds(0, key_ref.shape[0])
    for (first, last), out_ref in zip(chunks, outs):
        count = last - first
        for head in range(first, last):
            cols = pl.ds(head * HEAD_SIZE, HEAD_SIZE)
            key = key_ref[:, cols].astype(jnp.float32)
            rotated = key * cosines + swap_halves(key) * sines
            out_ref[own, pl.ds((head - first) * HEAD_SIZE, HEAD_SIZE)] = rotated.astype(jnp.bfloat16)
            out_ref[own, pl.ds((count + head - first) * HEAD_SIZE, HEAD_SIZE)] = value_ref[:, cols]


def prologue_kernel(chunks, positions_ref, frequency_ref, key_ref, value_ref, cos_ref, sin_ref, *outs):
    half = HEAD_SIZE // 2
    angles = frequency_ref[...] * positions_ref[...].astype(jnp.float32)
    both = jnp.transpose(jnp.concatenate([jnp.cos(angles), jnp.sin(angles)], axis=0))
    turned = swap_halves(both)
    low_half = lax.broadcasted_iota(jnp.int32, both.shape, 1) < half
    cosines = jnp.where(low_half, both, turned)
    sines = jnp.where(low_half, -turned, both)
    cos_ref[...] = cosines
    sin_ref[...] = sines
    rotate_into(chunks, cosines, sines, key_ref, value_ref, outs)


def later_prologue_kernel(chunks, cos_ref, sin_ref, key_ref, value_ref, *outs):
    rotate_into(chunks, cos_ref[...], sin_ref[...], key_ref, value_ref, outs)


def attention_kernel(first, start, up_columns, place_ref, *refs):
    if first:
        mask_ref, *refs = refs
    (
        query_hbm,
        gradient_hbm,
        own_hbm,
        one_hbm,
        even_hbm,
        odd_hbm,
        query_up_ref,
        value_up_ref,
        query_low_ref,
        query_low_t_ref,
        cos_ref,
        sin_ref,
        *refs,
    ) = refs
    if first:
        low_far_ref, low_one_ref, low_own_ref, *refs = refs
    else:
        key_extra_hbm, value_extra_hbm, _, _, back_in, *refs = refs
    out_hbm, partial_hbm, back_ref, *refs = refs
    if first:
        key_extra_hbm, value_extra_hbm, *refs = refs
    (
        query_in,
        gradient_in,
        out_buf,
        up_query_buf,
        up_value_buf,
        key_buf,
        value_buf,
        query_buf,
        gradient_buf,
        weight_buf,
        score_buf,
        product_buf,
        sems,
        head_sems,
    ) = refs
    heads = key_buf.shape[0]
    tokens = query_in.shape[0]
    keys = key_buf.shape[1]
    steps = tokens // SUB
    tiles = keys // SUB
    step_tiles = KEYS // SUB
    rows = GROUPS * SUB
    odd = place_ref[1] == 1

    def copy(source, target, sem):
        return pltpu.make_async_copy(source, target, sem)

    def start_far(even_source, odd_source, target, sem):
        @pl.when(odd)
        def _():
            copy(odd_source, target, sem).start()

        @pl.when(jnp.logical_not(odd))
        def _():
            copy(even_source, target, sem).start()

        return copy(even_source, target, sem)

    own_rows = pl.ds(0, tokens)
    chunk_cols = pl.ds(start * GROUP_WIDTH, heads * GROUP_WIDTH)
    query_copy = copy(query_hbm.at[:, chunk_cols], query_in, sems.at[0])
    query_copy.start()
    in_copies = []
    for head in range(heads):
        in_copies.append([])
        for kind, buf, at in ((0, key_buf, head), (1, value_buf, heads + head)):
            cols = pl.ds(at * HEAD_SIZE, HEAD_SIZE)
            main = pl.ds(0, HEAD_SIZE)
            sem = head_sems.at[head, kind]
            copies = [
                start_far(
                    even_hbm.at[own_rows, cols],
                    odd_hbm.at[own_rows, cols],
                    buf.at[head, pl.ds(0, tokens), main],
                    sem.at[0],
                ),
                copy(one_hbm.at[own_rows, cols], buf.at[head, pl.ds(tokens, tokens), main], sem.at[1]),
                copy(own_hbm.at[own_rows, cols], buf.at[head, pl.ds(2 * tokens, tokens), main], sem.at[2]),
            ]
            if not first:
                extra_hbm = (key_extra_hbm, value_extra_hbm)[kind]
                copies.append(copy(extra_hbm, buf.at[head, :, pl.ds(HEAD_SIZE, LANES)], sem.at[3]))
            for later in copies[1:]:
                later.start()
            in_copies[head].append(copies)
    gradient_copy = copy(gradient_hbm.at[:, chunk_cols], gradient_in, sems.at[1])
    gradient_copy.start()

    if first:
        first_block = place_ref[0] * (tokens // BLOCK)
        reach = WINDOW // BLOCK
        block_lane = lax.broadcasted_iota(jnp.int32, (BLOCK, LANES), 1)
        for key_block in range(keys // BLOCK):
            extra = jnp.where(block_lane == OFFSET_LANE, 1.0, 0.0)
            exists = first_block + (key_block - reach) >= 0
            for block in range(tokens // BLOCK):
                offset = reach + block - key_block
                if 0 <= offset <= reach:
                    hit = (mask_ref[offset, first_block + block] == 1) & exists
                    term = jnp.where(hit, 0.0, FORBIDDEN)
                else:
                    term = FORBIDDEN
                extra = jnp.where(block_lane == block, term, extra)
            for head in range(heads):
                key_buf[head, key_block * BLOCK : (key_block + 1) * BLOCK, HEAD_SIZE:] = extra.astype(
                    jnp.bfloat16
                )
        low = jnp.concatenate([low_far_ref[...], low_one_ref[...], low_own_ref[...]], axis=1)
        low = jnp.concatenate(
            [
                low.astype(jnp.float32),
                jnp.ones((2, keys), jnp.float32),
                jnp.zeros((LANES - RANK - 2, keys), jnp.float32),
            ],
            axis=0,
        )
        low = jnp.transpose(low).astype(jnp.bfloat16)
        for head in range(heads):
            value_buf[head, :, HEAD_SIZE:] = low
        extras = (
            copy(key_buf.at[0, :, pl.ds(HEAD_SIZE, LANES)], key_extra_hbm, sems.at[6]),
            copy(value_buf.at[0, :, pl.ds(HEAD_SIZE, LANES)], value_extra_hbm, sems.at[7]),
        )
        for extra_copy in extras:
            extra_copy.start()
        back_ref[...] = jnp.zeros_like(back_ref)
    else:
        extras = ()
        back_ref[...] = back_in[...]

    lane = lax.broadcasted_iota(jnp.int32, (rows, LANES), 1)
    row = lax.broadcasted_iota(jnp.int32, (rows, LANES), 0) % SUB
    ones = slice(HEAD_SIZE + ONES_LANE, HEAD_SIZE + ONES_LANE + 1)

    def own(step):
        return slice(step * SUB, (step + 1) * SUB)

    def span(step):
        return slice(step * rows, (step + 1) * rows)

    def window(step):
        return slice(step * SUB, step * SUB + KEYS)

    def tile_steps(tile):
        return max(0, tile - step_tiles + 1), min(steps, tile + 1)

    def slot(head):
        return head % GROUP

    def group_cols(head, member):
        return slice((head * GROUPS + member) * HEAD_SIZE, (head * GROUPS + member + 1) * HEAD_SIZE)

    def query_up_of(head):
        at = (start + head) * GROUP_WIDTH
        return query_up_ref[:, at : at + GROUP_WIDTH]

    def value_up_of(head):
        at = (start + head) * HEAD_SIZE
        return jnp.concatenate(
            [value_up_ref[:, at : at + HEAD_SIZE], jnp.zeros((LANES - RANK, HEAD_SIZE), jnp.bfloat16)],
            axis=0,
        )

    def limit(step, tile, part):
        place = tile - step
        if 0 < place < step_tiles - 1:
            return part
        halves = []
        for block in range(SUB // BLOCK):
            inside = lane > row % BLOCK if place == 0 else lane <= row % BLOCK
            inside = inside | (row // BLOCK != block)
            halves.append(
                jnp.where(inside, part[:, block * BLOCK : (block + 1) * BLOCK], FORBIDDEN)
            )
        return jnp.concatenate(halves, axis=1)

    def prepare(head):
        reach_of_key = jnp.max(
            jnp.abs(key_buf[head, :, :HEAD_SIZE].astype(jnp.float32)), axis=0, keepdims=True
        )
        for step in range(steps):
            cosines = cos_ref[own(step), :]
            sines = sin_ref[own(step), :]
            adapted = mm(query_low_ref[own(step), :], query_up_of(head))
            turned = []
            for member in range(GROUPS):
                part = query_in[own(step), group_cols(head, member)].astype(jnp.float32)
                part = part + adapted[:, member * HEAD_SIZE : (member + 1) * HEAD_SIZE]
                turned.append(part * cosines + swap_halves(part) * sines)
            queries = jnp.concatenate(turned, axis=0) * (SCORE_SCALE * LOG2_E)
            bound = jnp.sum(jnp.abs(queries) * reach_of_key, axis=1, keepdims=True)
            chosen = (lane == row // BLOCK + step * (SUB // BLOCK)).astype(jnp.float32)
            query_buf[slot(head), span(step), :HEAD_SIZE] = queries.astype(jnp.bfloat16)
            query_buf[slot(head), span(step), HEAD_SIZE:] = jnp.where(
                lane == OFFSET_LANE, -bound, chosen
            ).astype(jnp.bfloat16)

    def forward_scores(head):
        for tile in range(tiles):
            low, high = tile_steps(tile)
            cols = slice(tile * SUB, (tile + 1) * SUB)
            scores = mm(
                query_buf[slot(head), low * rows : high * rows, :], key_buf[head, cols, :], BOTH_MINOR
            )
            for step in range(low, high):
                part = limit(step, tile, scores[(step - low) * rows : (step - low + 1) * rows, :])
                weight_buf[slot(head), span(step), cols] = jnp.exp2(part).astype(jnp.bfloat16)

    def forward_products(head):
        for step in range(steps):
            product_buf[slot(head), span(step), :] = mm(
                weight_buf[slot(head), span(step), window(step)], value_buf[head, window(step), :]
            )

    def repeat(head, carry):
        for step in range(steps):
            extra = query_buf[slot(head), span(step), HEAD_SIZE:].astype(jnp.float32)
            query_buf[slot(head), span(step), HEAD_SIZE:] = jnp.where(lane == OFFSET_LANE, 0.0, extra).astype(
                jnp.bfloat16
            )
            highest = jnp.full((rows, 1), FORBIDDEN, jnp.float32)
            for tile in range(step, step + step_tiles):
                cols = slice(tile * SUB, (tile + 1) * SUB)
                part = mm(query_buf[slot(head), span(step), :], key_buf[head, cols, :], BOTH_MINOR)
                part = limit(step, tile, part)
                highest = jnp.maximum(highest, jnp.max(part, axis=1, keepdims=True))
            query_buf[slot(head), span(step), HEAD_SIZE:] = jnp.where(
                lane == OFFSET_LANE, -highest, extra
            ).astype(jnp.bfloat16)
        forward_scores(head)
        forward_products(head)
        return carry

    kept = {}

    def finish_forward(head):
        value_up = value_up_of(head)
        spreads = []
        inverses = []
        up_value = jnp.zeros((LANES, HEAD_SIZE), jnp.float32)
        for step in range(steps):
            gradient = jnp.concatenate(
                [gradient_in[own(step), group_cols(head, member)] for member in range(GROUPS)], axis=0
            )
            gradient_low = mm(gradient, value_up, BOTH_MINOR)
            inverse = 1.0 / product_buf[slot(head), span(step), ones]
            low_part = (product_buf[slot(head), span(step), HEAD_SIZE:] * inverse).astype(jnp.bfloat16)
            outputs = product_buf[slot(head), span(step), :HEAD_SIZE] * inverse + mm(low_part, value_up)
            outputs = outputs.astype(jnp.bfloat16)
            for member in range(GROUPS):
                out_buf[own(step), group_cols(head, member)] = outputs[own(member), :]
            delta = jnp.sum(
                outputs.astype(jnp.float32) * gradient.astype(jnp.float32), axis=1, keepdims=True
            )
            delta_high = delta.astype(jnp.bfloat16).astype(jnp.float32)
            extra = jnp.where(lane == ONES_LANE, -delta_high, gradient_low)
            extra = jnp.where(lane == ONES_LANE + 1, delta_high - delta, extra)
            gradient_buf[slot(head), span(step), :HEAD_SIZE] = gradient
            gradient_buf[slot(head), span(step), HEAD_SIZE:] = extra.astype(jnp.bfloat16)
            up_value += mm(low_part, gradient, BOTH_MAJOR)
            spreads.append(jnp.transpose(gradient_low * inverse)[:RANK, :].astype(jnp.bfloat16))
            inverses.append(inverse * SCORE_SCALE)
        up_value_buf[:, head * HEAD_SIZE : (head + 1) * HEAD_SIZE] = up_value[:RANK, :].astype(
            jnp.bfloat16
        )
        at = pl.ds(head * GROUP_WIDTH, GROUP_WIDTH)
        hbm_at = pl.ds((start + head) * GROUP_WIDTH, GROUP_WIDTH)
        out_copies.append(copy(out_buf.at[:, at], out_hbm.at[:, hbm_at], head_sems.at[head, 2, 0]))
        out_copies[-1].start()
        kept[head] = jnp.concatenate(spreads, axis=1), inverses

    def backward_scores(head):
        spread = kept[head][0]
        for tile in range(tiles):
            low, high = tile_steps(tile)
            cols = slice(tile * SUB, (tile + 1) * SUB)
            back_row = RANK + tile * SUB // tokens * RANK
            back_rows = slice(back_row, back_row + RANK)
            back_cols = slice(tile * SUB % tokens, tile * SUB % tokens + SUB)
            part = slice(low * rows, high * rows)
            grad_weights = mm(gradient_buf[slot(head), part, :], value_buf[head, cols, :], BOTH_MINOR)
            weights = weight_buf[slot(head), part, cols]
            score_buf[slot(head), part, cols] = weights * grad_weights.astype(jnp.bfloat16)
            back_ref[back_rows, back_cols] += mm(spread[:, part], weights)

    def backward_products(head):
        query_grads = []
        for step in range(steps):
            cosines = cos_ref[own(step), :]
            sines = sin_ref[own(step), :]
            sums = mm(score_buf[slot(head), span(step), window(step)], key_buf[head, window(step), :HEAD_SIZE])
            sums = sums * kept[head][1][step]
            turned = []
            for member in range(GROUPS):
                part = sums[own(member), :]
                turned.append(part * cosines - swap_halves(part) * sines)
            query_grads.append(jnp.concatenate(turned, axis=1).astype(jnp.bfloat16))
        query_grad = jnp.concatenate(query_grads, axis=0)
        up_query_buf[:, head * GROUP_WIDTH : (head + 1) * GROUP_WIDTH] = mm(
            query_low_t_ref[...], query_grad
        ).astype(jnp.bfloat16)
        back_ref[:RANK, :] += mm(query_up_of(head), query_grad, BOTH_MINOR)

    def arrive(head, kind):
        for in_copy in in_copies[head][kind]:
            in_copy.wait()

    out_copies = []
    query_copy.wait()
    for group in range(0, heads, GROUP):
        members = range(group, min(heads, group + GROUP))
        arrive(group, 0)
        prepare(group)
        for head in members:
            forward_scores(head)
            if head + 1 in members:
                arrive(head + 1, 0)
                prepare(head + 1)
            arrive(head, 1)
            forward_products(head)

        @pl.when(jnp.min(product_buf[: len(members), :, ones]) < 1e-18)
        def _():
            lax.fori_loop(members.start, members.stop, repeat, 0)

        if group == 0:
            gradient_copy.wait()
        finish_forward(group)
        for head in members:
            backward_scores(head)
            if head + 1 in members:
                finish_forward(head + 1)
            backward_products(head)
    up_copies = (
        copy(
            up_query_buf,
            partial_hbm.at[:, pl.ds(start * GROUP_WIDTH, heads * GROUP_WIDTH)],
            sems.at[8],
        ),
        copy(
            up_value_buf,
            partial_hbm.at[:, pl.ds(up_columns + start * HEAD_SIZE, heads * HEAD_SIZE)],
            sems.at[9],
        ),
    )
    for up_copy in up_copies:
        up_copy.start()
    for done in (*extras, *out_copies, *up_copies):
        done.wait()


VMEM = pl.BlockSpec(memory_space=pltpu.VMEM)
SMEM = pl.BlockSpec(memory_space=pltpu.SMEM)
ANY = pl.BlockSpec(memory_space=pl.ANY)
NEAR = 4


def attention_chunk(
    first, last, columns, place, mask, query_base, gradient, received, shared, lows, tables, carried
):
    count = last - first
    tokens = query_base.shape[0]
    keys = 3 * tokens
    rows = GROUPS * tokens
    slots = min(count, GROUP)
    out_specs = [ANY, ANY, VMEM]
    out_shape = [
        jax.ShapeDtypeStruct(query_base.shape, jnp.bfloat16),
        jax.ShapeDtypeStruct((RANK, columns), jnp.bfloat16),
        jax.ShapeDtypeStruct((RANK + keys // tokens * RANK, tokens), jnp.float32),
    ]
    arguments = [place]
    in_specs = [SMEM]
    if carried is None:
        arguments.append(mask)
        in_specs.append(SMEM)
        out_specs += [ANY, ANY]
        out_shape += [jax.ShapeDtypeStruct((keys, LANES), jnp.bfloat16)] * 2
    arguments += [query_base, gradient, *received, *shared]
    in_specs += [ANY] * 6 + [VMEM] * len(shared)
    aliases = {}
    if carried is None:
        arguments += lows
        in_specs += [VMEM] * len(lows)
    else:
        arguments += [*tables, *carried]
        in_specs += [ANY, ANY, ANY, ANY, VMEM]
        aliases = {len(arguments) - 3: 0, len(arguments) - 2: 1}
    wide_buf = HEAD_SIZE + LANES
    return pl.pallas_call(
        functools.partial(attention_kernel, carried is None, first, query_base.shape[1]),
        in_specs=in_specs,
        out_specs=out_specs,
        scratch_shapes=[
            pltpu.VMEM((tokens, count * GROUP_WIDTH), jnp.bfloat16),
            pltpu.VMEM((tokens, count * GROUP_WIDTH), jnp.bfloat16),
            pltpu.VMEM((tokens, count * GROUP_WIDTH), jnp.bfloat16),
            pltpu.VMEM((RANK, count * GROUP_WIDTH), jnp.bfloat16),
            pltpu.VMEM((RANK, count * HEAD_SIZE), jnp.bfloat16),
            pltpu.VMEM((count, keys, wide_buf), jnp.bfloat16),
            pltpu.VMEM((count, keys, wide_buf), jnp.bfloat16),
            pltpu.VMEM((slots, rows, wide_buf), jnp.bfloat16),
            pltpu.VMEM((slots, rows, wide_buf), jnp.bfloat16),
            pltpu.VMEM((slots, rows, keys), jnp.bfloat16),
            pltpu.VMEM((slots, rows, keys), jnp.bfloat16),
            pltpu.VMEM((slots, rows, wide_buf), jnp.float32),
            pltpu.SemaphoreType.DMA((10,)),
            pltpu.SemaphoreType.DMA((count, 3, 4)),
        ],
        out_shape=out_shape,
        input_output_aliases=aliases,
        compiler_params=pltpu.CompilerParams(vmem_limit_bytes=50 * 2**20),
    )(*arguments)


def down_kernel(first_column, back_ref, one_ref, two_ref, hidden_ref, _, partial_hbm, down_buf, sems):
    features = hidden_ref.shape[1]
    value_back = back_ref[3 * RANK :, :] + one_ref[...] + two_ref[...]
    back = jnp.concatenate([back_ref[:RANK, :], value_back], axis=0).astype(jnp.bfloat16)
    down_buf[...] = mm(back, hidden_ref[...]).astype(jnp.bfloat16)
    copies = [
        pltpu.make_async_copy(
            down_buf.at[pl.ds(at * RANK, RANK)],
            partial_hbm.at[:, pl.ds(first_column + at * features, features)],
            sems.at[at],
        )
        for at in range(2)
    ]
    for each in copies:
        each.start()
    for each in copies:
        each.wait()


def final_kernel(scale, place_ref, *refs):
    gathered = [ref[...].astype(jnp.float32) * scale for ref in refs[:NEAR]]
    query_up_ref, value_up_ref, query_down_ref, value_down_ref = refs[NEAR:]
    parts = []
    for at in range(NEAR):
        distance = (at % 2 * 2 + at // 2) ^ place_ref[0]
        part = gathered[0]
        for other in range(1, NEAR):
            part = jnp.where(distance == other, gathered[other], part)
        parts.append(part)
    total = jnp.concatenate(parts, axis=1)
    column = 0
    for ref in (query_up_ref, value_up_ref, query_down_ref, value_down_ref):
        ref[...] = total[:, column : column + ref.shape[1]]
        column += ref.shape[1]


def head_sum(x):
    if lax.axis_size("head") == 2:
        return x + lax.ppermute(x, "head", [(0, 1), (1, 0)])
    return lax.psum(x, "head")


def ctx_sum(x):
    devices = lax.axis_size("ctx")
    place = lax.axis_index("ctx") % NEAR

    def exchange(value, distance):
        return lax.ppermute(value, "ctx", [(i, i ^ distance) for i in range(devices)])

    def halve(value, bit, distance):
        half = value.shape[1] // 2
        kept = lax.dynamic_slice_in_dim(value, bit * half, half, 1)
        given = lax.dynamic_slice_in_dim(value, (1 - bit) * half, half, 1)
        return add(kept, exchange(given, distance))

    def add(one, other):
        return (one.astype(jnp.float32) + other.astype(jnp.float32)).astype(jnp.bfloat16)

    x = halve(x, place % 2, 1)
    x = halve(x, place // 2, 2)
    distance = NEAR
    while distance < devices:
        x = add(x, exchange(x, distance))
        distance *= 2
    return [x] + [exchange(x, distance) for distance in range(1, NEAR)]


def after(value, *others):
    return lax.optimization_barrier((value, *others))[0]


def per_device(
    hidden_states,
    query_base,
    key_base,
    frozen_value_rows,
    query_down,
    query_up,
    value_down,
    value_up_weight,
    positions,
    block_mask,
    output_gradient,
):
    tokens = hidden_states.shape[0]
    devices = lax.axis_size("ctx")
    device_index = lax.axis_index("ctx")
    kv_heads = key_base.shape[1] // HEAD_SIZE
    forward_one = [(i, i + 1) for i in range(devices - 1)]
    even_two = [(i, i + 2) for i in range(0, devices - 2, 2)]
    even_one = [(i, i + 1) for i in range(0, devices - 1, 2)]

    both_down = jnp.concatenate([query_down, value_down], axis=1)
    low = head_sum(mm(both_down, hidden_states, (((0,), (1,)), ((), ())))).astype(jnp.bfloat16)
    query_low_t = low[:RANK]
    value_low_t = low[RANK:]

    half = np.arange(HEAD_SIZE // 2, dtype=np.float64)
    frequency = (ROPE_BASE ** (-2.0 * half / HEAD_SIZE)).astype(np.float32)[:, None]

    def payload(chunk):
        first, last = chunk
        return jax.ShapeDtypeStruct((tokens, 2 * (last - first) * HEAD_SIZE), jnp.bfloat16)

    table = jax.ShapeDtypeStruct((tokens, HEAD_SIZE), jnp.float32)
    cosines, sines, packed_first = pl.pallas_call(
        functools.partial(prologue_kernel, CHUNKS[:1]),
        out_shape=[table, table, payload(CHUNKS[0])],
        compiler_params=pltpu.CompilerParams(vmem_limit_bytes=32 * 2**20),
    )(positions[None, :], jnp.asarray(frequency), key_base, frozen_value_rows)
    lows = [
        lax.ppermute(value_low_t, "ctx", [(i, i + 2) for i in range(devices - 2)]),
        lax.ppermute(value_low_t, "ctx", forward_one),
        value_low_t,
    ]
    packed_later = pl.pallas_call(
        functools.partial(later_prologue_kernel, CHUNKS[1:]),
        out_shape=[payload(chunk) for chunk in CHUNKS[1:]],
        compiler_params=pltpu.CompilerParams(vmem_limit_bytes=32 * 2**20),
    )(cosines, after(sines, packed_first, *lows[:2]), key_base, frozen_value_rows)
    packed = [packed_first, *packed_later]

    place = jnp.stack([device_index, device_index % 2]).astype(jnp.int32)
    shared = [query_up, value_up_weight, query_low_t.T, query_low_t, cosines, sines]

    ones, evens = [], []
    for chunk, own in enumerate(packed):
        if chunk > 1:
            own = after(own, ones[chunk - 1], evens[chunk - 2])
        ones.append(lax.ppermute(own, "ctx", forward_one))
        evens.append(lax.ppermute(own, "ctx", even_two))

    features = hidden_states.shape[1]
    query_columns = kv_heads * GROUP_WIDTH
    value_columns = kv_heads * HEAD_SIZE
    columns = query_columns + value_columns + 2 * features
    columns = -(-columns // (NEAR * LANES)) * NEAR * LANES
    carried = None
    tables = None
    for chunk, (first, last) in enumerate(CHUNKS):
        one = ones[chunk]
        one = after(one, evens[0] if carried is None else carried[2])
        odd = lax.ppermute(one, "ctx", even_one)
        *carried, = attention_chunk(
            first,
            last,
            columns,
            place,
            block_mask.T,
            query_base,
            output_gradient,
            [packed[chunk], one, evens[chunk], odd],
            shared,
            lows,
            tables,
            carried,
        )
        if tables is None:
            tables = carried[3:]
            carried = carried[:3]
    attention_out, partial, back = carried

    back = head_sum(back)
    back_one = lax.ppermute(
        back[2 * RANK : 3 * RANK], "ctx", [(i + 1, i) for i in range(devices - 1)]
    )
    back_two = lax.ppermute(back[RANK : 2 * RANK], "ctx", [(i + 2, i) for i in range(devices - 2)])
    arguments = [back, back_one, back_two, hidden_states, partial]
    partial = pl.pallas_call(
        functools.partial(down_kernel, query_columns + value_columns),
        in_specs=[VMEM] * (len(arguments) - 1) + [ANY],
        out_specs=ANY,
        out_shape=jax.ShapeDtypeStruct(partial.shape, partial.dtype),
        scratch_shapes=[
            pltpu.VMEM((2 * RANK, features), jnp.bfloat16),
            pltpu.SemaphoreType.DMA((2,)),
        ],
        input_output_aliases={len(arguments) - 1: 0},
        compiler_params=pltpu.CompilerParams(vmem_limit_bytes=32 * 2**20),
    )(*arguments)
    gathered = ctx_sum(partial)
    widths = (query_columns, value_columns, features, features)
    up_query, up_value, down_query, down_value = pl.pallas_call(
        functools.partial(final_kernel, float((devices * tokens) ** (-0.5))),
        in_specs=[SMEM] + [VMEM] * NEAR,
        out_specs=[VMEM] * 4,
        out_shape=[jax.ShapeDtypeStruct((RANK, width), jnp.float32) for width in widths],
    )((device_index % NEAR).astype(jnp.int32).reshape(1), *gathered)
    return attention_out, down_query.T, up_query, down_value.T, up_value


def solution(mesh):
    placed = (
        P("ctx", "head"),
        P("ctx", "head"),
        P("ctx", "head"),
        P("ctx", "head"),
        P("head", None),
        P(None, "head"),
        P("head", None),
        P(None, "head"),
        P("ctx"),
        P(),
        P("ctx", "head"),
    )
    return jax.shard_map(
        per_device,
        mesh=mesh,
        in_specs=placed,
        out_specs=(
            P("ctx", "head"),
            P("head", None),
            P(None, "head"),
            P("head", None),
            P(None, "head"),
        ),
        check_vma=False,
    )
```

```python
import functools

import jax
import jax.numpy as jnp
import numpy as np
from jax import lax
from jax.experimental import pallas as pl
from jax.experimental.pallas import tpu as pltpu
from jax.sharding import PartitionSpec as P

D = 5376
QUERY_HEADS = 32
KEY_VALUE_HEADS = 16
HEAD_SIZE = 128
WINDOW = 1024
BLOCK = 128
GROUPS = QUERY_HEADS // KEY_VALUE_HEADS
GROUP_WIDTH = GROUPS * HEAD_SIZE
SCORE_SCALE = (D // QUERY_HEADS) ** (-0.5)
LOG2_E = 1.4426950408889634
ROPE_BASE = 10000.0
FORBIDDEN = -1e30
RANK = 16

SUB = 256
KEYS = SUB + WINDOW
LANES = 128
OFFSET_LANE = 64
ONES_LANE = RANK

CHUNKS = ((0, 2), (2, 6), (6, 8))
TOGETHER = (2, 2, 1)

ROWS_BY_COLS = (((1,), (0,)), ((), ()))
BOTH_MINOR = (((1,), (1,)), ((), ()))
BOTH_MAJOR = (((0,), (0,)), ((), ()))


def mm(left, right, dims=ROWS_BY_COLS):
    return lax.dot_general(left, right, dims, preferred_element_type=jnp.float32)


def swap_halves(x):
    return pltpu.roll(x, HEAD_SIZE // 2, 1)


def rotate_into(chunks, cosines, sines, key_ref, value_ref, outs):
    own = pl.ds(0, key_ref.shape[0])
    for (first, last), out_ref in zip(chunks, outs):
        count = last - first
        for head in range(first, last):
            cols = pl.ds(head * HEAD_SIZE, HEAD_SIZE)
            key = key_ref[:, cols].astype(jnp.float32)
            rotated = key * cosines + swap_halves(key) * sines
            out_ref[own, pl.ds((head - first) * HEAD_SIZE, HEAD_SIZE)] = rotated.astype(jnp.bfloat16)
            out_ref[own, pl.ds((count + head - first) * HEAD_SIZE, HEAD_SIZE)] = value_ref[:, cols]


def prologue_kernel(chunks, positions_ref, frequency_ref, key_ref, value_ref, cos_ref, sin_ref, *outs):
    half = HEAD_SIZE // 2
    angles = frequency_ref[...] * positions_ref[...].astype(jnp.float32)
    both = jnp.transpose(jnp.concatenate([jnp.cos(angles), jnp.sin(angles)], axis=0))
    turned = swap_halves(both)
    low_half = lax.broadcasted_iota(jnp.int32, both.shape, 1) < half
    cosines = jnp.where(low_half, both, turned)
    sines = jnp.where(low_half, -turned, both)
    cos_ref[...] = cosines
    sin_ref[...] = sines
    rotate_into(chunks, cosines, sines, key_ref, value_ref, outs)


def later_prologue_kernel(chunks, cos_ref, sin_ref, key_ref, value_ref, *outs):
    rotate_into(chunks, cos_ref[...], sin_ref[...], key_ref, value_ref, outs)


def attention_kernel(first, start, up_columns, place_ref, *refs):
    if first:
        mask_ref, *refs = refs
    (
        query_hbm,
        gradient_hbm,
        own_hbm,
        one_hbm,
        even_hbm,
        odd_hbm,
        query_up_ref,
        value_up_ref,
        query_low_ref,
        query_low_t_ref,
        cos_ref,
        sin_ref,
        *refs,
    ) = refs
    if not first:
        key_extra_hbm, value_extra_hbm, _, _, back_in, *refs = refs
    out_hbm, partial_hbm, back_ref, *refs = refs
    if first:
        key_extra_hbm, value_extra_hbm, *refs = refs
    (
        query_in,
        gradient_in,
        out_buf,
        up_query_buf,
        up_value_buf,
        low_buf,
        key_buf,
        value_buf,
        query_buf,
        gradient_buf,
        weight_buf,
        score_buf,
        product_buf,
        sems,
        head_sems,
    ) = refs
    heads = key_buf.shape[0]
    together = query_buf.shape[0]
    tokens = query_in.shape[1]
    keys = key_buf.shape[1]
    steps = tokens // SUB
    tiles = keys // SUB
    step_tiles = KEYS // SUB
    rows = GROUPS * SUB
    odd = place_ref[1] == 1

    def copy(source, target, sem):
        return pltpu.make_async_copy(source, target, sem)

    def start_far(even_source, odd_source, target, sem):
        @pl.when(odd)
        def _():
            copy(odd_source, target, sem).start()

        @pl.when(jnp.logical_not(odd))
        def _():
            copy(even_source, target, sem).start()

        return copy(even_source, target, sem)

    own_rows = pl.ds(0, tokens)
    low_copies = []
    if first:
        last = pl.ds(tokens, RANK)
        low_copies.append(start_far(even_hbm.at[last], odd_hbm.at[last], low_buf.at[0], sems.at[3]))
        for at, source in ((1, one_hbm), (2, own_hbm)):
            low_copies.append(copy(source.at[last], low_buf.at[at], sems.at[3 + at]))
            low_copies[-1].start()
    def wide_copy(hbm, buf, head, kind, out=False):
        cols = pl.ds(pl.multiple_of((start + head) * GROUP_WIDTH, GROUP_WIDTH), GROUP_WIDTH)
        ends = (buf.at[head], hbm.at[:, cols]) if out else (hbm.at[:, cols], buf.at[head])
        return copy(*ends, head_sems.at[head, 2, kind])

    for head in range(heads):
        wide_copy(query_hbm, query_in, head, 0).start()
        for kind, buf, at in ((0, key_buf, head), (1, value_buf, heads + head)):
            cols = pl.ds(at * HEAD_SIZE, HEAD_SIZE)
            main = pl.ds(0, HEAD_SIZE)
            sem = head_sems.at[head, kind]
            copies = [
                start_far(
                    even_hbm.at[own_rows, cols],
                    odd_hbm.at[own_rows, cols],
                    buf.at[head, pl.ds(0, tokens), main],
                    sem.at[0],
                ),
                copy(one_hbm.at[own_rows, cols], buf.at[head, pl.ds(tokens, tokens), main], sem.at[1]),
                copy(own_hbm.at[own_rows, cols], buf.at[head, pl.ds(2 * tokens, tokens), main], sem.at[2]),
            ]
            if not first:
                extra_hbm = (key_extra_hbm, value_extra_hbm)[kind]
                copies.append(copy(extra_hbm, buf.at[head, :, pl.ds(HEAD_SIZE, LANES)], sem.at[3]))
            for later in copies[1:]:
                later.start()
        wide_copy(gradient_hbm, gradient_in, head, 1).start()

    if first:
        first_block = place_ref[0] * (tokens // BLOCK)
        reach = WINDOW // BLOCK
        block_lane = lax.broadcasted_iota(jnp.int32, (BLOCK, LANES), 1)
        for key_block in range(keys // BLOCK):
            extra = jnp.where(block_lane == OFFSET_LANE, 1.0, 0.0)
            exists = first_block + (key_block - reach) >= 0
            for block in range(tokens // BLOCK):
                offset = reach + block - key_block
                if 0 <= offset <= reach:
                    hit = (mask_ref[offset, first_block + block] == 1) & exists
                    term = jnp.where(hit, 0.0, FORBIDDEN)
                else:
                    term = FORBIDDEN
                extra = jnp.where(block_lane == block, term, extra)
            for head in range(heads):
                key_buf[head, key_block * BLOCK : (key_block + 1) * BLOCK, HEAD_SIZE:] = extra.astype(
                    jnp.bfloat16
                )
        for low_copy in low_copies:
            low_copy.wait()
        low = jnp.concatenate([low_buf[at] for at in range(3)], axis=1)
        low = jnp.concatenate(
            [
                low.astype(jnp.float32),
                jnp.ones((2, keys), jnp.float32),
                jnp.zeros((LANES - RANK - 2, keys), jnp.float32),
            ],
            axis=0,
        )
        low = jnp.transpose(low).astype(jnp.bfloat16)
        for head in range(heads):
            value_buf[head, :, HEAD_SIZE:] = low
        extras = (
            copy(key_buf.at[0, :, pl.ds(HEAD_SIZE, LANES)], key_extra_hbm, sems.at[6]),
            copy(value_buf.at[0, :, pl.ds(HEAD_SIZE, LANES)], value_extra_hbm, sems.at[7]),
        )
        for extra_copy in extras:
            extra_copy.start()
        back_ref[...] = jnp.zeros_like(back_ref)
    else:
        extras = ()
        back_ref[...] = back_in[...]

    lane = lax.broadcasted_iota(jnp.int32, (rows, LANES), 1)
    row = lax.broadcasted_iota(jnp.int32, (rows, LANES), 0) % SUB
    ones = slice(HEAD_SIZE + ONES_LANE, HEAD_SIZE + ONES_LANE + 1)

    def own(step):
        return slice(step * SUB, (step + 1) * SUB)

    def span(step):
        return slice(step * rows, (step + 1) * rows)

    def window(step):
        return slice(step * SUB, step * SUB + KEYS)

    def tile_steps(tile):
        return max(0, tile - step_tiles + 1), min(steps, tile + 1)

    def member_cols(member):
        return slice(member * HEAD_SIZE, (member + 1) * HEAD_SIZE)

    def value_up_of(head):
        return jnp.concatenate(
            [value_up_ref[start + head], jnp.zeros((LANES - RANK, HEAD_SIZE), jnp.bfloat16)], axis=0
        )

    def limit(step, tile, part):
        place = tile - step
        if 0 < place < step_tiles - 1:
            return part
        halves = []
        for block in range(SUB // BLOCK):
            inside = lane > row % BLOCK if place == 0 else lane <= row % BLOCK
            inside = inside | (row // BLOCK != block)
            halves.append(
                jnp.where(inside, part[:, block * BLOCK : (block + 1) * BLOCK], FORBIDDEN)
            )
        return jnp.concatenate(halves, axis=1)

    def prepare(head, slot):
        reach_of_key = jnp.max(
            jnp.abs(key_buf[head, :, :HEAD_SIZE].astype(jnp.float32)), axis=0, keepdims=True
        )
        for step in range(steps):
            cosines = cos_ref[own(step), :]
            sines = sin_ref[own(step), :]
            adapted = mm(query_low_ref[own(step), :], query_up_ref[start + head])
            turned = []
            for member in range(GROUPS):
                part = query_in[head, own(step), member_cols(member)].astype(jnp.float32)
                part = part + adapted[:, member * HEAD_SIZE : (member + 1) * HEAD_SIZE]
                turned.append(part * cosines + swap_halves(part) * sines)
            queries = jnp.concatenate(turned, axis=0) * (SCORE_SCALE * LOG2_E)
            bound = jnp.sum(jnp.abs(queries) * reach_of_key, axis=1, keepdims=True)
            chosen = (lane == row // BLOCK + step * (SUB // BLOCK)).astype(jnp.float32)
            query_buf[slot, span(step), :HEAD_SIZE] = queries.astype(jnp.bfloat16)
            query_buf[slot, span(step), HEAD_SIZE:] = jnp.where(
                lane == OFFSET_LANE, -bound, chosen
            ).astype(jnp.bfloat16)

    def forward_scores(head, slot):
        for tile in range(tiles):
            low, high = tile_steps(tile)
            cols = slice(tile * SUB, (tile + 1) * SUB)
            scores = mm(
                query_buf[slot, low * rows : high * rows, :], key_buf[head, cols, :], BOTH_MINOR
            )
            for step in range(low, high):
                part = limit(step, tile, scores[(step - low) * rows : (step - low + 1) * rows, :])
                weight_buf[slot, span(step), cols] = jnp.exp2(part).astype(jnp.bfloat16)

    def forward_products(head, slot):
        for step in range(steps):
            product_buf[slot, span(step), :] = mm(
                weight_buf[slot, span(step), window(step)], value_buf[head, window(step), :]
            )

    def repeat(head, slot):
        diagonal = lane - row % BLOCK

        def one_step(step, carry):
            here = pl.ds(pl.multiple_of(step * rows, rows), rows)

            def scores_of(tile):
                cols = pl.ds(pl.multiple_of((step + tile) * SUB, SUB), SUB)
                part = mm(query_buf[slot, here, :], key_buf[head, cols, :], BOTH_MINOR)
                lowest = jnp.where(tile == 0, 1, -BLOCK)
                highest = jnp.where(tile == step_tiles - 1, 0, BLOCK)
                halves = []
                for block in range(SUB // BLOCK):
                    inside = (diagonal >= lowest) & (diagonal <= highest)
                    inside = inside | (row // BLOCK != block)
                    halves.append(
                        jnp.where(inside, part[:, block * BLOCK : (block + 1) * BLOCK], FORBIDDEN)
                    )
                return jnp.concatenate(halves, axis=1), cols

            def top(tile, highest):
                part, _ = scores_of(tile)
                return jnp.maximum(highest, jnp.max(part, axis=1, keepdims=True))

            def again(tile, sums):
                part, cols = scores_of(tile)
                weights = jnp.exp2(part).astype(jnp.bfloat16)
                weight_buf[slot, here, cols] = weights
                return sums + mm(weights, value_buf[head, cols, :])

            extra = query_buf[slot, here, HEAD_SIZE:].astype(jnp.float32)
            query_buf[slot, here, HEAD_SIZE:] = jnp.where(lane == OFFSET_LANE, 0.0, extra).astype(
                jnp.bfloat16
            )
            highest = lax.fori_loop(
                0, step_tiles, top, jnp.full((rows, 1), FORBIDDEN, jnp.float32)
            )
            query_buf[slot, here, HEAD_SIZE:] = jnp.where(lane == OFFSET_LANE, -highest, extra).astype(
                jnp.bfloat16
            )
            product_buf[slot, here, :] = lax.fori_loop(
                0, step_tiles, again, jnp.zeros((rows, HEAD_SIZE + LANES), jnp.float32)
            )
            return carry

        lax.fori_loop(0, steps, one_step, 0)

    kept = {}

    def finish_forward(head, slot):
        value_up = value_up_of(head)
        spreads = []
        inverses = []
        up_value = jnp.zeros((LANES, HEAD_SIZE), jnp.float32)
        for step in range(steps):
            gradient = jnp.concatenate(
                [gradient_in[head, own(step), member_cols(member)] for member in range(GROUPS)], axis=0
            )
            gradient_low = mm(gradient, value_up, BOTH_MINOR)
            inverse = 1.0 / product_buf[slot, span(step), ones]
            low_part = (product_buf[slot, span(step), HEAD_SIZE:] * inverse).astype(jnp.bfloat16)
            outputs = product_buf[slot, span(step), :HEAD_SIZE] * inverse + mm(low_part, value_up)
            outputs = outputs.astype(jnp.bfloat16)
            for member in range(GROUPS):
                out_buf[head, own(step), member_cols(member)] = outputs[own(member), :]
            delta = jnp.sum(
                outputs.astype(jnp.float32) * gradient.astype(jnp.float32), axis=1, keepdims=True
            )
            delta_high = delta.astype(jnp.bfloat16).astype(jnp.float32)
            extra = jnp.where(lane == ONES_LANE, -delta_high, gradient_low)
            extra = jnp.where(lane == ONES_LANE + 1, delta_high - delta, extra)
            gradient_buf[slot, span(step), :HEAD_SIZE] = gradient
            gradient_buf[slot, span(step), HEAD_SIZE:] = extra.astype(jnp.bfloat16)
            up_value += mm(low_part, gradient, BOTH_MAJOR)
            spreads.append(jnp.transpose(gradient_low * inverse)[:RANK, :].astype(jnp.bfloat16))
            inverses.append(inverse * SCORE_SCALE)
        up_value_buf[head] = up_value[:RANK, :].astype(jnp.bfloat16)
        wide_copy(out_hbm, out_buf, head, 2, out=True).start()
        kept[slot] = jnp.concatenate(spreads, axis=1), inverses

    def backward_scores(head, slot):
        spread = kept[slot][0]
        for tile in range(tiles):
            low, high = tile_steps(tile)
            cols = slice(tile * SUB, (tile + 1) * SUB)
            back_row = RANK + tile * SUB // tokens * RANK
            back_rows = slice(back_row, back_row + RANK)
            back_cols = slice(tile * SUB % tokens, tile * SUB % tokens + SUB)
            part = slice(low * rows, high * rows)
            grad_weights = mm(gradient_buf[slot, part, :], value_buf[head, cols, :], BOTH_MINOR)
            weights = weight_buf[slot, part, cols]
            score_buf[slot, part, cols] = weights * grad_weights.astype(jnp.bfloat16)
            back_ref[back_rows, back_cols] += mm(spread[:, part], weights)

    def backward_products(head, slot):
        query_grads = []
        for step in range(steps):
            cosines = cos_ref[own(step), :]
            sines = sin_ref[own(step), :]
            sums = mm(score_buf[slot, span(step), window(step)], key_buf[head, window(step), :HEAD_SIZE])
            sums = sums * kept[slot][1][step]
            turned = []
            for member in range(GROUPS):
                part = sums[own(member), :]
                turned.append(part * cosines - swap_halves(part) * sines)
            query_grads.append(jnp.concatenate(turned, axis=1).astype(jnp.bfloat16))
        query_grad = jnp.concatenate(query_grads, axis=0)
        up_query_buf[head] = mm(query_low_t_ref[...], query_grad).astype(jnp.bfloat16)
        back_ref[:RANK, :] += mm(query_up_ref[start + head], query_grad, BOTH_MINOR)

    def arrive(head, kind):
        buf = (key_buf, value_buf)[kind]
        main = pl.ds(0, HEAD_SIZE)
        source = one_hbm.at[own_rows, main]
        for part in range(3):
            copy(
                source, buf.at[head, pl.ds(part * tokens, tokens), main], head_sems.at[head, kind, part]
            ).wait()
        if not first:
            extra_hbm = (key_extra_hbm, value_extra_hbm)[kind]
            copy(
                extra_hbm, buf.at[head, :, pl.ds(HEAD_SIZE, LANES)], head_sems.at[head, kind, 3]
            ).wait()

    def arrive_and_prepare(head, slot):
        arrive(head, 0)
        wide_copy(query_hbm, query_in, head, 0).wait()
        prepare(head, slot)

    def work(group, carry):
        members = [(group * together + slot, slot) for slot in range(together)]
        arrive_and_prepare(*members[0])
        for head, slot in members:
            forward_scores(head, slot)
            if slot + 1 < together:
                arrive_and_prepare(*members[slot + 1])
            arrive(head, 1)
            forward_products(head, slot)

        @pl.when(jnp.min(product_buf[:, :, ones]) < 1e-18)
        def _():
            lax.fori_loop(0, together, lambda slot, c: (repeat(group * together + slot, slot), c)[1], 0)

        for head, slot in members:
            wide_copy(gradient_hbm, gradient_in, head, 1).wait()
        finish_forward(*members[0])
        for head, slot in members:
            backward_scores(head, slot)
            if slot + 1 < together:
                finish_forward(*members[slot + 1])
            backward_products(head, slot)
        return carry

    if heads == together:
        work(0, 0)
    else:
        lax.fori_loop(0, heads // together, work, 0)
    up_copies = []
    for head in range(heads):
        at = pl.ds((start + head) * GROUP_WIDTH, GROUP_WIDTH)
        up_copies.append(copy(up_query_buf.at[head], partial_hbm.at[:, at], head_sems.at[head, 3, 0]))
        at = pl.ds(up_columns + (start + head) * HEAD_SIZE, HEAD_SIZE)
        up_copies.append(copy(up_value_buf.at[head], partial_hbm.at[:, at], head_sems.at[head, 3, 1]))
    for up_copy in up_copies:
        up_copy.start()
    for head in range(heads):
        wide_copy(out_hbm, out_buf, head, 2, out=True).wait()
    for done in (*extras, *up_copies):
        done.wait()


VMEM = pl.BlockSpec(memory_space=pltpu.VMEM)
SMEM = pl.BlockSpec(memory_space=pltpu.SMEM)
ANY = pl.BlockSpec(memory_space=pl.ANY)
NEAR = 4


def attention_chunk(
    first, last, together, columns, place, mask, query_base, gradient, received, shared, tables, carried
):
    count = last - first
    tokens = query_base.shape[0]
    keys = 3 * tokens
    rows = GROUPS * tokens
    out_specs = [ANY, ANY, VMEM]
    out_shape = [
        jax.ShapeDtypeStruct(query_base.shape, jnp.bfloat16),
        jax.ShapeDtypeStruct((RANK, columns), jnp.bfloat16),
        jax.ShapeDtypeStruct((RANK + keys // tokens * RANK, tokens), jnp.float32),
    ]
    arguments = [place]
    in_specs = [SMEM]
    if carried is None:
        arguments.append(mask)
        in_specs.append(SMEM)
        out_specs += [ANY, ANY]
        out_shape += [jax.ShapeDtypeStruct((keys, LANES), jnp.bfloat16)] * 2
    arguments += [query_base, gradient, *received, *shared]
    in_specs += [ANY] * 6 + [VMEM] * len(shared)
    aliases = {}
    if carried is not None:
        arguments += [*tables, *carried]
        in_specs += [ANY, ANY, ANY, ANY, VMEM]
        aliases = {len(arguments) - 3: 0, len(arguments) - 2: 1}
    wide_buf = HEAD_SIZE + LANES
    return pl.pallas_call(
        functools.partial(attention_kernel, carried is None, first, query_base.shape[1]),
        in_specs=in_specs,
        out_specs=out_specs,
        scratch_shapes=[
            pltpu.VMEM((count, tokens, GROUP_WIDTH), jnp.bfloat16),
            pltpu.VMEM((count, tokens, GROUP_WIDTH), jnp.bfloat16),
            pltpu.VMEM((count, tokens, GROUP_WIDTH), jnp.bfloat16),
            pltpu.VMEM((count, RANK, GROUP_WIDTH), jnp.bfloat16),
            pltpu.VMEM((count, RANK, HEAD_SIZE), jnp.bfloat16),
            pltpu.VMEM((3, RANK, tokens), jnp.bfloat16),
            pltpu.VMEM((count, keys, wide_buf), jnp.bfloat16),
            pltpu.VMEM((count, keys, wide_buf), jnp.bfloat16),
            pltpu.VMEM((together, rows, wide_buf), jnp.bfloat16),
            pltpu.VMEM((together, rows, wide_buf), jnp.bfloat16),
            pltpu.VMEM((together, rows, keys), jnp.bfloat16),
            pltpu.VMEM((together, rows, keys), jnp.bfloat16),
            pltpu.VMEM((together, rows, wide_buf), jnp.float32),
            pltpu.SemaphoreType.DMA((10,)),
            pltpu.SemaphoreType.DMA((count, 4, 4)),
        ],
        out_shape=out_shape,
        input_output_aliases=aliases,
        compiler_params=pltpu.CompilerParams(vmem_limit_bytes=50 * 2**20),
    )(*arguments)


def down_kernel(first_column, back_ref, one_ref, two_ref, hidden_ref, _, partial_hbm, down_buf, sems):
    features = hidden_ref.shape[1]
    value_back = back_ref[3 * RANK :, :].astype(jnp.float32)
    value_back = value_back + one_ref[...].astype(jnp.float32) + two_ref[...].astype(jnp.float32)
    back = jnp.concatenate([back_ref[:RANK, :], value_back.astype(jnp.bfloat16)], axis=0)
    down_buf[...] = mm(back, hidden_ref[...]).astype(jnp.bfloat16)
    copies = [
        pltpu.make_async_copy(
            down_buf.at[pl.ds(at * RANK, RANK)],
            partial_hbm.at[:, pl.ds(first_column + at * features, features)],
            sems.at[at],
        )
        for at in range(2)
    ]
    for each in copies:
        each.start()
    for each in copies:
        each.wait()


def final_kernel(scale, place_ref, *refs):
    gathered = [ref[...].astype(jnp.float32) * scale for ref in refs[:NEAR]]
    query_up_ref, value_up_ref, query_down_ref, value_down_ref = refs[NEAR:]
    parts = []
    for at in range(NEAR):
        distance = (at % 2 * 2 + at // 2) ^ place_ref[0]
        part = gathered[0]
        for other in range(1, NEAR):
            part = jnp.where(distance == other, gathered[other], part)
        parts.append(part)
    total = jnp.concatenate(parts, axis=1)
    column = 0
    for ref in (query_up_ref, value_up_ref, query_down_ref, value_down_ref):
        ref[...] = total[:, column : column + ref.shape[1]]
        column += ref.shape[1]


def head_sum(x):
    if lax.axis_size("head") == 2:
        other = lax.ppermute(x, "head", [(0, 1), (1, 0)])
        return (x.astype(jnp.float32) + other.astype(jnp.float32)).astype(x.dtype)
    return lax.psum(x, "head")


def ctx_sum(x):
    devices = lax.axis_size("ctx")
    place = lax.axis_index("ctx") % NEAR

    def exchange(value, distance):
        return lax.ppermute(value, "ctx", [(i, i ^ distance) for i in range(devices)])

    def halve(value, bit, distance):
        half = value.shape[1] // 2
        kept = lax.dynamic_slice_in_dim(value, bit * half, half, 1)
        given = lax.dynamic_slice_in_dim(value, (1 - bit) * half, half, 1)
        return add(kept, exchange(given, distance))

    def add(one, other):
        return (one.astype(jnp.float32) + other.astype(jnp.float32)).astype(jnp.bfloat16)

    x = halve(x, place % 2, 1)
    x = halve(x, place // 2, 2)
    distance = NEAR
    while distance < devices:
        x = add(x, exchange(x, distance))
        distance *= 2
    return [x] + [exchange(x, distance) for distance in range(1, NEAR)]


def after(value, *others):
    return lax.optimization_barrier((value, *others))[0]


def per_device(
    hidden_states,
    query_base,
    key_base,
    frozen_value_rows,
    query_down,
    query_up,
    value_down,
    value_up_weight,
    positions,
    block_mask,
    output_gradient,
):
    tokens = hidden_states.shape[0]
    devices = lax.axis_size("ctx")
    device_index = lax.axis_index("ctx")
    kv_heads = key_base.shape[1] // HEAD_SIZE
    forward_one = [(i, i + 1) for i in range(devices - 1)]
    even_two = [(i, i + 2) for i in range(0, devices - 2, 2)]
    even_one = [(i, i + 1) for i in range(0, devices - 1, 2)]

    both_down = jnp.concatenate([query_down, value_down], axis=1)
    low = head_sum(mm(both_down, hidden_states, (((0,), (1,)), ((), ())))).astype(jnp.bfloat16)
    query_low_t = low[:RANK]
    value_low_t = low[RANK:]

    half = np.arange(HEAD_SIZE // 2, dtype=np.float64)
    frequency = (ROPE_BASE ** (-2.0 * half / HEAD_SIZE)).astype(np.float32)[:, None]

    def payload(chunk):
        first, last = chunk
        extra = RANK if first == 0 else 0
        return jax.ShapeDtypeStruct((tokens + extra, 2 * (last - first) * HEAD_SIZE), jnp.bfloat16)

    table = jax.ShapeDtypeStruct((tokens, HEAD_SIZE), jnp.float32)
    cosines, sines, packed_first = pl.pallas_call(
        functools.partial(prologue_kernel, CHUNKS[:1]),
        out_shape=[table, table, payload(CHUNKS[0])],
        compiler_params=pltpu.CompilerParams(vmem_limit_bytes=32 * 2**20),
    )(positions[None, :], jnp.asarray(frequency), key_base, frozen_value_rows)
    packed_first = lax.dynamic_update_slice(packed_first, value_low_t, (tokens, 0))
    packed_later = pl.pallas_call(
        functools.partial(later_prologue_kernel, CHUNKS[1:]),
        out_shape=[payload(chunk) for chunk in CHUNKS[1:]],
        compiler_params=pltpu.CompilerParams(vmem_limit_bytes=32 * 2**20),
    )(cosines, after(sines, packed_first), key_base, frozen_value_rows)
    packed = [packed_first, *packed_later]

    place = jnp.stack([device_index, device_index % 2]).astype(jnp.int32)
    query_ups = query_up.reshape(RANK, kv_heads, GROUP_WIDTH).transpose(1, 0, 2)
    value_ups = value_up_weight.reshape(RANK, kv_heads, HEAD_SIZE).transpose(1, 0, 2)
    shared = [query_ups, value_ups, query_low_t.T, query_low_t, cosines, sines]

    ones, evens = [], []
    for chunk, own in enumerate(packed):
        if chunk > 1:
            own = after(own, ones[chunk - 1], evens[chunk - 2])
        ones.append(lax.ppermute(own, "ctx", forward_one))
        evens.append(lax.ppermute(own, "ctx", even_two))

    features = hidden_states.shape[1]
    query_columns = kv_heads * GROUP_WIDTH
    value_columns = kv_heads * HEAD_SIZE
    columns = query_columns + value_columns + 2 * features
    columns = -(-columns // (NEAR * LANES)) * NEAR * LANES
    carried = None
    tables = None
    for chunk, (first, last) in enumerate(CHUNKS):
        one = ones[chunk]
        one = after(one, evens[0] if carried is None else carried[2])
        odd = lax.ppermute(one, "ctx", even_one)
        *carried, = attention_chunk(
            first,
            last,
            TOGETHER[chunk],
            columns,
            place,
            block_mask.T,
            query_base,
            output_gradient,
            [packed[chunk], one, evens[chunk], odd],
            shared,
            tables,
            carried,
        )
        if tables is None:
            tables = carried[3:]
            carried = carried[:3]
    attention_out, partial, back = carried

    back = head_sum(back.astype(jnp.bfloat16))
    back_one = lax.ppermute(
        back[2 * RANK : 3 * RANK], "ctx", [(i + 1, i) for i in range(devices - 1)]
    )
    back_two = lax.ppermute(back[RANK : 2 * RANK], "ctx", [(i + 2, i) for i in range(devices - 2)])
    arguments = [back, back_one, back_two, hidden_states, partial]
    partial = pl.pallas_call(
        functools.partial(down_kernel, query_columns + value_columns),
        in_specs=[VMEM] * (len(arguments) - 1) + [ANY],
        out_specs=ANY,
        out_shape=jax.ShapeDtypeStruct(partial.shape, partial.dtype),
        scratch_shapes=[
            pltpu.VMEM((2 * RANK, features), jnp.bfloat16),
            pltpu.SemaphoreType.DMA((2,)),
        ],
        input_output_aliases={len(arguments) - 1: 0},
        compiler_params=pltpu.CompilerParams(vmem_limit_bytes=32 * 2**20),
    )(*arguments)
    gathered = ctx_sum(partial)
    widths = (query_columns, value_columns, features, features)
    up_query, up_value, down_query, down_value = pl.pallas_call(
        functools.partial(final_kernel, float((devices * tokens) ** (-0.5))),
        in_specs=[SMEM] + [VMEM] * NEAR,
        out_specs=[VMEM] * 4,
        out_shape=[jax.ShapeDtypeStruct((RANK, width), jnp.float32) for width in widths],
    )((device_index % NEAR).astype(jnp.int32).reshape(1), *gathered)
    return attention_out, down_query.T, up_query, down_value.T, up_value


def solution(mesh):
    placed = (
        P("ctx", "head"),
        P("ctx", "head"),
        P("ctx", "head"),
        P("ctx", "head"),
        P("head", None),
        P(None, "head"),
        P("head", None),
        P(None, "head"),
        P("ctx"),
        P(),
        P("ctx", "head"),
    )
    return jax.shard_map(
        per_device,
        mesh=mesh,
        in_specs=placed,
        out_specs=(
            P("ctx", "head"),
            P("head", None),
            P(None, "head"),
            P("head", None),
            P(None, "head"),
        ),
        check_vma=False,
    )
```

```python
import functools

import jax
import jax.numpy as jnp
import numpy as np
from jax import lax
from jax.experimental import pallas as pl
from jax.experimental.pallas import tpu as pltpu
from jax.sharding import PartitionSpec as P

D = 5376
QUERY_HEADS = 32
KEY_VALUE_HEADS = 16
HEAD_SIZE = 128
WINDOW = 1024
BLOCK = 128
GROUPS = QUERY_HEADS // KEY_VALUE_HEADS
GROUP_WIDTH = GROUPS * HEAD_SIZE
SCORE_SCALE = (D // QUERY_HEADS) ** (-0.5)
LOG2_E = 1.4426950408889634
ROPE_BASE = 10000.0
FORBIDDEN = -1e30
RANK = 16

SUB = 256
KEYS = SUB + WINDOW
LANES = 128
OFFSET_LANE = 64
ONES_LANE = RANK

CHUNKS = ((0, 2), (2, 6), (6, 8))
TOGETHER = (2, 2, 1)

ROWS_BY_COLS = (((1,), (0,)), ((), ()))
BOTH_MINOR = (((1,), (1,)), ((), ()))
BOTH_MAJOR = (((0,), (0,)), ((), ()))


def mm(left, right, dims=ROWS_BY_COLS):
    return lax.dot_general(left, right, dims, preferred_element_type=jnp.float32)


def swap_halves(x):
    return pltpu.roll(x, HEAD_SIZE // 2, 1)


def rotate_into(chunks, cosines, sines, key_ref, value_ref, outs):
    for (first, last), out_ref in zip(chunks, outs):
        count = last - first
        own = pl.ds(0, key_ref.shape[0])

        def one_head(head, carry, first=first, count=count, out_ref=out_ref, own=own):
            def cols(at):
                return pl.ds(pl.multiple_of(at * HEAD_SIZE, HEAD_SIZE), HEAD_SIZE)

            key = key_ref[:, cols(first + head)].astype(jnp.float32)
            rotated = key * cosines + swap_halves(key) * sines
            out_ref[own, cols(head)] = rotated.astype(jnp.bfloat16)
            out_ref[own, cols(count + head)] = value_ref[:, cols(first + head)]
            return carry

        lax.fori_loop(0, count, one_head, 0)


def prologue_kernel(chunks, positions_ref, frequency_ref, key_ref, value_ref, cos_ref, sin_ref, *outs):
    half = HEAD_SIZE // 2
    angles = frequency_ref[...] * positions_ref[...].astype(jnp.float32)
    both = jnp.transpose(jnp.concatenate([jnp.cos(angles), jnp.sin(angles)], axis=0))
    turned = swap_halves(both)
    low_half = lax.broadcasted_iota(jnp.int32, both.shape, 1) < half
    cosines = jnp.where(low_half, both, turned)
    sines = jnp.where(low_half, -turned, both)
    cos_ref[...] = cosines
    sin_ref[...] = sines
    rotate_into(chunks, cosines, sines, key_ref, value_ref, outs)


def later_prologue_kernel(chunks, mask_ref, cos_ref, sin_ref, key_ref, value_ref, extra_ref, *outs):
    rotate_into(chunks, cos_ref[...], sin_ref[...], key_ref, value_ref, outs)
    tokens = key_ref.shape[0]
    first_block = lax.axis_index("ctx") * (tokens // BLOCK)
    reach = WINDOW // BLOCK
    lane = lax.broadcasted_iota(jnp.int32, (BLOCK, LANES), 1)
    for key_block in range(extra_ref.shape[0] // BLOCK):
        extra = jnp.where(lane == OFFSET_LANE, 1.0, 0.0)
        exists = first_block + (key_block - reach) >= 0
        for block in range(tokens // BLOCK):
            offset = reach + block - key_block
            if 0 <= offset <= reach:
                hit = (mask_ref[offset, first_block + block] == 1) & exists
                term = jnp.where(hit, 0.0, FORBIDDEN)
            else:
                term = FORBIDDEN
            extra = jnp.where(lane == block, term, extra)
        extra_ref[key_block * BLOCK : (key_block + 1) * BLOCK, :] = extra.astype(jnp.bfloat16)


def attention_kernel(first, start, up_columns, *refs):
    (
        query_hbm,
        gradient_hbm,
        own_hbm,
        one_hbm,
        even_hbm,
        odd_hbm,
        query_up_ref,
        value_up_ref,
        query_low_t_ref,
        cos_ref,
        sin_ref,
        key_extra_hbm,
        *refs,
    ) = refs
    if not first:
        value_extra_hbm, _, _, back_in, *refs = refs
    out_hbm, partial_hbm, back_ref, *refs = refs
    if first:
        value_extra_hbm, *refs = refs
    (
        query_in,
        gradient_in,
        out_buf,
        up_query_buf,
        up_value_buf,
        low_buf,
        key_buf,
        value_buf,
        query_buf,
        gradient_buf,
        weight_buf,
        score_buf,
        product_buf,
        sems,
        head_sems,
    ) = refs
    heads = key_buf.shape[0]
    together = query_buf.shape[0]
    tokens = query_in.shape[1]
    keys = key_buf.shape[1]
    steps = tokens // SUB
    tiles = keys // SUB
    step_tiles = KEYS // SUB
    rows = GROUPS * SUB
    odd = lax.axis_index("ctx") % 2 == 1

    def copy(source, target, sem):
        return pltpu.make_async_copy(source, target, sem)

    def start_far(even_source, odd_source, target, sem):
        @pl.when(odd)
        def _():
            copy(odd_source, target, sem).start()

        @pl.when(jnp.logical_not(odd))
        def _():
            copy(even_source, target, sem).start()

        return copy(even_source, target, sem)

    own_rows = pl.ds(0, tokens)
    low_copies = []
    if first:
        last = pl.ds(tokens, RANK)
        low_copies.append(start_far(even_hbm.at[last], odd_hbm.at[last], low_buf.at[0], sems.at[3]))
        for at, source in ((1, one_hbm), (2, own_hbm)):
            low_copies.append(copy(source.at[last], low_buf.at[at], sems.at[3 + at]))
            low_copies[-1].start()
    def wide_copy(hbm, buf, head, kind, out=False):
        cols = pl.ds(pl.multiple_of((start + head) * GROUP_WIDTH, GROUP_WIDTH), GROUP_WIDTH)
        ends = (buf.at[head], hbm.at[:, cols]) if out else (hbm.at[:, cols], buf.at[head])
        return copy(*ends, head_sems.at[head, 2, kind])

    for head in range(heads):
        wide_copy(query_hbm, query_in, head, 0).start()
        for kind, buf, at in ((0, key_buf, head), (1, value_buf, heads + head)):
            cols = pl.ds(at * HEAD_SIZE, HEAD_SIZE)
            main = pl.ds(0, HEAD_SIZE)
            sem = head_sems.at[head, kind]
            copies = [
                start_far(
                    even_hbm.at[own_rows, cols],
                    odd_hbm.at[own_rows, cols],
                    buf.at[head, pl.ds(0, tokens), main],
                    sem.at[0],
                ),
                copy(one_hbm.at[own_rows, cols], buf.at[head, pl.ds(tokens, tokens), main], sem.at[1]),
                copy(own_hbm.at[own_rows, cols], buf.at[head, pl.ds(2 * tokens, tokens), main], sem.at[2]),
            ]
            if kind == 0 or not first:
                extra_hbm = (key_extra_hbm, value_extra_hbm)[kind]
                copies.append(copy(extra_hbm, buf.at[head, :, pl.ds(HEAD_SIZE, LANES)], sem.at[3]))
            for later in copies[1:]:
                later.start()
        wide_copy(gradient_hbm, gradient_in, head, 1).start()

    if first:
        for low_copy in low_copies:
            low_copy.wait()
        low = jnp.concatenate([low_buf[at] for at in range(3)], axis=1)
        low = jnp.concatenate(
            [
                low.astype(jnp.float32),
                jnp.ones((2, keys), jnp.float32),
                jnp.zeros((LANES - RANK - 2, keys), jnp.float32),
            ],
            axis=0,
        )
        low = jnp.transpose(low).astype(jnp.bfloat16)
        for head in range(heads):
            value_buf[head, :, HEAD_SIZE:] = low
        extras = (copy(value_buf.at[0, :, pl.ds(HEAD_SIZE, LANES)], value_extra_hbm, sems.at[7]),)
        for extra_copy in extras:
            extra_copy.start()
        back_ref[...] = jnp.zeros_like(back_ref)
    else:
        extras = ()
        back_ref[...] = back_in[...]

    lane = lax.broadcasted_iota(jnp.int32, (rows, LANES), 1)
    row = lax.broadcasted_iota(jnp.int32, (rows, LANES), 0) % SUB
    ones = slice(HEAD_SIZE + ONES_LANE, HEAD_SIZE + ONES_LANE + 1)

    def own(step):
        return slice(step * SUB, (step + 1) * SUB)

    def span(step):
        return slice(step * rows, (step + 1) * rows)

    def window(step):
        return slice(step * SUB, step * SUB + KEYS)

    def tile_steps(tile):
        return max(0, tile - step_tiles + 1), min(steps, tile + 1)

    def member_cols(member):
        return slice(member * HEAD_SIZE, (member + 1) * HEAD_SIZE)

    def value_up_of(head):
        return jnp.concatenate(
            [value_up_ref[start + head], jnp.zeros((LANES - RANK, HEAD_SIZE), jnp.bfloat16)], axis=0
        )

    def limit(step, tile, part):
        place = tile - step
        if 0 < place < step_tiles - 1:
            return part
        halves = []
        for block in range(SUB // BLOCK):
            inside = lane > row % BLOCK if place == 0 else lane <= row % BLOCK
            inside = inside | (row // BLOCK != block)
            halves.append(
                jnp.where(inside, part[:, block * BLOCK : (block + 1) * BLOCK], FORBIDDEN)
            )
        return jnp.concatenate(halves, axis=1)

    def prepare(head, slot):
        reach_of_key = jnp.max(
            jnp.abs(key_buf[head, :, :HEAD_SIZE].astype(jnp.float32)), axis=0, keepdims=True
        )
        for step in range(steps):
            cosines = cos_ref[own(step), :]
            sines = sin_ref[own(step), :]
            adapted = mm(query_low_t_ref[:, own(step)], query_up_ref[start + head], BOTH_MAJOR)
            turned = []
            for member in range(GROUPS):
                part = query_in[head, own(step), member_cols(member)].astype(jnp.float32)
                part = part + adapted[:, member * HEAD_SIZE : (member + 1) * HEAD_SIZE]
                turned.append(part * cosines + swap_halves(part) * sines)
            queries = jnp.concatenate(turned, axis=0) * (SCORE_SCALE * LOG2_E)
            bound = jnp.sum(jnp.abs(queries) * reach_of_key, axis=1, keepdims=True)
            chosen = (lane == row // BLOCK + step * (SUB // BLOCK)).astype(jnp.float32)
            query_buf[slot, span(step), :HEAD_SIZE] = queries.astype(jnp.bfloat16)
            query_buf[slot, span(step), HEAD_SIZE:] = jnp.where(
                lane == OFFSET_LANE, -bound, chosen
            ).astype(jnp.bfloat16)

    def forward_scores(head, slot):
        for tile in range(tiles):
            low, high = tile_steps(tile)
            cols = slice(tile * SUB, (tile + 1) * SUB)
            scores = mm(
                query_buf[slot, low * rows : high * rows, :], key_buf[head, cols, :], BOTH_MINOR
            )
            for step in range(low, high):
                part = limit(step, tile, scores[(step - low) * rows : (step - low + 1) * rows, :])
                weight_buf[slot, span(step), cols] = jnp.exp2(part).astype(jnp.bfloat16)

    def forward_products(head, slot):
        for step in range(steps):
            product_buf[slot, span(step), :] = mm(
                weight_buf[slot, span(step), window(step)], value_buf[head, window(step), :]
            )

    def repeat(head, slot):
        diagonal = lane - row % BLOCK

        def one_step(step, carry):
            here = pl.ds(pl.multiple_of(step * rows, rows), rows)

            def scores_of(tile):
                cols = pl.ds(pl.multiple_of((step + tile) * SUB, SUB), SUB)
                part = mm(query_buf[slot, here, :], key_buf[head, cols, :], BOTH_MINOR)
                lowest = jnp.where(tile == 0, 1, -BLOCK)
                highest = jnp.where(tile == step_tiles - 1, 0, BLOCK)
                halves = []
                for block in range(SUB // BLOCK):
                    inside = (diagonal >= lowest) & (diagonal <= highest)
                    inside = inside | (row // BLOCK != block)
                    halves.append(
                        jnp.where(inside, part[:, block * BLOCK : (block + 1) * BLOCK], FORBIDDEN)
                    )
                return jnp.concatenate(halves, axis=1), cols

            def top(tile, highest):
                part, _ = scores_of(tile)
                return jnp.maximum(highest, jnp.max(part, axis=1, keepdims=True))

            def again(tile, sums):
                part, cols = scores_of(tile)
                weights = jnp.exp2(part).astype(jnp.bfloat16)
                weight_buf[slot, here, cols] = weights
                return sums + mm(weights, value_buf[head, cols, :])

            extra = query_buf[slot, here, HEAD_SIZE:].astype(jnp.float32)
            query_buf[slot, here, HEAD_SIZE:] = jnp.where(lane == OFFSET_LANE, 0.0, extra).astype(
                jnp.bfloat16
            )
            highest = lax.fori_loop(
                0, step_tiles, top, jnp.full((rows, 1), FORBIDDEN, jnp.float32)
            )
            query_buf[slot, here, HEAD_SIZE:] = jnp.where(lane == OFFSET_LANE, -highest, extra).astype(
                jnp.bfloat16
            )
            product_buf[slot, here, :] = lax.fori_loop(
                0, step_tiles, again, jnp.zeros((rows, HEAD_SIZE + LANES), jnp.float32)
            )
            return carry

        lax.fori_loop(0, steps, one_step, 0)

    kept = {}

    def finish_forward(head, slot):
        value_up = value_up_of(head)
        spreads = []
        inverses = []
        up_value = jnp.zeros((LANES, HEAD_SIZE), jnp.float32)
        for step in range(steps):
            gradient = jnp.concatenate(
                [gradient_in[head, own(step), member_cols(member)] for member in range(GROUPS)], axis=0
            )
            gradient_low = mm(gradient, value_up, BOTH_MINOR)
            inverse = 1.0 / product_buf[slot, span(step), ones]
            low_part = (product_buf[slot, span(step), HEAD_SIZE:] * inverse).astype(jnp.bfloat16)
            outputs = product_buf[slot, span(step), :HEAD_SIZE] * inverse + mm(low_part, value_up)
            outputs = outputs.astype(jnp.bfloat16)
            for member in range(GROUPS):
                out_buf[head, own(step), member_cols(member)] = outputs[own(member), :]
            delta = jnp.sum(
                outputs.astype(jnp.float32) * gradient.astype(jnp.float32), axis=1, keepdims=True
            )
            delta_high = delta.astype(jnp.bfloat16).astype(jnp.float32)
            extra = jnp.where(lane == ONES_LANE, -delta_high, gradient_low)
            extra = jnp.where(lane == ONES_LANE + 1, delta_high - delta, extra)
            gradient_buf[slot, span(step), :HEAD_SIZE] = gradient
            gradient_buf[slot, span(step), HEAD_SIZE:] = extra.astype(jnp.bfloat16)
            up_value += mm(low_part, gradient, BOTH_MAJOR)
            spreads.append(jnp.transpose(gradient_low * inverse)[:RANK, :].astype(jnp.bfloat16))
            inverses.append(inverse * SCORE_SCALE)
        up_value_buf[head] = up_value[:RANK, :].astype(jnp.bfloat16)
        wide_copy(out_hbm, out_buf, head, 2, out=True).start()
        kept[slot] = jnp.concatenate(spreads, axis=1), inverses

    def backward_scores(head, slot):
        spread = kept[slot][0]
        for tile in range(tiles):
            low, high = tile_steps(tile)
            cols = slice(tile * SUB, (tile + 1) * SUB)
            back_row = RANK + tile * SUB // tokens * RANK
            back_rows = slice(back_row, back_row + RANK)
            back_cols = slice(tile * SUB % tokens, tile * SUB % tokens + SUB)
            part = slice(low * rows, high * rows)
            grad_weights = mm(gradient_buf[slot, part, :], value_buf[head, cols, :], BOTH_MINOR)
            weights = weight_buf[slot, part, cols]
            score_buf[slot, part, cols] = weights * grad_weights.astype(jnp.bfloat16)
            back_ref[back_rows, back_cols] += mm(spread[:, part], weights)

    def backward_products(head, slot):
        query_grads = []
        for step in range(steps):
            cosines = cos_ref[own(step), :]
            sines = sin_ref[own(step), :]
            sums = mm(score_buf[slot, span(step), window(step)], key_buf[head, window(step), :HEAD_SIZE])
            sums = sums * kept[slot][1][step]
            turned = []
            for member in range(GROUPS):
                part = sums[own(member), :]
                turned.append(part * cosines - swap_halves(part) * sines)
            query_grads.append(jnp.concatenate(turned, axis=1).astype(jnp.bfloat16))
        query_grad = jnp.concatenate(query_grads, axis=0)
        up_query_buf[head] = mm(query_low_t_ref[...], query_grad).astype(jnp.bfloat16)
        back_ref[:RANK, :] += mm(query_up_ref[start + head], query_grad, BOTH_MINOR)

    def arrive(head, kind):
        buf = (key_buf, value_buf)[kind]
        main = pl.ds(0, HEAD_SIZE)
        source = one_hbm.at[own_rows, main]
        for part in range(3):
            copy(
                source, buf.at[head, pl.ds(part * tokens, tokens), main], head_sems.at[head, kind, part]
            ).wait()
        if kind == 0 or not first:
            extra_hbm = (key_extra_hbm, value_extra_hbm)[kind]
            copy(
                extra_hbm, buf.at[head, :, pl.ds(HEAD_SIZE, LANES)], head_sems.at[head, kind, 3]
            ).wait()

    def arrive_and_prepare(head, slot):
        arrive(head, 0)
        wide_copy(query_hbm, query_in, head, 0).wait()
        prepare(head, slot)

    def work(group, carry):
        members = [(group * together + slot, slot) for slot in range(together)]
        arrive_and_prepare(*members[0])
        for head, slot in members:
            forward_scores(head, slot)
            if slot + 1 < together:
                arrive_and_prepare(*members[slot + 1])
            arrive(head, 1)
            forward_products(head, slot)

        @pl.when(jnp.min(product_buf[:, :, ones]) < 1e-18)
        def _():
            lax.fori_loop(0, together, lambda slot, c: (repeat(group * together + slot, slot), c)[1], 0)

        for head, slot in members:
            wide_copy(gradient_hbm, gradient_in, head, 1).wait()
        finish_forward(*members[0])
        for head, slot in members:
            backward_scores(head, slot)
            if slot + 1 < together:
                finish_forward(*members[slot + 1])
            backward_products(head, slot)
        return carry

    if heads == together:
        work(0, 0)
    else:
        lax.fori_loop(0, heads // together, work, 0)
    up_copies = []
    for head in range(heads):
        at = pl.ds((start + head) * GROUP_WIDTH, GROUP_WIDTH)
        up_copies.append(copy(up_query_buf.at[head], partial_hbm.at[:, at], head_sems.at[head, 3, 0]))
        at = pl.ds(up_columns + (start + head) * HEAD_SIZE, HEAD_SIZE)
        up_copies.append(copy(up_value_buf.at[head], partial_hbm.at[:, at], head_sems.at[head, 3, 1]))
    for up_copy in up_copies:
        up_copy.start()
    for head in range(heads):
        wide_copy(out_hbm, out_buf, head, 2, out=True).wait()
    for done in (*extras, *up_copies):
        done.wait()


VMEM = pl.BlockSpec(memory_space=pltpu.VMEM)
SMEM = pl.BlockSpec(memory_space=pltpu.SMEM)
ANY = pl.BlockSpec(memory_space=pl.ANY)
NEAR = 4


def attention_chunk(
    first, last, together, columns, query_base, gradient, received, shared, tables, carried
):
    count = last - first
    tokens = query_base.shape[0]
    keys = 3 * tokens
    rows = GROUPS * tokens
    out_specs = [ANY, ANY, VMEM]
    out_shape = [
        jax.ShapeDtypeStruct(query_base.shape, jnp.bfloat16),
        jax.ShapeDtypeStruct((RANK, columns), jnp.bfloat16),
        jax.ShapeDtypeStruct((RANK + keys // tokens * RANK, tokens), jnp.float32),
    ]
    if carried is None:
        out_specs.append(ANY)
        out_shape.append(jax.ShapeDtypeStruct((keys, LANES), jnp.bfloat16))
    arguments = [query_base, gradient, *received, *shared, *tables]
    in_specs = [ANY] * 6 + [VMEM] * len(shared) + [ANY] * len(tables)
    aliases = {}
    if carried is not None:
        arguments += carried
        in_specs += [ANY, ANY, VMEM]
        aliases = {len(arguments) - 3: 0, len(arguments) - 2: 1}
    wide_buf = HEAD_SIZE + LANES
    return pl.pallas_call(
        functools.partial(attention_kernel, carried is None, first, query_base.shape[1]),
        in_specs=in_specs,
        out_specs=out_specs,
        scratch_shapes=[
            pltpu.VMEM((count, tokens, GROUP_WIDTH), jnp.bfloat16),
            pltpu.VMEM((count, tokens, GROUP_WIDTH), jnp.bfloat16),
            pltpu.VMEM((count, tokens, GROUP_WIDTH), jnp.bfloat16),
            pltpu.VMEM((count, RANK, GROUP_WIDTH), jnp.bfloat16),
            pltpu.VMEM((count, RANK, HEAD_SIZE), jnp.bfloat16),
            pltpu.VMEM((3, RANK, tokens), jnp.bfloat16),
            pltpu.VMEM((count, keys, wide_buf), jnp.bfloat16),
            pltpu.VMEM((count, keys, wide_buf), jnp.bfloat16),
            pltpu.VMEM((together, rows, wide_buf), jnp.bfloat16),
            pltpu.VMEM((together, rows, wide_buf), jnp.bfloat16),
            pltpu.VMEM((together, rows, keys), jnp.bfloat16),
            pltpu.VMEM((together, rows, keys), jnp.bfloat16),
            pltpu.VMEM((together, rows, wide_buf), jnp.float32),
            pltpu.SemaphoreType.DMA((10,)),
            pltpu.SemaphoreType.DMA((count, 4, 4)),
        ],
        out_shape=out_shape,
        input_output_aliases=aliases,
        compiler_params=pltpu.CompilerParams(vmem_limit_bytes=40 * 2**20),
    )(*arguments)


def down_kernel(first_column, back_ref, one_ref, two_ref, hidden_ref, _, partial_hbm, down_buf, sems):
    features = hidden_ref.shape[1]
    value_back = back_ref[3 * RANK :, :].astype(jnp.float32)
    value_back = value_back + one_ref[...].astype(jnp.float32) + two_ref[...].astype(jnp.float32)
    back = jnp.concatenate([back_ref[:RANK, :], value_back.astype(jnp.bfloat16)], axis=0)
    down_buf[...] = mm(back, hidden_ref[...]).astype(jnp.bfloat16)
    copies = [
        pltpu.make_async_copy(
            down_buf.at[pl.ds(at * RANK, RANK)],
            partial_hbm.at[:, pl.ds(first_column + at * features, features)],
            sems.at[at],
        )
        for at in range(2)
    ]
    for each in copies:
        each.start()
    for each in copies:
        each.wait()


def final_kernel(scale, *refs):
    place = lax.axis_index("ctx") % NEAR
    gathered = [ref[...].astype(jnp.float32) * scale for ref in refs[:NEAR]]
    query_up_ref, value_up_ref, query_down_ref, value_down_ref = refs[NEAR:]
    parts = []
    for at in range(NEAR):
        distance = (at % 2 * 2 + at // 2) ^ place
        part = gathered[0]
        for other in range(1, NEAR):
            part = jnp.where(distance == other, gathered[other], part)
        parts.append(part)
    total = jnp.concatenate(parts, axis=1)
    column = 0
    for ref in (query_up_ref, value_up_ref, query_down_ref, value_down_ref):
        ref[...] = total[:, column : column + ref.shape[1]]
        column += ref.shape[1]


def head_sum(x):
    if lax.axis_size("head") == 2:
        other = lax.ppermute(x, "head", [(0, 1), (1, 0)])
        return (x.astype(jnp.float32) + other.astype(jnp.float32)).astype(x.dtype)
    return lax.psum(x, "head")


def ctx_sum(x):
    devices = lax.axis_size("ctx")
    place = lax.axis_index("ctx") % NEAR

    def exchange(value, distance):
        return lax.ppermute(value, "ctx", [(i, i ^ distance) for i in range(devices)])

    def halve(value, bit, distance):
        half = value.shape[1] // 2
        kept = lax.dynamic_slice_in_dim(value, bit * half, half, 1)
        given = lax.dynamic_slice_in_dim(value, (1 - bit) * half, half, 1)
        return add(kept, exchange(given, distance))

    def add(one, other):
        return (one.astype(jnp.float32) + other.astype(jnp.float32)).astype(jnp.bfloat16)

    x = halve(x, place % 2, 1)
    x = halve(x, place // 2, 2)
    distance = NEAR
    while distance < devices:
        radix = 4 if distance * 4 <= devices else 2
        others = [exchange(x, distance * part) for part in range(1, radix)]
        x = sum([other.astype(jnp.float32) for other in others], x.astype(jnp.float32))
        x = x.astype(jnp.bfloat16)
        distance *= radix
    return [x] + [exchange(x, distance) for distance in range(1, NEAR)]


def after(value, *others):
    return lax.optimization_barrier((value, *others))[0]


def per_device(
    hidden_states,
    query_base,
    key_base,
    frozen_value_rows,
    query_down,
    query_up,
    value_down,
    value_up_weight,
    positions,
    block_mask,
    output_gradient,
):
    tokens = hidden_states.shape[0]
    devices = lax.axis_size("ctx")
    kv_heads = key_base.shape[1] // HEAD_SIZE
    forward_one = [(i, i + 1) for i in range(devices - 1)]
    even_two = [(i, i + 2) for i in range(0, devices - 2, 2)]
    even_one = [(i, i + 1) for i in range(0, devices - 1, 2)]

    both_down = jnp.concatenate([query_down, value_down], axis=1)
    low = head_sum(mm(both_down, hidden_states, (((0,), (1,)), ((), ())))).astype(jnp.bfloat16)
    query_low_t = low[:RANK]
    value_low_t = low[RANK:]

    half = np.arange(HEAD_SIZE // 2, dtype=np.float64)
    frequency = (ROPE_BASE ** (-2.0 * half / HEAD_SIZE)).astype(np.float32)[:, None]

    def payload(chunk):
        first, last = chunk
        extra = RANK if first == 0 else 0
        return jax.ShapeDtypeStruct((tokens + extra, 2 * (last - first) * HEAD_SIZE), jnp.bfloat16)

    table = jax.ShapeDtypeStruct((tokens, HEAD_SIZE), jnp.float32)
    cosines, sines, packed_first = pl.pallas_call(
        functools.partial(prologue_kernel, CHUNKS[:1]),
        out_shape=[table, table, payload(CHUNKS[0])],
        compiler_params=pltpu.CompilerParams(vmem_limit_bytes=16 * 2**20),
    )(positions[None, :], jnp.asarray(frequency), key_base, frozen_value_rows)
    packed_first = lax.dynamic_update_slice(packed_first, value_low_t, (tokens, 0))
    key_extra, *packed_later = pl.pallas_call(
        functools.partial(later_prologue_kernel, CHUNKS[1:]),
        in_specs=[SMEM] + [VMEM] * 4,
        out_shape=[
            jax.ShapeDtypeStruct((3 * tokens, LANES), jnp.bfloat16),
            *(payload(chunk) for chunk in CHUNKS[1:]),
        ],
        compiler_params=pltpu.CompilerParams(vmem_limit_bytes=16 * 2**20),
    )(block_mask.T, cosines, after(sines, packed_first), key_base, frozen_value_rows)
    packed = [packed_first, *packed_later]

    query_ups = query_up.reshape(RANK, kv_heads, GROUP_WIDTH).transpose(1, 0, 2)
    value_ups = value_up_weight.reshape(RANK, kv_heads, HEAD_SIZE).transpose(1, 0, 2)
    shared = [query_ups, value_ups, query_low_t, cosines, sines]

    ones, evens = [], []
    for chunk, own in enumerate(packed):
        if chunk > 1:
            own = after(own, ones[chunk - 1], evens[chunk - 2])
        ones.append(lax.ppermute(own, "ctx", forward_one))
        evens.append(lax.ppermute(own, "ctx", even_two))

    features = hidden_states.shape[1]
    query_columns = kv_heads * GROUP_WIDTH
    value_columns = kv_heads * HEAD_SIZE
    columns = query_columns + value_columns + 2 * features
    columns = -(-columns // (NEAR * LANES)) * NEAR * LANES
    carried = None
    tables = [key_extra]
    for chunk, (first, last) in enumerate(CHUNKS):
        one = ones[chunk]
        one = after(one, evens[chunk], *([] if carried is None else [carried[2]]))
        odd = lax.ppermute(one, "ctx", even_one)
        *carried, = attention_chunk(
            first,
            last,
            TOGETHER[chunk],
            columns,
            query_base,
            output_gradient,
            [packed[chunk], one, evens[chunk], odd],
            shared,
            tables,
            carried,
        )
        tables = tables + carried[3:]
        carried = carried[:3]
    attention_out, partial, back = carried

    back = head_sum(back.astype(jnp.bfloat16))
    back_one = lax.ppermute(
        back[2 * RANK : 3 * RANK], "ctx", [(i + 1, i) for i in range(devices - 1)]
    )
    back_two = lax.ppermute(back[RANK : 2 * RANK], "ctx", [(i + 2, i) for i in range(devices - 2)])
    arguments = [back, back_one, back_two, hidden_states, partial]
    partial = pl.pallas_call(
        functools.partial(down_kernel, query_columns + value_columns),
        in_specs=[VMEM] * (len(arguments) - 1) + [ANY],
        out_specs=ANY,
        out_shape=jax.ShapeDtypeStruct(partial.shape, partial.dtype),
        scratch_shapes=[
            pltpu.VMEM((2 * RANK, features), jnp.bfloat16),
            pltpu.SemaphoreType.DMA((2,)),
        ],
        input_output_aliases={len(arguments) - 1: 0},
        compiler_params=pltpu.CompilerParams(vmem_limit_bytes=16 * 2**20),
    )(*arguments)
    gathered = ctx_sum(partial)
    widths = (query_columns, value_columns, features, features)
    up_query, up_value, down_query, down_value = pl.pallas_call(
        functools.partial(final_kernel, float((devices * tokens) ** (-0.5))),
        in_specs=[VMEM] * NEAR,
        out_specs=[VMEM] * 4,
        out_shape=[jax.ShapeDtypeStruct((RANK, width), jnp.float32) for width in widths],
    )(*gathered)
    return attention_out, down_query.T, up_query, down_value.T, up_value


def solution(mesh):
    placed = (
        P("ctx", "head"),
        P("ctx", "head"),
        P("ctx", "head"),
        P("ctx", "head"),
        P("head", None),
        P(None, "head"),
        P("head", None),
        P(None, "head"),
        P("ctx"),
        P(),
        P("ctx", "head"),
    )
    return jax.shard_map(
        per_device,
        mesh=mesh,
        in_specs=placed,
        out_specs=(
            P("ctx", "head"),
            P("head", None),
            P(None, "head"),
            P("head", None),
            P(None, "head"),
        ),
        check_vma=False,
    )
```

```python
import functools

import jax
import jax.numpy as jnp
import numpy as np
from jax import lax
from jax.experimental import pallas as pl
from jax.experimental.pallas import tpu as pltpu
from jax.sharding import PartitionSpec as P

D = 5376
QUERY_HEADS = 32
KEY_VALUE_HEADS = 16
HEAD_SIZE = 128
WINDOW = 1024
BLOCK = 128
GROUPS = QUERY_HEADS // KEY_VALUE_HEADS
GROUP_WIDTH = GROUPS * HEAD_SIZE
SCORE_SCALE = (D // QUERY_HEADS) ** (-0.5)
LOG2_E = 1.4426950408889634
ROPE_BASE = 10000.0
FORBIDDEN = -1e30
RANK = 16

SUB = 256
KEYS = SUB + WINDOW
LANES = 128
OFFSET_LANE = 64
ONES_LANE = RANK

CHUNKS = ((0, 2), (2, 5), (5, 8))
TOGETHER = (2, 1, 1)

ROWS_BY_COLS = (((1,), (0,)), ((), ()))
BOTH_MINOR = (((1,), (1,)), ((), ()))
BOTH_MAJOR = (((0,), (0,)), ((), ()))


def mm(left, right, dims=ROWS_BY_COLS):
    return lax.dot_general(left, right, dims, preferred_element_type=jnp.float32)


def swap_halves(x):
    return pltpu.roll(x, HEAD_SIZE // 2, 1)


def rotate_into(chunks, cosines, sines, key_ref, value_ref, outs):
    for (first, last), out_ref in zip(chunks, outs):
        count = last - first
        own = pl.ds(0, key_ref.shape[0])

        def one_head(head, carry, first=first, count=count, out_ref=out_ref, own=own):
            def cols(at):
                return pl.ds(pl.multiple_of(at * HEAD_SIZE, HEAD_SIZE), HEAD_SIZE)

            key = key_ref[:, cols(first + head)].astype(jnp.float32)
            rotated = key * cosines + swap_halves(key) * sines
            out_ref[own, cols(head)] = rotated.astype(jnp.bfloat16)
            out_ref[own, cols(count + head)] = value_ref[:, cols(first + head)]
            return carry

        lax.fori_loop(0, count, one_head, 0)


def prologue_kernel(chunks, positions_ref, frequency_ref, key_ref, value_ref, cos_ref, sin_ref, *outs):
    half = HEAD_SIZE // 2
    angles = frequency_ref[...] * positions_ref[...].astype(jnp.float32)
    both = jnp.transpose(jnp.concatenate([jnp.cos(angles), jnp.sin(angles)], axis=0))
    turned = swap_halves(both)
    low_half = lax.broadcasted_iota(jnp.int32, both.shape, 1) < half
    cosines = jnp.where(low_half, both, turned)
    sines = jnp.where(low_half, -turned, both)
    cos_ref[...] = cosines
    sin_ref[...] = sines
    rotate_into(chunks, cosines, sines, key_ref, value_ref, outs)


def later_prologue_kernel(chunks, mask_ref, cos_ref, sin_ref, key_ref, value_ref, extra_ref, *outs):
    rotate_into(chunks, cos_ref[...], sin_ref[...], key_ref, value_ref, outs)
    tokens = key_ref.shape[0]
    first_block = lax.axis_index("ctx") * (tokens // BLOCK)
    reach = WINDOW // BLOCK
    lane = lax.broadcasted_iota(jnp.int32, (BLOCK, LANES), 1)
    for key_block in range(extra_ref.shape[0] // BLOCK):
        extra = jnp.where(lane == OFFSET_LANE, 1.0, 0.0)
        exists = first_block + (key_block - reach) >= 0
        for block in range(tokens // BLOCK):
            offset = reach + block - key_block
            if 0 <= offset <= reach:
                hit = (mask_ref[offset, first_block + block] == 1) & exists
                term = jnp.where(hit, 0.0, FORBIDDEN)
            else:
                term = FORBIDDEN
            extra = jnp.where(lane == block, term, extra)
        extra_ref[key_block * BLOCK : (key_block + 1) * BLOCK, :] = extra.astype(jnp.bfloat16)


def attention_kernel(first, start, up_columns, *refs):
    (
        query_hbm,
        gradient_hbm,
        own_hbm,
        one_hbm,
        even_hbm,
        odd_hbm,
        query_up_ref,
        value_up_ref,
        query_low_t_ref,
        cos_ref,
        sin_ref,
        key_extra_hbm,
        *refs,
    ) = refs
    if not first:
        value_extra_hbm, _, _, back_in, *refs = refs
    out_hbm, partial_hbm, back_ref, *refs = refs
    if first:
        value_extra_hbm, *refs = refs
    (
        query_in,
        gradient_in,
        out_buf,
        up_query_buf,
        up_value_buf,
        low_buf,
        key_buf,
        value_buf,
        query_buf,
        gradient_buf,
        weight_buf,
        score_buf,
        product_buf,
        sems,
        head_sems,
    ) = refs
    heads = key_buf.shape[0]
    together = query_buf.shape[0]
    tokens = query_in.shape[1]
    keys = key_buf.shape[1]
    steps = tokens // SUB
    tiles = keys // SUB
    step_tiles = KEYS // SUB
    rows = GROUPS * SUB
    odd = lax.axis_index("ctx") % 2 == 1

    def copy(source, target, sem):
        return pltpu.make_async_copy(source, target, sem)

    def start_far(even_source, odd_source, target, sem):
        @pl.when(odd)
        def _():
            copy(odd_source, target, sem).start()

        @pl.when(jnp.logical_not(odd))
        def _():
            copy(even_source, target, sem).start()

        return copy(even_source, target, sem)

    own_rows = pl.ds(0, tokens)
    low_copies = []
    if first:
        last = pl.ds(tokens, RANK)
        low_copies.append(start_far(even_hbm.at[last], odd_hbm.at[last], low_buf.at[0], sems.at[3]))
        for at, source in ((1, one_hbm), (2, own_hbm)):
            low_copies.append(copy(source.at[last], low_buf.at[at], sems.at[3 + at]))
            low_copies[-1].start()
    def wide_copy(hbm, buf, head, kind, out=False):
        cols = pl.ds(pl.multiple_of((start + head) * GROUP_WIDTH, GROUP_WIDTH), GROUP_WIDTH)
        ends = (buf.at[head], hbm.at[:, cols]) if out else (hbm.at[:, cols], buf.at[head])
        return copy(*ends, head_sems.at[head, 2, kind])

    for head in range(heads):
        wide_copy(query_hbm, query_in, head, 0).start()
        for kind, buf, at in ((0, key_buf, head), (1, value_buf, heads + head)):
            cols = pl.ds(at * HEAD_SIZE, HEAD_SIZE)
            main = pl.ds(0, HEAD_SIZE)
            sem = head_sems.at[head, kind]
            copies = [
                start_far(
                    even_hbm.at[own_rows, cols],
                    odd_hbm.at[own_rows, cols],
                    buf.at[head, pl.ds(0, tokens), main],
                    sem.at[0],
                ),
                copy(one_hbm.at[own_rows, cols], buf.at[head, pl.ds(tokens, tokens), main], sem.at[1]),
                copy(own_hbm.at[own_rows, cols], buf.at[head, pl.ds(2 * tokens, tokens), main], sem.at[2]),
            ]
            if kind == 0 or not first:
                extra_hbm = (key_extra_hbm, value_extra_hbm)[kind]
                copies.append(copy(extra_hbm, buf.at[head, :, pl.ds(HEAD_SIZE, LANES)], sem.at[3]))
            for later in copies[1:]:
                later.start()
        wide_copy(gradient_hbm, gradient_in, head, 1).start()

    if first:
        for low_copy in low_copies:
            low_copy.wait()
        low = jnp.concatenate([low_buf[at] for at in range(3)], axis=1)
        low = jnp.concatenate(
            [
                low.astype(jnp.float32),
                jnp.ones((2, keys), jnp.float32),
                jnp.zeros((LANES - RANK - 2, keys), jnp.float32),
            ],
            axis=0,
        )
        low = jnp.transpose(low).astype(jnp.bfloat16)
        for head in range(heads):
            value_buf[head, :, HEAD_SIZE:] = low
        extras = (copy(value_buf.at[0, :, pl.ds(HEAD_SIZE, LANES)], value_extra_hbm, sems.at[7]),)
        for extra_copy in extras:
            extra_copy.start()
        back_ref[...] = jnp.zeros_like(back_ref)
    else:
        extras = ()
        back_ref[...] = back_in[...]

    lane = lax.broadcasted_iota(jnp.int32, (rows, LANES), 1)
    row = lax.broadcasted_iota(jnp.int32, (rows, LANES), 0) % SUB
    ones = slice(HEAD_SIZE + ONES_LANE, HEAD_SIZE + ONES_LANE + 1)

    def own(step):
        return slice(step * SUB, (step + 1) * SUB)

    def span(step):
        return slice(step * rows, (step + 1) * rows)

    def window(step):
        return slice(step * SUB, step * SUB + KEYS)

    def tile_steps(tile):
        return max(0, tile - step_tiles + 1), min(steps, tile + 1)

    def member_cols(member):
        return slice(member * HEAD_SIZE, (member + 1) * HEAD_SIZE)

    def value_up_of(head):
        return jnp.concatenate(
            [value_up_ref[start + head], jnp.zeros((LANES - RANK, HEAD_SIZE), jnp.bfloat16)], axis=0
        )

    def limit(step, tile, part):
        place = tile - step
        if 0 < place < step_tiles - 1:
            return part
        halves = []
        for block in range(SUB // BLOCK):
            inside = lane > row % BLOCK if place == 0 else lane <= row % BLOCK
            inside = inside | (row // BLOCK != block)
            halves.append(
                jnp.where(inside, part[:, block * BLOCK : (block + 1) * BLOCK], FORBIDDEN)
            )
        return jnp.concatenate(halves, axis=1)

    def prepare(head, slot):
        reach_of_key = jnp.max(
            jnp.abs(key_buf[head, :, :HEAD_SIZE].astype(jnp.float32)), axis=0, keepdims=True
        )
        for step in range(steps):
            cosines = cos_ref[own(step), :]
            sines = sin_ref[own(step), :]
            adapted = mm(query_low_t_ref[:, own(step)], query_up_ref[start + head], BOTH_MAJOR)
            turned = []
            for member in range(GROUPS):
                part = query_in[head, own(step), member_cols(member)].astype(jnp.float32)
                part = part + adapted[:, member * HEAD_SIZE : (member + 1) * HEAD_SIZE]
                turned.append(part * cosines + swap_halves(part) * sines)
            queries = jnp.concatenate(turned, axis=0) * (SCORE_SCALE * LOG2_E)
            bound = jnp.sum(jnp.abs(queries) * reach_of_key, axis=1, keepdims=True)
            chosen = (lane == row // BLOCK + step * (SUB // BLOCK)).astype(jnp.float32)
            query_buf[slot, span(step), :HEAD_SIZE] = queries.astype(jnp.bfloat16)
            query_buf[slot, span(step), HEAD_SIZE:] = jnp.where(
                lane == OFFSET_LANE, -bound, chosen
            ).astype(jnp.bfloat16)

    def forward_scores(head, slot):
        for tile in range(tiles):
            low, high = tile_steps(tile)
            cols = slice(tile * SUB, (tile + 1) * SUB)
            scores = mm(
                query_buf[slot, low * rows : high * rows, :], key_buf[head, cols, :], BOTH_MINOR
            )
            for step in range(low, high):
                part = limit(step, tile, scores[(step - low) * rows : (step - low + 1) * rows, :])
                weight_buf[slot, span(step), cols] = jnp.exp2(part).astype(jnp.bfloat16)

    def forward_products(head, slot):
        for step in range(steps):
            product_buf[slot, span(step), :] = mm(
                weight_buf[slot, span(step), window(step)], value_buf[head, window(step), :]
            )

    def repeat(head, slot):
        diagonal = lane - row % BLOCK

        def one_step(step, carry):
            here = pl.ds(pl.multiple_of(step * rows, rows), rows)

            def scores_of(tile):
                cols = pl.ds(pl.multiple_of((step + tile) * SUB, SUB), SUB)
                part = mm(query_buf[slot, here, :], key_buf[head, cols, :], BOTH_MINOR)
                lowest = jnp.where(tile == 0, 1, -BLOCK)
                highest = jnp.where(tile == step_tiles - 1, 0, BLOCK)
                halves = []
                for block in range(SUB // BLOCK):
                    inside = (diagonal >= lowest) & (diagonal <= highest)
                    inside = inside | (row // BLOCK != block)
                    halves.append(
                        jnp.where(inside, part[:, block * BLOCK : (block + 1) * BLOCK], FORBIDDEN)
                    )
                return jnp.concatenate(halves, axis=1), cols

            def top(tile, highest):
                part, _ = scores_of(tile)
                return jnp.maximum(highest, jnp.max(part, axis=1, keepdims=True))

            def again(tile, sums):
                part, cols = scores_of(tile)
                weights = jnp.exp2(part).astype(jnp.bfloat16)
                weight_buf[slot, here, cols] = weights
                return sums + mm(weights, value_buf[head, cols, :])

            extra = query_buf[slot, here, HEAD_SIZE:].astype(jnp.float32)
            query_buf[slot, here, HEAD_SIZE:] = jnp.where(lane == OFFSET_LANE, 0.0, extra).astype(
                jnp.bfloat16
            )
            highest = lax.fori_loop(
                0, step_tiles, top, jnp.full((rows, 1), FORBIDDEN, jnp.float32)
            )
            query_buf[slot, here, HEAD_SIZE:] = jnp.where(lane == OFFSET_LANE, -highest, extra).astype(
                jnp.bfloat16
            )
            product_buf[slot, here, :] = lax.fori_loop(
                0, step_tiles, again, jnp.zeros((rows, HEAD_SIZE + LANES), jnp.float32)
            )
            return carry

        lax.fori_loop(0, steps, one_step, 0)

    kept = {}

    def finish_forward(head, slot):
        value_up = value_up_of(head)
        spreads = []
        inverses = []
        up_value = jnp.zeros((LANES, HEAD_SIZE), jnp.float32)
        for step in range(steps):
            gradient = jnp.concatenate(
                [gradient_in[head, own(step), member_cols(member)] for member in range(GROUPS)], axis=0
            )
            gradient_low = mm(gradient, value_up, BOTH_MINOR)
            inverse = 1.0 / product_buf[slot, span(step), ones]
            low_part = (product_buf[slot, span(step), HEAD_SIZE:] * inverse).astype(jnp.bfloat16)
            outputs = product_buf[slot, span(step), :HEAD_SIZE] * inverse + mm(low_part, value_up)
            outputs = outputs.astype(jnp.bfloat16)
            for member in range(GROUPS):
                out_buf[head, own(step), member_cols(member)] = outputs[own(member), :]
            delta = jnp.sum(
                outputs.astype(jnp.float32) * gradient.astype(jnp.float32), axis=1, keepdims=True
            )
            delta_high = delta.astype(jnp.bfloat16).astype(jnp.float32)
            extra = jnp.where(lane == ONES_LANE, -delta_high, gradient_low)
            extra = jnp.where(lane == ONES_LANE + 1, delta_high - delta, extra)
            gradient_buf[slot, span(step), :HEAD_SIZE] = gradient
            gradient_buf[slot, span(step), HEAD_SIZE:] = extra.astype(jnp.bfloat16)
            up_value += mm(low_part, gradient, BOTH_MAJOR)
            spreads.append(jnp.transpose(gradient_low * inverse)[:RANK, :].astype(jnp.bfloat16))
            inverses.append(inverse * SCORE_SCALE)
        up_value_buf[head] = up_value[:RANK, :].astype(jnp.bfloat16)
        wide_copy(out_hbm, out_buf, head, 2, out=True).start()
        kept[slot] = jnp.concatenate(spreads, axis=1), inverses

    def backward_scores(head, slot):
        spread = kept[slot][0]
        for tile in range(tiles):
            low, high = tile_steps(tile)
            cols = slice(tile * SUB, (tile + 1) * SUB)
            back_row = RANK + tile * SUB // tokens * RANK
            back_rows = slice(back_row, back_row + RANK)
            back_cols = slice(tile * SUB % tokens, tile * SUB % tokens + SUB)
            part = slice(low * rows, high * rows)
            grad_weights = mm(gradient_buf[slot, part, :], value_buf[head, cols, :], BOTH_MINOR)
            weights = weight_buf[slot, part, cols]
            score_buf[slot, part, cols] = weights * grad_weights.astype(jnp.bfloat16)
            back_ref[back_rows, back_cols] += mm(spread[:, part], weights)

    def backward_products(head, slot):
        query_grads = []
        for step in range(steps):
            cosines = cos_ref[own(step), :]
            sines = sin_ref[own(step), :]
            sums = mm(score_buf[slot, span(step), window(step)], key_buf[head, window(step), :HEAD_SIZE])
            sums = sums * kept[slot][1][step]
            turned = []
            for member in range(GROUPS):
                part = sums[own(member), :]
                turned.append(part * cosines - swap_halves(part) * sines)
            query_grads.append(jnp.concatenate(turned, axis=1).astype(jnp.bfloat16))
        query_grad = jnp.concatenate(query_grads, axis=0)
        up_query_buf[head] = mm(query_low_t_ref[...], query_grad).astype(jnp.bfloat16)
        back_ref[:RANK, :] += mm(query_up_ref[start + head], query_grad, BOTH_MINOR)

    def arrive(head, kind):
        buf = (key_buf, value_buf)[kind]
        main = pl.ds(0, HEAD_SIZE)
        source = one_hbm.at[own_rows, main]
        for part in range(3):
            copy(
                source, buf.at[head, pl.ds(part * tokens, tokens), main], head_sems.at[head, kind, part]
            ).wait()
        if kind == 0 or not first:
            extra_hbm = (key_extra_hbm, value_extra_hbm)[kind]
            copy(
                extra_hbm, buf.at[head, :, pl.ds(HEAD_SIZE, LANES)], head_sems.at[head, kind, 3]
            ).wait()

    def arrive_and_prepare(head, slot):
        arrive(head, 0)
        wide_copy(query_hbm, query_in, head, 0).wait()
        prepare(head, slot)

    def work(group, carry):
        members = [(group * together + slot, slot) for slot in range(together)]
        arrive_and_prepare(*members[0])
        for head, slot in members:
            forward_scores(head, slot)
            if slot + 1 < together:
                arrive_and_prepare(*members[slot + 1])
            arrive(head, 1)
            forward_products(head, slot)

        @pl.when(jnp.min(product_buf[:, :, ones]) < 1e-27)
        def _():
            lax.fori_loop(0, together, lambda slot, c: (repeat(group * together + slot, slot), c)[1], 0)

        for head, slot in members:
            wide_copy(gradient_hbm, gradient_in, head, 1).wait()
        finish_forward(*members[0])
        for head, slot in members:
            backward_scores(head, slot)
            if slot + 1 < together:
                finish_forward(*members[slot + 1])
            backward_products(head, slot)
        return carry

    if heads == together:
        work(0, 0)
    else:
        lax.fori_loop(0, heads // together, work, 0)
    up_copies = []
    for head in range(heads):
        at = pl.ds((start + head) * GROUP_WIDTH, GROUP_WIDTH)
        up_copies.append(copy(up_query_buf.at[head], partial_hbm.at[:, at], head_sems.at[head, 3, 0]))
        at = pl.ds(up_columns + (start + head) * HEAD_SIZE, HEAD_SIZE)
        up_copies.append(copy(up_value_buf.at[head], partial_hbm.at[:, at], head_sems.at[head, 3, 1]))
    for up_copy in up_copies:
        up_copy.start()
    for head in range(heads):
        wide_copy(out_hbm, out_buf, head, 2, out=True).wait()
    for done in (*extras, *up_copies):
        done.wait()


VMEM = pl.BlockSpec(memory_space=pltpu.VMEM)
SMEM = pl.BlockSpec(memory_space=pltpu.SMEM)
ANY = pl.BlockSpec(memory_space=pl.ANY)
NEAR = 4


def attention_chunk(
    first, last, together, columns, query_base, gradient, received, shared, tables, carried
):
    count = last - first
    tokens = query_base.shape[0]
    keys = 3 * tokens
    rows = GROUPS * tokens
    out_specs = [ANY, ANY, VMEM]
    out_shape = [
        jax.ShapeDtypeStruct(query_base.shape, jnp.bfloat16),
        jax.ShapeDtypeStruct((RANK, columns), jnp.bfloat16),
        jax.ShapeDtypeStruct((RANK + keys // tokens * RANK, tokens), jnp.float32),
    ]
    if carried is None:
        out_specs.append(ANY)
        out_shape.append(jax.ShapeDtypeStruct((keys, LANES), jnp.bfloat16))
    arguments = [query_base, gradient, *received, *shared, *tables]
    in_specs = [ANY] * 6 + [VMEM] * len(shared) + [ANY] * len(tables)
    aliases = {}
    if carried is not None:
        arguments += carried
        in_specs += [ANY, ANY, VMEM]
        aliases = {len(arguments) - 3: 0, len(arguments) - 2: 1}
    wide_buf = HEAD_SIZE + LANES
    return pl.pallas_call(
        functools.partial(attention_kernel, carried is None, first, query_base.shape[1]),
        in_specs=in_specs,
        out_specs=out_specs,
        scratch_shapes=[
            pltpu.VMEM((count, tokens, GROUP_WIDTH), jnp.bfloat16),
            pltpu.VMEM((count, tokens, GROUP_WIDTH), jnp.bfloat16),
            pltpu.VMEM((count, tokens, GROUP_WIDTH), jnp.bfloat16),
            pltpu.VMEM((count, RANK, GROUP_WIDTH), jnp.bfloat16),
            pltpu.VMEM((count, RANK, HEAD_SIZE), jnp.bfloat16),
            pltpu.VMEM((3, RANK, tokens), jnp.bfloat16),
            pltpu.VMEM((count, keys, wide_buf), jnp.bfloat16),
            pltpu.VMEM((count, keys, wide_buf), jnp.bfloat16),
            pltpu.VMEM((together, rows, wide_buf), jnp.bfloat16),
            pltpu.VMEM((together, rows, wide_buf), jnp.bfloat16),
            pltpu.VMEM((together, rows, keys), jnp.bfloat16),
            pltpu.VMEM((together, rows, keys), jnp.bfloat16),
            pltpu.VMEM((together, rows, wide_buf), jnp.float32),
            pltpu.SemaphoreType.DMA((10,)),
            pltpu.SemaphoreType.DMA((count, 4, 4)),
        ],
        out_shape=out_shape,
        input_output_aliases=aliases,
        compiler_params=pltpu.CompilerParams(vmem_limit_bytes=40 * 2**20),
    )(*arguments)


def down_kernel(first_column, back_ref, one_ref, two_ref, hidden_ref, _, partial_hbm, down_buf, sems):
    features = hidden_ref.shape[1]
    value_back = back_ref[3 * RANK :, :].astype(jnp.float32)
    value_back = value_back + one_ref[...].astype(jnp.float32) + two_ref[...].astype(jnp.float32)
    back = jnp.concatenate([back_ref[:RANK, :], value_back.astype(jnp.bfloat16)], axis=0)
    down_buf[...] = mm(back, hidden_ref[...]).astype(jnp.bfloat16)
    copies = [
        pltpu.make_async_copy(
            down_buf.at[pl.ds(at * RANK, RANK)],
            partial_hbm.at[:, pl.ds(first_column + at * features, features)],
            sems.at[at],
        )
        for at in range(2)
    ]
    for each in copies:
        each.start()
    for each in copies:
        each.wait()


def final_kernel(scale, *refs):
    place = lax.axis_index("ctx") % NEAR
    gathered = [ref[...].astype(jnp.float32) * scale for ref in refs[:NEAR]]
    query_up_ref, value_up_ref, query_down_ref, value_down_ref = refs[NEAR:]
    parts = []
    for at in range(NEAR):
        distance = (at % 2 * 2 + at // 2) ^ place
        part = gathered[0]
        for other in range(1, NEAR):
            part = jnp.where(distance == other, gathered[other], part)
        parts.append(part)
    total = jnp.concatenate(parts, axis=1)
    column = 0
    for ref in (query_up_ref, value_up_ref, query_down_ref, value_down_ref):
        ref[...] = total[:, column : column + ref.shape[1]]
        column += ref.shape[1]


def head_sum(x):
    if lax.axis_size("head") == 2:
        other = lax.ppermute(x, "head", [(0, 1), (1, 0)])
        return (x.astype(jnp.float32) + other.astype(jnp.float32)).astype(x.dtype)
    return lax.psum(x, "head")


def ctx_sum(x):
    devices = lax.axis_size("ctx")
    place = lax.axis_index("ctx") % NEAR

    def exchange(value, distance):
        return lax.ppermute(value, "ctx", [(i, i ^ distance) for i in range(devices)])

    def halve(value, bit, distance):
        half = value.shape[1] // 2
        kept = lax.dynamic_slice_in_dim(value, bit * half, half, 1)
        given = lax.dynamic_slice_in_dim(value, (1 - bit) * half, half, 1)
        return add(kept, exchange(given, distance))

    def add(one, other):
        return (one.astype(jnp.float32) + other.astype(jnp.float32)).astype(jnp.bfloat16)

    x = halve(x, place % 2, 1)
    x = halve(x, place // 2, 2)
    distance = NEAR
    while distance < devices:
        radix = 4 if distance * 4 <= devices else 2
        others = [exchange(x, distance * part) for part in range(1, radix)]
        x = sum([other.astype(jnp.float32) for other in others], x.astype(jnp.float32))
        x = x.astype(jnp.bfloat16)
        distance *= radix
    return [x] + [exchange(x, distance) for distance in range(1, NEAR)]


def after(value, *others):
    return lax.optimization_barrier((value, *others))[0]


def per_device(
    hidden_states,
    query_base,
    key_base,
    frozen_value_rows,
    query_down,
    query_up,
    value_down,
    value_up_weight,
    positions,
    block_mask,
    output_gradient,
):
    tokens = hidden_states.shape[0]
    devices = lax.axis_size("ctx")
    kv_heads = key_base.shape[1] // HEAD_SIZE
    forward_one = [(i, i + 1) for i in range(devices - 1)]
    even_two = [(i, i + 2) for i in range(0, devices - 2, 2)]
    even_one = [(i, i + 1) for i in range(0, devices - 1, 2)]

    both_down = jnp.concatenate([query_down, value_down], axis=1)
    low = head_sum(mm(both_down, hidden_states, (((0,), (1,)), ((), ())))).astype(jnp.bfloat16)
    query_low_t = low[:RANK]
    value_low_t = low[RANK:]

    half = np.arange(HEAD_SIZE // 2, dtype=np.float64)
    frequency = (ROPE_BASE ** (-2.0 * half / HEAD_SIZE)).astype(np.float32)[:, None]

    def payload(chunk):
        first, last = chunk
        extra = RANK if first == 0 else 0
        return jax.ShapeDtypeStruct((tokens + extra, 2 * (last - first) * HEAD_SIZE), jnp.bfloat16)

    table = jax.ShapeDtypeStruct((tokens, HEAD_SIZE), jnp.float32)
    cosines, sines, packed_first = pl.pallas_call(
        functools.partial(prologue_kernel, CHUNKS[:1]),
        out_shape=[table, table, payload(CHUNKS[0])],
        compiler_params=pltpu.CompilerParams(vmem_limit_bytes=16 * 2**20),
    )(positions[None, :], jnp.asarray(frequency), key_base, frozen_value_rows)
    packed_first = lax.dynamic_update_slice(packed_first, value_low_t, (tokens, 0))
    key_extra, *packed_later = pl.pallas_call(
        functools.partial(later_prologue_kernel, CHUNKS[1:]),
        in_specs=[SMEM] + [VMEM] * 4,
        out_shape=[
            jax.ShapeDtypeStruct((3 * tokens, LANES), jnp.bfloat16),
            *(payload(chunk) for chunk in CHUNKS[1:]),
        ],
        compiler_params=pltpu.CompilerParams(vmem_limit_bytes=16 * 2**20),
    )(block_mask.T, cosines, after(sines, packed_first), key_base, frozen_value_rows)
    packed = [packed_first, *packed_later]

    query_ups = query_up.reshape(RANK, kv_heads, GROUP_WIDTH).transpose(1, 0, 2)
    value_ups = value_up_weight.reshape(RANK, kv_heads, HEAD_SIZE).transpose(1, 0, 2)
    shared = [query_ups, value_ups, query_low_t, cosines, sines]

    ones, evens = [], []
    for chunk, own in enumerate(packed):
        if chunk > 1:
            own = after(own, ones[chunk - 1], evens[chunk - 2])
        ones.append(lax.ppermute(own, "ctx", forward_one))
        evens.append(lax.ppermute(own, "ctx", even_two))

    features = hidden_states.shape[1]
    query_columns = kv_heads * GROUP_WIDTH
    value_columns = kv_heads * HEAD_SIZE
    columns = query_columns + value_columns + 2 * features
    columns = -(-columns // (NEAR * LANES)) * NEAR * LANES
    carried = None
    tables = [key_extra]
    for chunk, (first, last) in enumerate(CHUNKS):
        one = ones[chunk]
        one = after(one, evens[chunk], *([] if carried is None else [carried[2]]))
        odd = lax.ppermute(one, "ctx", even_one)
        *carried, = attention_chunk(
            first,
            last,
            TOGETHER[chunk],
            columns,
            query_base,
            output_gradient,
            [packed[chunk], one, evens[chunk], odd],
            shared,
            tables,
            carried,
        )
        tables = tables + carried[3:]
        carried = carried[:3]
    attention_out, partial, back = carried

    back = head_sum(back.astype(jnp.bfloat16))
    back_one = lax.ppermute(
        back[2 * RANK : 3 * RANK], "ctx", [(i + 1, i) for i in range(devices - 1)]
    )
    back_two = lax.ppermute(back[RANK : 2 * RANK], "ctx", [(i + 2, i) for i in range(devices - 2)])
    arguments = [back, back_one, back_two, hidden_states, partial]
    partial = pl.pallas_call(
        functools.partial(down_kernel, query_columns + value_columns),
        in_specs=[VMEM] * (len(arguments) - 1) + [ANY],
        out_specs=ANY,
        out_shape=jax.ShapeDtypeStruct(partial.shape, partial.dtype),
        scratch_shapes=[
            pltpu.VMEM((2 * RANK, features), jnp.bfloat16),
            pltpu.SemaphoreType.DMA((2,)),
        ],
        input_output_aliases={len(arguments) - 1: 0},
        compiler_params=pltpu.CompilerParams(vmem_limit_bytes=16 * 2**20),
    )(*arguments)
    gathered = ctx_sum(partial)
    widths = (query_columns, value_columns, features, features)
    up_query, up_value, down_query, down_value = pl.pallas_call(
        functools.partial(final_kernel, float((devices * tokens) ** (-0.5))),
        in_specs=[VMEM] * NEAR,
        out_specs=[VMEM] * 4,
        out_shape=[jax.ShapeDtypeStruct((RANK, width), jnp.float32) for width in widths],
    )(*gathered)
    return attention_out, down_query.T, up_query, down_value.T, up_value


def solution(mesh):
    placed = (
        P("ctx", "head"),
        P("ctx", "head"),
        P("ctx", "head"),
        P("ctx", "head"),
        P("head", None),
        P(None, "head"),
        P("head", None),
        P(None, "head"),
        P("ctx"),
        P(),
        P("ctx", "head"),
    )
    return jax.shard_map(
        per_device,
        mesh=mesh,
        in_specs=placed,
        out_specs=(
            P("ctx", "head"),
            P("head", None),
            P(None, "head"),
            P("head", None),
            P(None, "head"),
        ),
        check_vma=False,
    )
```

```python
import functools

import jax
import jax.numpy as jnp
import numpy as np
from jax import lax
from jax.experimental import pallas as pl
from jax.experimental.pallas import tpu as pltpu
from jax.sharding import PartitionSpec as P

D = 5376
QUERY_HEADS = 32
KEY_VALUE_HEADS = 16
HEAD_SIZE = 128
WINDOW = 1024
BLOCK = 128
GROUPS = QUERY_HEADS // KEY_VALUE_HEADS
GROUP_WIDTH = GROUPS * HEAD_SIZE
SCORE_SCALE = (D // QUERY_HEADS) ** (-0.5)
LOG2_E = 1.4426950408889634
ROPE_BASE = 10000.0
FORBIDDEN = -1e30
RANK = 16

SUB = 256
KEYS = SUB + WINDOW
LANES = 128
OFFSET_LANE = 64
ONES_LANE = RANK

CHUNKS = ((0, 2), (2, 5), (5, 8))

ROWS_BY_COLS = (((1,), (0,)), ((), ()))
BOTH_MINOR = (((1,), (1,)), ((), ()))
BOTH_MAJOR = (((0,), (0,)), ((), ()))


def mm(left, right, dims=ROWS_BY_COLS):
    return lax.dot_general(left, right, dims, preferred_element_type=jnp.float32)


def swap_halves(x):
    return pltpu.roll(x, HEAD_SIZE // 2, 1)


def rotate_into(chunks, cosines, sines, key_ref, value_ref, outs):
    for (first, last), out_ref in zip(chunks, outs):
        count = last - first
        own = pl.ds(0, key_ref.shape[0])

        def one_head(head, carry, first=first, count=count, out_ref=out_ref, own=own):
            def cols(at):
                return pl.ds(pl.multiple_of(at * HEAD_SIZE, HEAD_SIZE), HEAD_SIZE)

            key = key_ref[:, cols(first + head)].astype(jnp.float32)
            rotated = key * cosines + swap_halves(key) * sines
            out_ref[own, cols(head)] = rotated.astype(jnp.bfloat16)
            out_ref[own, cols(count + head)] = value_ref[:, cols(first + head)]
            return carry

        lax.fori_loop(0, count, one_head, 0)


def prologue_kernel(chunks, positions_ref, frequency_ref, key_ref, value_ref, cos_ref, sin_ref, *outs):
    half = HEAD_SIZE // 2
    angles = frequency_ref[...] * positions_ref[...].astype(jnp.float32)
    both = jnp.transpose(jnp.concatenate([jnp.cos(angles), jnp.sin(angles)], axis=0))
    turned = swap_halves(both)
    low_half = lax.broadcasted_iota(jnp.int32, both.shape, 1) < half
    cosines = jnp.where(low_half, both, turned)
    sines = jnp.where(low_half, -turned, both)
    cos_ref[...] = cosines
    sin_ref[...] = sines
    rotate_into(chunks, cosines, sines, key_ref, value_ref, outs)


def later_prologue_kernel(chunks, mask_ref, cos_ref, sin_ref, key_ref, value_ref, extra_ref, *outs):
    rotate_into(chunks, cos_ref[...], sin_ref[...], key_ref, value_ref, outs)
    tokens = key_ref.shape[0]
    first_block = lax.axis_index("ctx") * (tokens // BLOCK)
    reach = WINDOW // BLOCK
    lane = lax.broadcasted_iota(jnp.int32, (BLOCK, LANES), 1)
    for key_block in range(extra_ref.shape[0] // BLOCK):
        extra = jnp.where(lane == OFFSET_LANE, 1.0, 0.0)
        exists = first_block + (key_block - reach) >= 0
        for block in range(tokens // BLOCK):
            offset = reach + block - key_block
            if 0 <= offset <= reach:
                hit = (mask_ref[offset, first_block + block] == 1) & exists
                term = jnp.where(hit, 0.0, FORBIDDEN)
            else:
                term = FORBIDDEN
            extra = jnp.where(lane == block, term, extra)
        extra_ref[key_block * BLOCK : (key_block + 1) * BLOCK, :] = extra.astype(jnp.bfloat16)


def attention_kernel(first, start, up_columns, *refs):
    (
        query_hbm,
        gradient_hbm,
        own_hbm,
        one_hbm,
        even_hbm,
        odd_hbm,
        query_up_ref,
        value_up_ref,
        query_low_t_ref,
        cos_ref,
        sin_ref,
        key_extra_hbm,
        *refs,
    ) = refs
    if not first:
        value_extra_hbm, _, _, back_in, *refs = refs
    out_hbm, partial_hbm, back_ref, *refs = refs
    if first:
        value_extra_hbm, *refs = refs
    (
        query_in,
        gradient_in,
        out_buf,
        up_query_buf,
        up_value_buf,
        low_buf,
        key_buf,
        value_buf,
        query_buf,
        gradient_buf,
        weight_buf,
        score_buf,
        product_buf,
        sems,
        head_sems,
    ) = refs
    heads = key_buf.shape[0]
    tokens = query_in.shape[1]
    keys = key_buf.shape[1]
    steps = tokens // SUB
    tiles = keys // SUB
    step_tiles = KEYS // SUB
    rows = GROUPS * SUB
    odd = lax.axis_index("ctx") % 2 == 1

    def copy(source, target, sem):
        return pltpu.make_async_copy(source, target, sem)

    def start_far(even_source, odd_source, target, sem):
        @pl.when(odd)
        def _():
            copy(odd_source, target, sem).start()

        @pl.when(jnp.logical_not(odd))
        def _():
            copy(even_source, target, sem).start()

        return copy(even_source, target, sem)

    own_rows = pl.ds(0, tokens)
    low_copies = []
    if first:
        last = pl.ds(tokens, RANK)
        low_copies.append(start_far(even_hbm.at[last], odd_hbm.at[last], low_buf.at[0], sems.at[3]))
        for at, source in ((1, one_hbm), (2, own_hbm)):
            low_copies.append(copy(source.at[last], low_buf.at[at], sems.at[3 + at]))
            low_copies[-1].start()
    def wide_copy(hbm, buf, head, kind, out=False):
        cols = pl.ds(pl.multiple_of((start + head) * GROUP_WIDTH, GROUP_WIDTH), GROUP_WIDTH)
        ends = (buf.at[head], hbm.at[:, cols]) if out else (hbm.at[:, cols], buf.at[head])
        return copy(*ends, head_sems.at[head, 2, kind])

    def start_copies(head):
        def cols(at):
            return pl.ds(pl.multiple_of(at * HEAD_SIZE, HEAD_SIZE), HEAD_SIZE)

        main = pl.ds(0, HEAD_SIZE)
        wide_copy(query_hbm, query_in, head, 0).start()
        for kind, buf, at in ((0, key_buf, cols(head)), (1, value_buf, cols(heads + head))):
            start_far(
                even_hbm.at[own_rows, at],
                odd_hbm.at[own_rows, at],
                buf.at[head, pl.ds(0, tokens), main],
                head_sems.at[head, kind, 0],
            )
            for part, source in ((1, one_hbm), (2, own_hbm)):
                copy(
                    source.at[own_rows, at],
                    buf.at[head, pl.ds(part * tokens, tokens), main],
                    head_sems.at[head, kind, part],
                ).start()
            if kind == 0 or not first:
                extra_hbm = (key_extra_hbm, value_extra_hbm)[kind]
                copy(
                    extra_hbm, buf.at[head, :, pl.ds(HEAD_SIZE, LANES)], head_sems.at[head, kind, 3]
                ).start()
        wide_copy(gradient_hbm, gradient_in, head, 1).start()

    start_copies(0)

    if first:
        for low_copy in low_copies:
            low_copy.wait()
        low = jnp.concatenate([low_buf[at] for at in range(3)], axis=1)
        low = jnp.concatenate(
            [
                low.astype(jnp.float32),
                jnp.ones((2, keys), jnp.float32),
                jnp.zeros((LANES - RANK - 2, keys), jnp.float32),
            ],
            axis=0,
        )
        low = jnp.transpose(low).astype(jnp.bfloat16)
        for head in range(heads):
            value_buf[head, :, HEAD_SIZE:] = low
        extras = (copy(value_buf.at[0, :, pl.ds(HEAD_SIZE, LANES)], value_extra_hbm, sems.at[7]),)
        for extra_copy in extras:
            extra_copy.start()
        back_ref[...] = jnp.zeros_like(back_ref)
    else:
        extras = ()
        back_ref[...] = back_in[...]

    lane = lax.broadcasted_iota(jnp.int32, (rows, LANES), 1)
    row = lax.broadcasted_iota(jnp.int32, (rows, LANES), 0) % SUB
    ones = slice(HEAD_SIZE + ONES_LANE, HEAD_SIZE + ONES_LANE + 1)

    def own(step):
        return slice(step * SUB, (step + 1) * SUB)

    def span(step):
        return slice(step * rows, (step + 1) * rows)

    def window(step):
        return slice(step * SUB, step * SUB + KEYS)

    def tile_steps(tile):
        return max(0, tile - step_tiles + 1), min(steps, tile + 1)

    def member_cols(member):
        return slice(member * HEAD_SIZE, (member + 1) * HEAD_SIZE)

    def value_up_of(head):
        return jnp.concatenate(
            [value_up_ref[start + head], jnp.zeros((LANES - RANK, HEAD_SIZE), jnp.bfloat16)], axis=0
        )

    def limit(step, tile, part):
        place = tile - step
        if 0 < place < step_tiles - 1:
            return part
        halves = []
        for block in range(SUB // BLOCK):
            inside = lane > row % BLOCK if place == 0 else lane <= row % BLOCK
            inside = inside | (row // BLOCK != block)
            halves.append(
                jnp.where(inside, part[:, block * BLOCK : (block + 1) * BLOCK], FORBIDDEN)
            )
        return jnp.concatenate(halves, axis=1)

    def prepare(head, slot):
        reach_of_key = jnp.max(
            jnp.abs(key_buf[head, :, :HEAD_SIZE].astype(jnp.float32)), axis=0, keepdims=True
        )
        for step in range(steps):
            cosines = cos_ref[own(step), :]
            sines = sin_ref[own(step), :]
            adapted = mm(query_low_t_ref[:, own(step)], query_up_ref[start + head], BOTH_MAJOR)
            turned = []
            for member in range(GROUPS):
                part = query_in[head, own(step), member_cols(member)].astype(jnp.float32)
                part = part + adapted[:, member * HEAD_SIZE : (member + 1) * HEAD_SIZE]
                turned.append(part * cosines + swap_halves(part) * sines)
            queries = jnp.concatenate(turned, axis=0) * (SCORE_SCALE * LOG2_E)
            bound = jnp.sum(jnp.abs(queries) * reach_of_key, axis=1, keepdims=True)
            chosen = (lane == row // BLOCK + step * (SUB // BLOCK)).astype(jnp.float32)
            query_buf[slot, span(step), :HEAD_SIZE] = queries.astype(jnp.bfloat16)
            query_buf[slot, span(step), HEAD_SIZE:] = jnp.where(
                lane == OFFSET_LANE, -bound, chosen
            ).astype(jnp.bfloat16)

    def forward_scores(head):
        for tile in range(tiles):
            low, high = tile_steps(tile)
            cols = slice(tile * SUB, (tile + 1) * SUB)
            scores = mm(
                query_buf[head % 3, low * rows : high * rows, :], key_buf[head, cols, :], BOTH_MINOR
            )
            for step in range(low, high):
                part = limit(step, tile, scores[(step - low) * rows : (step - low + 1) * rows, :])
                weight_buf[head % 2, span(step), cols] = jnp.exp2(part).astype(jnp.bfloat16)

    def forward_products(head):
        for step in range(steps):
            product_buf[head % 2, span(step), :] = mm(
                weight_buf[head % 2, span(step), window(step)], value_buf[head, window(step), :]
            )

    def repeat(head):
        diagonal = lane - row % BLOCK

        def one_step(step, carry):
            here = pl.ds(pl.multiple_of(step * rows, rows), rows)

            def scores_of(tile):
                cols = pl.ds(pl.multiple_of((step + tile) * SUB, SUB), SUB)
                part = mm(query_buf[head % 3, here, :], key_buf[head, cols, :], BOTH_MINOR)
                lowest = jnp.where(tile == 0, 1, -BLOCK)
                highest = jnp.where(tile == step_tiles - 1, 0, BLOCK)
                halves = []
                for block in range(SUB // BLOCK):
                    inside = (diagonal >= lowest) & (diagonal <= highest)
                    inside = inside | (row // BLOCK != block)
                    halves.append(
                        jnp.where(inside, part[:, block * BLOCK : (block + 1) * BLOCK], FORBIDDEN)
                    )
                return jnp.concatenate(halves, axis=1), cols

            def top(tile, highest):
                part, _ = scores_of(tile)
                return jnp.maximum(highest, jnp.max(part, axis=1, keepdims=True))

            def again(tile, sums):
                part, cols = scores_of(tile)
                weights = jnp.exp2(part).astype(jnp.bfloat16)
                weight_buf[head % 2, here, cols] = weights
                return sums + mm(weights, value_buf[head, cols, :])

            extra = query_buf[head % 3, here, HEAD_SIZE:].astype(jnp.float32)
            query_buf[head % 3, here, HEAD_SIZE:] = jnp.where(lane == OFFSET_LANE, 0.0, extra).astype(
                jnp.bfloat16
            )
            highest = lax.fori_loop(
                0, step_tiles, top, jnp.full((rows, 1), FORBIDDEN, jnp.float32)
            )
            query_buf[head % 3, here, HEAD_SIZE:] = jnp.where(lane == OFFSET_LANE, -highest, extra).astype(
                jnp.bfloat16
            )
            product_buf[head % 2, here, :] = lax.fori_loop(
                0, step_tiles, again, jnp.zeros((rows, HEAD_SIZE + LANES), jnp.float32)
            )
            return carry

        lax.fori_loop(0, steps, one_step, 0)

    kept = {}

    def finish_forward(head):
        value_up = value_up_of(head)
        spreads = []
        inverses = []
        up_value = jnp.zeros((LANES, HEAD_SIZE), jnp.float32)
        for step in range(steps):
            gradient = jnp.concatenate(
                [gradient_in[head, own(step), member_cols(member)] for member in range(GROUPS)], axis=0
            )
            gradient_low = mm(gradient, value_up, BOTH_MINOR)
            inverse = 1.0 / product_buf[head % 2, span(step), ones]
            low_part = (product_buf[head % 2, span(step), HEAD_SIZE:] * inverse).astype(jnp.bfloat16)
            outputs = product_buf[head % 2, span(step), :HEAD_SIZE] * inverse + mm(low_part, value_up)
            outputs = outputs.astype(jnp.bfloat16)
            for member in range(GROUPS):
                out_buf[head, own(step), member_cols(member)] = outputs[own(member), :]
            delta = jnp.sum(
                outputs.astype(jnp.float32) * gradient.astype(jnp.float32), axis=1, keepdims=True
            )
            delta_high = delta.astype(jnp.bfloat16).astype(jnp.float32)
            extra = jnp.where(lane == ONES_LANE, -delta_high, gradient_low)
            extra = jnp.where(lane == ONES_LANE + 1, delta_high - delta, extra)
            gradient_buf[0, span(step), :HEAD_SIZE] = gradient
            gradient_buf[0, span(step), HEAD_SIZE:] = extra.astype(jnp.bfloat16)
            up_value += mm(low_part, gradient, BOTH_MAJOR)
            spreads.append(jnp.transpose(gradient_low * inverse)[:RANK, :].astype(jnp.bfloat16))
            inverses.append(inverse * SCORE_SCALE)
        up_value_buf[head] = up_value[:RANK, :].astype(jnp.bfloat16)
        wide_copy(out_hbm, out_buf, head, 2, out=True).start()
        kept[0] = jnp.concatenate(spreads, axis=1), inverses

    def backward_scores(head):
        spread = kept[0][0]
        for tile in range(tiles):
            low, high = tile_steps(tile)
            cols = slice(tile * SUB, (tile + 1) * SUB)
            back_row = RANK + tile * SUB // tokens * RANK
            back_rows = slice(back_row, back_row + RANK)
            back_cols = slice(tile * SUB % tokens, tile * SUB % tokens + SUB)
            part = slice(low * rows, high * rows)
            grad_weights = mm(gradient_buf[0, part, :], value_buf[head, cols, :], BOTH_MINOR)
            weights = weight_buf[head % 2, part, cols]
            score_buf[0, part, cols] = weights * grad_weights.astype(jnp.bfloat16)
            back_ref[back_rows, back_cols] += mm(spread[:, part], weights)

    def backward_products(head):
        query_grads = []
        for step in range(steps):
            cosines = cos_ref[own(step), :]
            sines = sin_ref[own(step), :]
            sums = mm(score_buf[0, span(step), window(step)], key_buf[head, window(step), :HEAD_SIZE])
            sums = sums * kept[0][1][step]
            turned = []
            for member in range(GROUPS):
                part = sums[own(member), :]
                turned.append(part * cosines - swap_halves(part) * sines)
            query_grads.append(jnp.concatenate(turned, axis=1).astype(jnp.bfloat16))
        query_grad = jnp.concatenate(query_grads, axis=0)
        up_query_buf[head] = mm(query_low_t_ref[...], query_grad).astype(jnp.bfloat16)
        back_ref[:RANK, :] += mm(query_up_ref[start + head], query_grad, BOTH_MINOR)

    def arrive(head, kind):
        buf = (key_buf, value_buf)[kind]
        main = pl.ds(0, HEAD_SIZE)
        source = one_hbm.at[own_rows, main]
        for part in range(3):
            copy(
                source, buf.at[head, pl.ds(part * tokens, tokens), main], head_sems.at[head, kind, part]
            ).wait()
        if kind == 0 or not first:
            extra_hbm = (key_extra_hbm, value_extra_hbm)[kind]
            copy(
                extra_hbm, buf.at[head, :, pl.ds(HEAD_SIZE, LANES)], head_sems.at[head, kind, 3]
            ).wait()

    def arrive_queries(head):
        arrive(head, 0)
        wide_copy(query_hbm, query_in, head, 0).wait()

    def check(head):
        @pl.when(jnp.min(product_buf[head % 2, :, ones]) < 1e-27)
        def _():
            repeat(head)

        wide_copy(gradient_hbm, gradient_in, head, 1).wait()

    def work_alone(head, carry):
        forward_scores(head)
        arrive(head, 1)
        forward_products(head)
        check(head)

        @pl.when(head + 1 < heads)
        def _():
            arrive_queries(head + 1)

        finish_forward(head)
        backward_scores(head)
        prepare(jnp.minimum(head + 1, heads - 1), (head + 1) % 3)
        backward_products(head)
        return carry

    if heads < 3:
        arrive_queries(0)
        prepare(0, 0)
        for head in range(1, heads):
            start_copies(head)
        lax.fori_loop(0, heads, work_alone, 0)
    else:
        for head in range(1, heads):
            start_copies(head)
        for head in range(2):
            arrive_queries(head)
            prepare(head, head)
        arrive(0, 1)
        forward_scores(0)
        forward_products(0)

        def work(head, carry):
            check(head)
            arrive(head + 1, 1)

            @pl.when(head + 2 < heads)
            def _():
                arrive_queries(head + 2)

            finish_forward(head)
            forward_scores(head + 1)
            backward_scores(head)
            prepare(jnp.minimum(head + 2, heads - 1), (head + 2) % 3)
            forward_products(head + 1)
            backward_products(head)
            return carry

        lax.fori_loop(0, heads - 1, work, 0)
        check(heads - 1)
        finish_forward(heads - 1)
        backward_scores(heads - 1)
        backward_products(heads - 1)
    up_copies = []
    for head in range(heads):
        at = pl.ds((start + head) * GROUP_WIDTH, GROUP_WIDTH)
        up_copies.append(copy(up_query_buf.at[head], partial_hbm.at[:, at], head_sems.at[head, 3, 0]))
        at = pl.ds(up_columns + (start + head) * HEAD_SIZE, HEAD_SIZE)
        up_copies.append(copy(up_value_buf.at[head], partial_hbm.at[:, at], head_sems.at[head, 3, 1]))
    for up_copy in up_copies:
        up_copy.start()
    for head in range(heads):
        wide_copy(out_hbm, out_buf, head, 2, out=True).wait()
    for done in (*extras, *up_copies):
        done.wait()


VMEM = pl.BlockSpec(memory_space=pltpu.VMEM)
SMEM = pl.BlockSpec(memory_space=pltpu.SMEM)
ANY = pl.BlockSpec(memory_space=pl.ANY)
NEAR = 4


def attention_chunk(
    first, last, columns, query_base, gradient, received, shared, tables, carried
):
    count = last - first
    tokens = query_base.shape[0]
    keys = 3 * tokens
    rows = GROUPS * tokens
    out_specs = [ANY, ANY, VMEM]
    out_shape = [
        jax.ShapeDtypeStruct(query_base.shape, jnp.bfloat16),
        jax.ShapeDtypeStruct((RANK, columns), jnp.bfloat16),
        jax.ShapeDtypeStruct((RANK + keys // tokens * RANK, tokens), jnp.float32),
    ]
    if carried is None:
        out_specs.append(ANY)
        out_shape.append(jax.ShapeDtypeStruct((keys, LANES), jnp.bfloat16))
    arguments = [query_base, gradient, *received, *shared, *tables]
    in_specs = [ANY] * 6 + [VMEM] * len(shared) + [ANY] * len(tables)
    aliases = {}
    if carried is not None:
        arguments += carried
        in_specs += [ANY, ANY, VMEM]
        aliases = {len(arguments) - 3: 0, len(arguments) - 2: 1}
    wide_buf = HEAD_SIZE + LANES
    return pl.pallas_call(
        functools.partial(attention_kernel, carried is None, first, query_base.shape[1]),
        in_specs=in_specs,
        out_specs=out_specs,
        scratch_shapes=[
            pltpu.VMEM((count, tokens, GROUP_WIDTH), jnp.bfloat16),
            pltpu.VMEM((count, tokens, GROUP_WIDTH), jnp.bfloat16),
            pltpu.VMEM((count, tokens, GROUP_WIDTH), jnp.bfloat16),
            pltpu.VMEM((count, RANK, GROUP_WIDTH), jnp.bfloat16),
            pltpu.VMEM((count, RANK, HEAD_SIZE), jnp.bfloat16),
            pltpu.VMEM((3, RANK, tokens), jnp.bfloat16),
            pltpu.VMEM((count, keys, wide_buf), jnp.bfloat16),
            pltpu.VMEM((count, keys, wide_buf), jnp.bfloat16),
            pltpu.VMEM((3, rows, wide_buf), jnp.bfloat16),
            pltpu.VMEM((1, rows, wide_buf), jnp.bfloat16),
            pltpu.VMEM((2, rows, keys), jnp.bfloat16),
            pltpu.VMEM((1, rows, keys), jnp.bfloat16),
            pltpu.VMEM((2, rows, wide_buf), jnp.float32),
            pltpu.SemaphoreType.DMA((10,)),
            pltpu.SemaphoreType.DMA((count, 4, 4)),
        ],
        out_shape=out_shape,
        input_output_aliases=aliases,
        compiler_params=pltpu.CompilerParams(vmem_limit_bytes=40 * 2**20),
    )(*arguments)


def down_kernel(first_column, back_ref, one_ref, two_ref, hidden_ref, _, partial_hbm, down_buf, sems):
    features = hidden_ref.shape[1]
    value_back = back_ref[3 * RANK :, :].astype(jnp.float32)
    value_back = value_back + one_ref[...].astype(jnp.float32) + two_ref[...].astype(jnp.float32)
    back = jnp.concatenate([back_ref[:RANK, :], value_back.astype(jnp.bfloat16)], axis=0)
    down_buf[...] = mm(back, hidden_ref[...]).astype(jnp.bfloat16)
    copies = [
        pltpu.make_async_copy(
            down_buf.at[pl.ds(at * RANK, RANK)],
            partial_hbm.at[:, pl.ds(first_column + at * features, features)],
            sems.at[at],
        )
        for at in range(2)
    ]
    for each in copies:
        each.start()
    for each in copies:
        each.wait()


def final_kernel(scale, *refs):
    place = lax.axis_index("ctx") % NEAR
    gathered = [ref[...].astype(jnp.float32) * scale for ref in refs[:NEAR]]
    query_up_ref, value_up_ref, query_down_ref, value_down_ref = refs[NEAR:]
    parts = []
    for at in range(NEAR):
        distance = (at % 2 * 2 + at // 2) ^ place
        part = gathered[0]
        for other in range(1, NEAR):
            part = jnp.where(distance == other, gathered[other], part)
        parts.append(part)
    total = jnp.concatenate(parts, axis=1)
    column = 0
    for ref in (query_up_ref, value_up_ref, query_down_ref, value_down_ref):
        ref[...] = total[:, column : column + ref.shape[1]]
        column += ref.shape[1]


def head_sum(x):
    if lax.axis_size("head") == 2:
        other = lax.ppermute(x, "head", [(0, 1), (1, 0)])
        return (x.astype(jnp.float32) + other.astype(jnp.float32)).astype(x.dtype)
    return lax.psum(x, "head")


def ctx_sum(x):
    devices = lax.axis_size("ctx")
    place = lax.axis_index("ctx") % NEAR

    def exchange(value, distance):
        return lax.ppermute(value, "ctx", [(i, i ^ distance) for i in range(devices)])

    def halve(value, bit, distance):
        half = value.shape[1] // 2
        kept = lax.dynamic_slice_in_dim(value, bit * half, half, 1)
        given = lax.dynamic_slice_in_dim(value, (1 - bit) * half, half, 1)
        return add(kept, exchange(given, distance))

    def add(one, other):
        return (one.astype(jnp.float32) + other.astype(jnp.float32)).astype(jnp.bfloat16)

    x = halve(x, place % 2, 1)
    x = halve(x, place // 2, 2)
    distance = NEAR
    while distance < devices:
        radix = 4 if distance * 4 <= devices else 2
        others = [exchange(x, distance * part) for part in range(1, radix)]
        x = sum([other.astype(jnp.float32) for other in others], x.astype(jnp.float32))
        x = x.astype(jnp.bfloat16)
        distance *= radix
    return [x] + [exchange(x, distance) for distance in range(1, NEAR)]


def after(value, *others):
    return lax.optimization_barrier((value, *others))[0]


def per_device(
    hidden_states,
    query_base,
    key_base,
    frozen_value_rows,
    query_down,
    query_up,
    value_down,
    value_up_weight,
    positions,
    block_mask,
    output_gradient,
):
    tokens = hidden_states.shape[0]
    devices = lax.axis_size("ctx")
    kv_heads = key_base.shape[1] // HEAD_SIZE
    forward_one = [(i, i + 1) for i in range(devices - 1)]
    even_two = [(i, i + 2) for i in range(0, devices - 2, 2)]
    even_one = [(i, i + 1) for i in range(0, devices - 1, 2)]

    both_down = jnp.concatenate([query_down, value_down], axis=1)
    low = head_sum(mm(both_down, hidden_states, (((0,), (1,)), ((), ())))).astype(jnp.bfloat16)
    query_low_t = low[:RANK]
    value_low_t = low[RANK:]

    half = np.arange(HEAD_SIZE // 2, dtype=np.float64)
    frequency = (ROPE_BASE ** (-2.0 * half / HEAD_SIZE)).astype(np.float32)[:, None]

    def payload(chunk):
        first, last = chunk
        extra = RANK if first == 0 else 0
        return jax.ShapeDtypeStruct((tokens + extra, 2 * (last - first) * HEAD_SIZE), jnp.bfloat16)

    table = jax.ShapeDtypeStruct((tokens, HEAD_SIZE), jnp.float32)
    cosines, sines, packed_first = pl.pallas_call(
        functools.partial(prologue_kernel, CHUNKS[:1]),
        out_shape=[table, table, payload(CHUNKS[0])],
        compiler_params=pltpu.CompilerParams(vmem_limit_bytes=16 * 2**20),
    )(positions[None, :], jnp.asarray(frequency), key_base, frozen_value_rows)
    packed_first = lax.dynamic_update_slice(packed_first, value_low_t, (tokens, 0))
    key_extra, *packed_later = pl.pallas_call(
        functools.partial(later_prologue_kernel, CHUNKS[1:]),
        in_specs=[SMEM] + [VMEM] * 4,
        out_shape=[
            jax.ShapeDtypeStruct((3 * tokens, LANES), jnp.bfloat16),
            *(payload(chunk) for chunk in CHUNKS[1:]),
        ],
        compiler_params=pltpu.CompilerParams(vmem_limit_bytes=16 * 2**20),
    )(block_mask.T, cosines, after(sines, packed_first), key_base, frozen_value_rows)
    packed = [packed_first, *packed_later]

    query_ups = query_up.reshape(RANK, kv_heads, GROUP_WIDTH).transpose(1, 0, 2)
    value_ups = value_up_weight.reshape(RANK, kv_heads, HEAD_SIZE).transpose(1, 0, 2)
    shared = [query_ups, value_ups, query_low_t, cosines, sines]

    ones, evens = [], []
    for chunk, own in enumerate(packed):
        if chunk > 1:
            own = after(own, ones[chunk - 1], evens[chunk - 2])
        ones.append(lax.ppermute(own, "ctx", forward_one))
        evens.append(lax.ppermute(own, "ctx", even_two))

    features = hidden_states.shape[1]
    query_columns = kv_heads * GROUP_WIDTH
    value_columns = kv_heads * HEAD_SIZE
    columns = query_columns + value_columns + 2 * features
    columns = -(-columns // (NEAR * LANES)) * NEAR * LANES
    carried = None
    tables = [key_extra]
    for chunk, (first, last) in enumerate(CHUNKS):
        one = ones[chunk]
        one = after(one, evens[chunk], *([] if carried is None else [carried[2]]))
        odd = lax.ppermute(one, "ctx", even_one)
        *carried, = attention_chunk(
            first,
            last,
            columns,
            query_base,
            output_gradient,
            [packed[chunk], one, evens[chunk], odd],
            shared,
            tables,
            carried,
        )
        tables = tables + carried[3:]
        carried = carried[:3]
    attention_out, partial, back = carried

    back = head_sum(back.astype(jnp.bfloat16))
    back_one = lax.ppermute(
        back[2 * RANK : 3 * RANK], "ctx", [(i + 1, i) for i in range(devices - 1)]
    )
    back_two = lax.ppermute(back[RANK : 2 * RANK], "ctx", [(i + 2, i) for i in range(devices - 2)])
    arguments = [back, back_one, back_two, hidden_states, partial]
    partial = pl.pallas_call(
        functools.partial(down_kernel, query_columns + value_columns),
        in_specs=[VMEM] * (len(arguments) - 1) + [ANY],
        out_specs=ANY,
        out_shape=jax.ShapeDtypeStruct(partial.shape, partial.dtype),
        scratch_shapes=[
            pltpu.VMEM((2 * RANK, features), jnp.bfloat16),
            pltpu.SemaphoreType.DMA((2,)),
        ],
        input_output_aliases={len(arguments) - 1: 0},
        compiler_params=pltpu.CompilerParams(vmem_limit_bytes=16 * 2**20),
    )(*arguments)
    gathered = ctx_sum(partial)
    widths = (query_columns, value_columns, features, features)
    up_query, up_value, down_query, down_value = pl.pallas_call(
        functools.partial(final_kernel, float((devices * tokens) ** (-0.5))),
        in_specs=[VMEM] * NEAR,
        out_specs=[VMEM] * 4,
        out_shape=[jax.ShapeDtypeStruct((RANK, width), jnp.float32) for width in widths],
    )(*gathered)
    return attention_out, down_query.T, up_query, down_value.T, up_value


def solution(mesh):
    placed = (
        P("ctx", "head"),
        P("ctx", "head"),
        P("ctx", "head"),
        P("ctx", "head"),
        P("head", None),
        P(None, "head"),
        P("head", None),
        P(None, "head"),
        P("ctx"),
        P(),
        P("ctx", "head"),
    )
    return jax.shard_map(
        per_device,
        mesh=mesh,
        in_specs=placed,
        out_specs=(
            P("ctx", "head"),
            P("head", None),
            P(None, "head"),
            P("head", None),
            P(None, "head"),
        ),
        check_vma=False,
    )
```
